32 devices in a mesh: fsdp: 2 (over x), ctx: 4 (over y, core), tp: 4 (over z).
Axes of the slice: x: 2, y: 2, z: 4, core: 2. Of those that a mesh axis runs over, the one named last changes fastest.
Arguments:
- tokens: bfloat16 [2, 1024, 768], P('fsdp', 'ctx'), may hold values from -6 to 6
- mixing_weight: bfloat16 [768, 3, 768], P(('fsdp', 'ctx'), None, 'tp'), may hold values from -0.21875 to 0.21875
- output_weight: bfloat16 [768, 768], P('tp', ('fsdp', 'ctx')), may hold values from -3.5 to 3.5
- first_gain: bfloat16 [768], P(('fsdp', 'ctx')), may hold values from 0.5 to 1.5
- second_gain: bfloat16 [768], P(('fsdp', 'ctx')), may hold values from 0.5 to 1.5
- centroids: bfloat16 [32, 768], P(None, ('fsdp', 'ctx')), may hold values from -0.109375 to 0.109375
- expert_up: bfloat16 [32, 768, 3072], P('fsdp', 'ctx', 'tp'), may hold values from -0.21875 to 0.21875
- expert_down: bfloat16 [32, 3072, 768], P('fsdp', 'tp', 'ctx'), may hold values from -0.3125 to 0.3125
- prefix_length: int32 [2], P('fsdp'), may hold values from 0 to 1024
- assignment: int32 [2, 1024, 1], P('fsdp', 'ctx'), may hold values from 0 to 31, as said below
- validity: int32 [2, 1024], P('fsdp', 'ctx'), may hold values 0 or 1
- teacher: bfloat16 [2, 1024, 768], P('fsdp', 'ctx'), may hold values from -6 to 6
- cotangent: bfloat16 [2, 1024, 768], P('fsdp', 'ctx'), may hold values from -6 to 6
Outputs:
- activations: bfloat16 [2, 1024, 768], P('fsdp', 'ctx')
- tokens_gradient: bfloat16 [2, 1024, 768], P('fsdp', 'ctx')
- mixing_gradient: float32 [768, 3, 768], P(('fsdp', 'ctx'), None, 'tp')
- output_gradient: float32 [768, 768], P('tp', ('fsdp', 'ctx'))
- first_gradient: float32 [768], P(('fsdp', 'ctx'))
- second_gradient: float32 [768], P(('fsdp', 'ctx'))
- centroid_gradient: float32 [32, 768], P(None, ('fsdp', 'ctx'))
- upward_gradient: float32 [32, 768, 3072], P('fsdp', 'ctx', 'tp')
- downward_gradient: float32 [32, 3072, 768], P('fsdp', 'tp', 'ctx')
- balance_loss: float32 [], replicated
- distill_loss: float32 [], replicated
The draws below stay inside these ranges and needn't reach their ends.
Inputs may be any that keep to these rules, and one draw needn't show every extreme that they name: `assignment`: in each aligned block of 256 tokens (the tokens of one sequence piece, in order of sequence and position) a quarter of the experts are named by exactly 16 tokens, half by exactly 8, and the rest by none; which experts these are differs from block to block.
All inputs are finite; a program needn't handle non-finite values. No bound on the sum of `validity` on one device may be relied on, other than what follows from the above.
Results may differ from the reference program's by a relative error of at most 0.015.
Values may be sent and summed in bfloat16 or wider, within the bound.
A program may use at most 256 MiB of HBM per device.

```python
import math
import jax
import jax.numpy as jnp
import numpy as np
from jax import lax

D = 768
HEADS = 12
HD = 64
FF = 3072
EXPERTS = 32
TOK_DEV = 256
LEN = 1024
SEQS = 2
TOKENS = 2048
CAP = 16
N_CTX = 4


def draw_assignment(key, part):
    mean_load = TOK_DEV // EXPERTS
    quarter = EXPERTS // 4
    loads = np.array([2 * mean_load] * quarter + [mean_load] * (EXPERTS // 2) + [0] * (EXPERTS - quarter - EXPERTS // 2))
    pattern = jnp.asarray(np.repeat(np.arange(EXPERTS), loads), jnp.int32)
    block_total = SEQS * LEN // TOK_DEV

    def one_block(index):
        block_key = jax.random.fold_in(key, index)
        first_key, second_key = jax.random.split(block_key)
        order = jax.random.permutation(first_key, EXPERTS).astype(jnp.int32)
        shuffle = jax.random.permutation(second_key, TOK_DEV).astype(jnp.int32)
        return order[pattern[shuffle]]
    drawn = jax.vmap(one_block)(jnp.arange(block_total, dtype=jnp.int32))
    return drawn.reshape(SEQS, LEN, 1).astype(jnp.int32)


def with_ends(values, stream_key, least, top_value):
    longest = values.shape.index(max(values.shape))
    spots = []
    for shift in (0, 1):
        where = [jax.random.randint(jax.random.fold_in(stream_key, axis), (), 0, length) for axis, length in enumerate(values.shape)]
        where[longest] = (where[longest] + shift) % values.shape[longest]
        spots.append(tuple(where))
    return values.at[spots[0]].set(least).at[spots[1]].set(top_value)


def shard_levels(own_key, extent, pieces, smallest, high):
    def one(axis_at, blocks):
        steps = jax.random.uniform(jax.random.fold_in(jax.random.fold_in(own_key, 6), axis_at), (blocks,), jnp.float32, smallest / len(pieces), high / len(pieces))
        return jnp.repeat(jnp.exp(steps), extent[axis_at] // blocks).reshape((-1,) + (1,) * (len(extent) - axis_at - 1))

    level = one(*pieces[0])
    for cut in pieces[1:]:
        level = level * one(*cut)
    return level


def normal_values(own_key, extent, spread, limit, cuts=(), kind=jnp.bfloat16):
    values = spread * jax.random.normal(own_key, extent, jnp.float32)
    if cuts:
        values = values * shard_levels(own_key, extent, cuts, -0.22, 0.18)
    return jnp.clip(values, -limit, limit).astype(kind)


def setup_inputs(seed: int = 0) -> dict:
    splits = jax.random.split(jax.random.key(seed), 14)
    tokens = normal_values(splits[0], (SEQS, LEN, D), 1.0, 6.0, ((0, 2), (1, 4)))
    mixing_weight = normal_values(splits[1], (D, 3, D), D ** -0.5, 0.21875, ((0, 8), (2, 4)))
    output_weight = normal_values(splits[2], (D, D), (max(1, 5 * D // LEN)) ** -0.5, 3.5, ((0, 4), (1, 8)))
    first_gain = jnp.clip(1.0 + 0.1 * jax.random.normal(splits[3], (D,), jnp.float32), 0.5, 1.5).astype(jnp.bfloat16)
    second_gain = jnp.clip(1.0 + 0.1 * jax.random.normal(splits[4], (D,), jnp.float32), 0.5, 1.5).astype(jnp.bfloat16)
    centroids = normal_values(splits[5], (EXPERTS, D), (4 * D) ** -0.5, 0.109375, ((1, 8),))
    expert_up = normal_values(splits[6], (EXPERTS, D, FF), D ** -0.5, 0.21875, ((0, 2), (1, 4), (2, 4)))
    expert_down = normal_values(splits[7], (EXPERTS, FF, D), (FF // 8) ** -0.5, 0.3125, ((0, 2), (1, 4), (2, 4)))
    prefix_length = jax.random.randint(splits[8], (SEQS,), 0, LEN + 1).astype(jnp.int32)
    assignment = draw_assignment(jax.random.fold_in(splits[13], 71), 0)
    validity = with_ends((jax.random.randint(splits[10], (SEQS, LEN), 0, 4) < 3).astype(jnp.int32), jax.random.fold_in(splits[10], 1), 0, 1)
    teacher = normal_values(splits[11], (SEQS, LEN, D), 1.0, 6.0, ((0, 2), (1, 4)))
    cotangent = normal_values(splits[12], (SEQS, LEN, D), 1.0, 6.0, ((0, 2), (1, 4)))
    return dict(tokens=tokens, mixing_weight=mixing_weight, output_weight=output_weight, first_gain=first_gain, second_gain=second_gain, centroids=centroids, expert_up=expert_up, expert_down=expert_down, prefix_length=prefix_length, assignment=assignment, validity=validity, teacher=teacher, cotangent=cotangent)


@jax.custom_vjp
def low(v):
    return lax.optimization_barrier(v.astype(jnp.bfloat16)).astype(jnp.float32)

@jax.custom_vjp
def low_back(v):
    return v

def low_keep(v):
    return (low(v), None)

def low_pass(kept, grad):
    return (grad,)

def back_keep(v):
    return (v, None)

def back_low(kept, grad):
    return (low(grad),)
low.defvjp(low_keep, low_pass)
low_back.defvjp(back_keep, back_low)
EPSILON = 1e-05
TOP_PRECISION = lax.Precision.HIGHEST

def layer_norm(values, gain):
    centred = values - lax.optimization_barrier(jnp.mean(values, axis=-1, keepdims=True))
    variance = lax.optimization_barrier(jnp.mean(centred * centred, axis=-1, keepdims=True))
    return centred * lax.rsqrt(variance + EPSILON) * gain

def attend_block(queries, keys, values, offset, prefix, validity):
    raw_scores = jnp.einsum('qhd,khd->hqk', queries, keys, precision=TOP_PRECISION) * (1.0 / math.sqrt(HD))
    scores = low_back(raw_scores)
    query_pos = offset + jnp.arange(queries.shape[0], dtype=jnp.int32)
    key_pos = jnp.arange(keys.shape[0], dtype=jnp.int32)
    visible = (key_pos[None, :] <= query_pos[:, None]) | (key_pos[None, :] < prefix)
    allowed = visible & ((validity[None, :] == 1) | (key_pos[None, :] == query_pos[:, None]))
    masked = jnp.where(allowed[None], scores, -1e+30)
    row_max = lax.optimization_barrier(jnp.max(masked, axis=-1, keepdims=True))
    unscaled = jnp.exp(masked - row_max)
    weights = unscaled / lax.optimization_barrier(jnp.sum(unscaled, axis=-1, keepdims=True))
    return jnp.einsum('hqk,khd->qhd', low(weights), values, precision=TOP_PRECISION)

def sequence_attention(queries, keys, values, prefix, validity):
    block_rows = min(512, LEN)
    block_count = LEN // block_rows
    query_blocks = queries.reshape(block_count, block_rows, HEADS, HD)
    offsets = jnp.arange(block_count, dtype=jnp.int32) * block_rows
    checked = jax.checkpoint(attend_block)

    def one_block(packet):
        return checked(packet[0], keys, values, packet[1], prefix, validity)
    result = lax.map(one_block, (query_blocks, offsets))
    return result.reshape(LEN, HEADS * HD)

def expert_apply(rows, upward, downward):
    hidden = low_back(jnp.dot(rows, upward, precision=TOP_PRECISION))
    activated = low(jax.nn.gelu(hidden, approximate=False))
    return low(low_back(jnp.dot(activated, downward, precision=TOP_PRECISION)))

def forward(tokens, mixing_layer, layer_output, first, second, centroids, upward, downward, prefix, assignment, validity, teacher):
    normalized_input = low(layer_norm(tokens, first))
    projected_heads = jnp.einsum('cmq,qny->cmny', normalized_input, mixing_layer, precision=TOP_PRECISION)
    queries = low(low_back(projected_heads[:, :, 0])).reshape(SEQS, LEN, HEADS, HD)
    keys = low(low_back(projected_heads[:, :, 1])).reshape(SEQS, LEN, HEADS, HD)
    values = low(low_back(projected_heads[:, :, 2])).reshape(SEQS, LEN, HEADS, HD)
    attended_context = lax.map(lambda packet: sequence_attention(*packet), (queries, keys, values, prefix, validity))
    attended_context = low(low_back(attended_context))
    branch_output = low_back(jnp.einsum('ucw,wp->ucp', attended_context, layer_output, precision=TOP_PRECISION))
    residual = tokens + branch_output
    mixed_in = low(layer_norm(residual, second))
    flat_in = mixed_in.reshape(TOKENS, D)
    chosen = assignment.reshape(TOKENS).astype(jnp.int32)
    onehot = chosen[:, None] == jnp.arange(EXPERTS, dtype=jnp.int32)[None, :]
    hot_int = onehot.astype(jnp.int32)
    earlier = jnp.cumsum(hot_int.reshape(SEQS * N_CTX, TOK_DEV, EXPERTS), axis=1).reshape(TOKENS, EXPERTS) - hot_int
    rank = lax.optimization_barrier(jnp.sum(earlier * hot_int, axis=1))
    block_index = jnp.arange(TOKENS, dtype=jnp.int32) // TOK_DEV
    slots = (chosen * (SEQS * N_CTX * CAP) + block_index * CAP + rank).astype(jnp.int32)
    logits = lax.optimization_barrier(jnp.sum(flat_in * centroids[chosen], axis=-1))
    gates = jax.nn.sigmoid(logits)
    buffer = jnp.zeros((EXPERTS * SEQS * N_CTX * CAP, D), jnp.float32).at[slots].set(flat_in)
    dispatched = low_back(buffer.reshape(EXPERTS, SEQS * N_CTX * CAP, D))
    checked_expert = jax.checkpoint(expert_apply)
    expert_rows = lax.map(lambda packet: checked_expert(*packet), (dispatched, upward, downward))
    returned = expert_rows.reshape(EXPERTS * SEQS * N_CTX * CAP, D)[slots]
    mixed = residual + (gates[:, None] * returned).reshape(SEQS, LEN, D)
    counts = lax.optimization_barrier(jnp.sum(onehot.astype(jnp.float32), axis=0))
    gate_total = lax.optimization_barrier(jnp.sum(jnp.where(onehot, gates[:, None], 0.0), axis=0))
    all_tokens = float(TOKENS)
    balance = EXPERTS * EXPERTS * jnp.sum((counts / all_tokens - 1.0 / EXPERTS) * gate_total / all_tokens)
    valid_float = validity.astype(jnp.float32)
    valid_count = jnp.sum(valid_float)
    difference = mixed - teacher
    distill = jnp.sum(valid_float[..., None] * difference * difference) / (valid_count * D)
    return (mixed, balance, distill)

def reference(tokens, mixing_weight, output_weight, first_gain, second_gain, centroids, expert_up, expert_down, prefix_length, assignment, validity, teacher, cotangent):
    floats = tuple((array_in.astype(jnp.float32) for array_in in (tokens, mixing_weight, output_weight, first_gain, second_gain, centroids, expert_up, expert_down)))
    teacher_float = teacher.astype(jnp.float32)

    def objective(*weights):
        return forward(*weights, prefix_length, assignment, validity, teacher_float)
    outputs, pull = jax.vjp(objective, *floats)
    mixed, balance, distill = outputs
    gradients = pull((cotangent.astype(jnp.float32), jnp.zeros((), jnp.float32), jnp.ones((), jnp.float32)))
    return (mixed.astype(jnp.bfloat16), gradients[0].astype(jnp.bfloat16), gradients[1], gradients[2], gradients[3], gradients[4], gradients[5], gradients[6], gradients[7], balance, distill)
```

```python
from functools import partial
import math

import jax
import jax.numpy as jnp
from jax import lax
from jax.experimental import pallas as pl
from jax.experimental.pallas import tpu as pltpu
from jax.sharding import PartitionSpec as P

HD = 64
EPSILON = 1e-05
BF = jnp.bfloat16
F32 = jnp.float32
MESH = pl.DeviceIdType.MESH
TOP = lax.Precision.HIGHEST
VMEM = pltpu.VMEM
ANY = pl.ANY
COLS = 896
OUT_AT = 640
CEN_AT = 832


def _dot(a, b, ca, cb, precision=None):
    return lax.dot_general(
        a, b, (((ca,), (cb,)), ((), ())), preferred_element_type=F32, precision=precision
    )


def nn(a, b):
    return _dot(a, b, 1, 0)


def nt(a, b):
    return _dot(a, b, 1, 1)


def tn(a, b):
    return _dot(a, b, 0, 0)


def vspec():
    return pl.BlockSpec(memory_space=VMEM)


def sds(shape, dtype):
    return jax.ShapeDtypeStruct(shape, dtype)


def params(cid=None, mib=56):
    if cid is None:
        return pltpu.CompilerParams(vmem_limit_bytes=mib * 2**20)
    return pltpu.CompilerParams(
        vmem_limit_bytes=mib * 2**20, collective_id=cid, has_side_effects=True
    )


def iota(shape, dim):
    return lax.broadcasted_iota(jnp.int32, shape, dim)


def to_col(row):
    n = row.shape[1]
    return jnp.sum(jnp.where(iota((n, n), 0) == iota((n, n), 1), row, 0.0), axis=1, keepdims=True)


def to_row(col):
    n = col.shape[0]
    return jnp.sum(jnp.where(iota((n, n), 0) == iota((n, n), 1), col, 0.0), axis=0, keepdims=True)


def norm_parts(x):
    c = x - jnp.mean(x, axis=-1, keepdims=True)
    inv = lax.rsqrt(jnp.mean(c * c, axis=-1, keepdims=True) + EPSILON)
    return c * inv, inv


def norm_back(grad, xhat, inv, gain):
    gx = grad * gain
    return inv * (
        gx
        - jnp.mean(gx, axis=-1, keepdims=True)
        - xhat * jnp.mean(gx * xhat, axis=-1, keepdims=True)
    )


def route(chosen, experts, cap):
    n = chosen.shape[0]
    hot = (chosen == iota((n, experts), 1)).astype(F32)
    lower = (iota((n, n), 1) < iota((n, n), 0)).astype(BF)
    earlier = nn(lower, hot.astype(BF))
    rank = jnp.sum(earlier * hot, axis=1, keepdims=True)
    return hot, chosen.astype(F32) * cap + rank


def slot_rows(slot, rows, slots, s_ref):
    n, d = rows.shape
    place = (iota((slots, n), 0).astype(F32) == to_row(slot)).astype(BF)
    filled = nn(place, rows).astype(BF)
    fs, _, _, r, h = s_ref.shape
    for f in range(fs):
        for c in range(2):
            at = (f * 2 + c) * r
            for y in range(2):
                s_ref[f, y, c] = filled[at : at + r, y * h : (y + 1) * h]


def token_rows(slot, rb_ref, slots):
    n = slot.shape[0]
    sources = rb_ref.shape[0]
    parts = []
    for f in range(sources // 4):
        for c in range(2):
            parts.append(
                jnp.concatenate([rb_ref[f * 4 + c], rb_ref[f * 4 + 2 + c]], axis=1)
            )
    rows = jnp.concatenate(parts, axis=0)
    place = (iota((n, slots), 1).astype(F32) == slot).astype(BF)
    return nn(place, rows)


def z_peers(zs):
    f, i, z = lax.axis_index("fsdp"), lax.axis_index("ctx"), lax.axis_index("tp")
    return [(f, i, lax.rem(z + s, zs)) for s in range(1, zs)]


def greet(peers):
    barrier = pltpu.get_barrier_semaphore()
    for peer in peers:
        pl.semaphore_signal(barrier, inc=1, device_id=peer, device_id_type=MESH)
    pl.semaphore_wait(barrier, len(peers))


def remote(src, dst, send, recv, peer):
    return pltpu.make_async_remote_copy(
        src_ref=src, dst_ref=dst, send_sem=send, recv_sem=recv, device_id=peer, device_id_type=MESH
    )


def sum_over_z(zs, x_ref, o_ref, parts, send, recv):
    z = lax.axis_index("tp")
    n = x_ref.shape[0] // zs
    peers = z_peers(zs)

    def chunk(at):
        return pl.ds(pl.multiple_of(at * n, n), n)

    first = []
    for s in range(1, zs):
        to = lax.rem(z + s, zs)
        cp = remote(x_ref.at[chunk(to)], parts.at[s - 1], send.at[0, s - 1], recv.at[0, s - 1], peers[s - 1])
        cp.start()
        first.append(cp)
    total = x_ref[chunk(z), :].astype(F32)
    for s in range(1, zs):
        first[s - 1].wait_recv()
        total = total + parts[s - 1].astype(F32)
    o_ref[chunk(z), :] = total.astype(BF)
    second = []
    for s in range(1, zs):
        cp = remote(o_ref.at[chunk(z)], o_ref.at[chunk(z)], send.at[1, s - 1], recv.at[1, s - 1], peers[s - 1])
        cp.start()
        second.append(cp)
    for cp in second:
        cp.wait_recv()
    for cp in first + second:
        cp.wait_send()


def sum_scratch(zs, n, d):
    return [
        VMEM((zs - 1, n // zs, d), BF),
        pltpu.SemaphoreType.DMA((2, zs - 1)),
        pltpu.SemaphoreType.DMA((2, zs - 1)),
    ]


def group_peers(fs):
    f, i, z = lax.axis_index("fsdp"), lax.axis_index("ctx"), lax.axis_index("tp")
    y, c = lax.div(i, 2), lax.rem(i, 2)
    out = []
    for df in range(fs):
        for dy in range(2):
            for dc in range(2):
                if df or dy or dc:
                    fp = lax.rem(f + df, fs)
                    yp = y if dy == 0 else 1 - y
                    cp = c if dc == 0 else 1 - c
                    out.append((fp, yp, cp, (fp, yp * 2 + cp, z)))
    return out


def project_body(tok_ref, w_ref, t_ref, normed_ref, qt_ref, kv_ref):
    d, k = tok_ref.shape[1], qt_ref.shape[0]
    xhat, _ = norm_parts(tok_ref[...].astype(F32))
    normed = (xhat * t_ref[32:33, :].astype(F32)).astype(BF)
    normed_ref[...] = normed
    qkv = nn(normed, w_ref[:, : 3 * k])
    qt_ref[...] = jnp.transpose(qkv[:, :k]).astype(BF)
    kv_ref[...] = qkv[:, k:].astype(BF)


def attend_body(at_ref, qt_ref, own_ref, far_ref, sib_ref, valid_ref, w_ref, pt_ref, ctx_ref, out_ref):
    k, n = qt_ref.shape
    mine, prefix = at_ref[0], at_ref[1]
    pieces = [own_ref[...], far_ref[...], sib_ref[0], sib_ref[1]]
    offsets = [at_ref[2 + j] for j in range(4)]
    query = iota((n, n), 1) + mine * n
    allowed = []
    for j in range(4):
        key = iota((n, n), 0) + offsets[j] * n
        col = to_col(valid_ref[pl.ds(offsets[j], 1), :])
        allowed.append(((key <= query) | (key < prefix)) & ((col > 0.5) | (key == query)))
    outs = []
    for h in range(k // HD):
        lo = h * HD
        qt = qt_ref[lo : lo + HD, :]
        scores = [
            jnp.where(allowed[j], nn(pieces[j][:, lo : lo + HD], qt) * (1.0 / math.sqrt(HD)), -1e30)
            for j in range(4)
        ]
        top = jnp.max(scores[0], axis=0, keepdims=True)
        for j in range(1, 4):
            top = jnp.maximum(top, jnp.max(scores[j], axis=0, keepdims=True))
        exps = [jnp.exp(s - top) for s in scores]
        total = sum(jnp.sum(e, axis=0, keepdims=True) for e in exps)
        acc = jnp.zeros((HD, n), F32)
        for j in range(4):
            w = (exps[j] / total).astype(BF)
            pt_ref[h, j] = w
            acc = acc + tn(pieces[j][:, k + lo : k + lo + HD], w)
        outs.append(acc)
    ctx = jnp.transpose(jnp.concatenate(outs, axis=0)).astype(BF)
    ctx_ref[...] = ctx
    out_ref[...] = nt(ctx, w_ref[:, OUT_AT : OUT_AT + k]).astype(BF)


def attend_back_body(gb_ref, qt_ref, own_ref, far_ref, sib_ref, pt_ref, ctx_ref, w_ref, dq_ref, near_ref, away_ref, og_ref):
    k, n = qt_ref.shape
    scale = 1.0 / math.sqrt(HD)
    gb = gb_ref[...]
    og_ref[...] = tn(gb, ctx_ref[...])
    gct = jnp.transpose(nn(gb, w_ref[:, OUT_AT : OUT_AT + k]).astype(BF).astype(F32)).astype(BF)
    pieces = [own_ref[...], far_ref[...], sib_ref[0], sib_ref[1]]
    dqs = []
    for h in range(k // HD):
        lo = h * HD
        dot_ = gct[lo : lo + HD, :]
        qt = qt_ref[lo : lo + HD, :]
        ws = [pt_ref[h, j] for j in range(4)]
        dps = [nn(pieces[j][:, k + lo : k + lo + HD], dot_) for j in range(4)]
        mean = sum(jnp.sum(ws[j].astype(F32) * dps[j], axis=0, keepdims=True) for j in range(4))
        dq = jnp.zeros((HD, n), F32)
        for j in range(4):
            ds = (ws[j].astype(F32) * (dps[j] - mean)).astype(BF)
            dq = dq + tn(pieces[j][:, lo : lo + HD], ds)
            target = near_ref if j < 2 else away_ref
            target[j % 2, :, lo : lo + HD] = nt(ds, qt) * scale
            target[j % 2, :, k + lo : k + lo + HD] = nt(ws[j], dot_)
        dqs.append(dq * scale)
    dq_ref[...] = jnp.transpose(jnp.concatenate(dqs, axis=0)).astype(BF)


def mixing_back_body(normed_ref, dq_ref, near_ref, sib_ref, far_ref, w_ref, mg_ref, gn_ref):
    kv = (near_ref[0] + sib_ref[0] + far_ref[...].astype(F32)).astype(BF)
    g = jnp.concatenate([dq_ref[...], kv], axis=1)
    mg_ref[...] = tn(normed_ref[...], g)
    gn_ref[...] = nt(g, w_ref[:, : g.shape[1]]).astype(BF)


def expert_grad_body(c_ref, half, act_ref, actx_ref, gh_ref, ghx_ref, r_ref, rx_ref, g_ref, gx_ref, up_ref, down_ref):
    e = pl.program_id(0)
    c = c_ref[0]
    q = up_ref.shape[1]

    def emit(a, g, rows, grads):
        n = a.shape[0]
        rows = rows.reshape(n, 2 * q)
        grads = grads.reshape(n, 2 * q)
        rows = jnp.where(c == 0, rows[:, :q], rows[:, q:])
        grads = jnp.where(c == 0, grads[:, :q], grads[:, q:])
        up_ref[0] = tn(rows, g)
        down_ref[0] = tn(a, grads)

    own = lax.div(e, half) == c

    @pl.when(own)
    def _():
        emit(act_ref[0], gh_ref[0], r_ref[...], g_ref[...])

    @pl.when(jnp.logical_not(own))
    def _():
        emit(actx_ref[0], ghx_ref[0], rx_ref[...], gx_ref[...])


def mix_body(zs, cap, br_ref, tok_ref, t_ref, as_ref, res_ref, mi_ref, gate_ref, s_ref, summed, parts, send, recv):
    greet(z_peers(zs))
    sum_over_z(zs, br_ref, summed, parts, send, recv)
    residual = tok_ref[...].astype(F32) + summed[...].astype(F32)
    res_ref[...] = residual
    xhat, _ = norm_parts(residual)
    mixed_in = (xhat * t_ref[33:34, :].astype(F32)).astype(BF)
    mi_ref[...] = mixed_in
    hot, slot = route(as_ref[...], 32, cap)
    rows = nn(hot.astype(BF), t_ref[0:32, :])
    logit = jnp.sum(mixed_in.astype(F32) * rows, axis=-1, keepdims=True)
    gate_ref[...] = jax.nn.sigmoid(logit)
    slot_rows(slot, mixed_in, 32 * cap, s_ref)


def loss_body(zs, cap, rb_ref, res_ref, gate_ref, as_ref, valid_ref, at_ref, tea_ref, cot_ref,
              act_ref, gm_ref, gl_ref, stat_ref, s_ref, partial_rows, summed, parts, send, recv):
    greet(z_peers(zs))
    hot, slot = route(as_ref[...], 32, cap)
    partial_rows[...] = token_rows(slot, rb_ref, 32 * cap).astype(BF)
    sum_over_z(zs, partial_rows, summed, parts, send, recv)
    returned = summed[...].astype(F32)
    gate = gate_ref[...]
    d = returned.shape[1]
    mixed = res_ref[...] + gate * returned
    act_ref[...] = mixed.astype(BF)
    diff = mixed - tea_ref[...].astype(F32)
    valid = to_col(valid_ref[pl.ds(at_ref[6], 1), :])
    scale = 1.0 / (jnp.sum(valid_ref[...]) * d)
    weighted = valid * diff
    grad = cot_ref[...].astype(F32) + 2.0 * weighted * scale
    gm_ref[...] = grad
    grad_gate = jnp.sum(grad * returned, axis=-1, keepdims=True)
    gl_ref[...] = grad_gate * gate * (1.0 - gate)
    stat_ref[...] = jnp.zeros_like(stat_ref)
    stat_ref[0:1, 0:32] = jnp.sum(hot, axis=0, keepdims=True)
    stat_ref[1:2, 0:32] = jnp.sum(hot * gate, axis=0, keepdims=True)
    stat_ref[2:3, :] = jnp.broadcast_to(jnp.sum(weighted * diff * scale), (1, 128))
    slot_rows(slot, (gate * grad).astype(BF), 32 * cap, s_ref)


def norm2_body(zs, cap, rb_ref, res_ref, mi_ref, gm_ref, gl_ref, as_ref, t_ref,
               gr_ref, gb_ref, cg_ref, g2_ref, partial_rows, summed, parts, send, recv):
    greet(z_peers(zs))
    hot, slot = route(as_ref[...], 32, cap)
    partial_rows[...] = token_rows(slot, rb_ref, 32 * cap).astype(BF)
    sum_over_z(zs, partial_rows, summed, parts, send, recv)
    gl = gl_ref[...]
    rows = nn(hot.astype(BF), t_ref[0:32, :])
    grad_in = summed[...].astype(F32) + gl * rows
    cg_ref[...] = _dot(mi_ref[...].astype(F32), hot * gl, 0, 0, TOP)
    xhat, inv = norm_parts(res_ref[...])
    g2_ref[...] = jnp.broadcast_to(jnp.sum(grad_in * xhat, axis=0, keepdims=True), g2_ref.shape)
    grad = gm_ref[...] + norm_back(grad_in, xhat, inv, t_ref[33:34, :].astype(F32))
    gr_ref[...] = grad
    gb_ref[...] = grad.astype(BF)


def norm1_body(zs, gn_ref, tok_ref, t_ref, gr_ref, tg_ref, g1_ref, summed, parts, send, recv):
    greet(z_peers(zs))
    sum_over_z(zs, gn_ref, summed, parts, send, recv)
    grad = summed[...].astype(F32)
    xhat, inv = norm_parts(tok_ref[...].astype(F32))
    g1_ref[...] = jnp.broadcast_to(jnp.sum(grad * xhat, axis=0, keepdims=True), g1_ref.shape)
    tg_ref[...] = (gr_ref[...] + norm_back(grad, xhat, inv, t_ref[32:33, :].astype(F32))).astype(BF)


def expert_body(back, fs, *refs):
    if back:
        (s_ref, up_ref, upx_ref, dn_ref, dnx_ref, gp_ref, st_ref,
         rb_ref, h_ref, r_ref, sto_ref,
         wu, wd, ps, pr, ret, stin, wsem, d_s, d_r, x_s, x_r, b_s, b_r, t_s, t_r) = refs
    else:
        (s_ref, up_ref, upx_ref, dn_ref, dnx_ref,
         rb_ref, h_ref, r_ref, gp_ref,
         wu, wd, ps, pr, ret, wsem, d_s, d_r, x_s, x_r, b_s, b_r) = refs
    f, i, z = lax.axis_index("fsdp"), lax.axis_index("ctx"), lax.axis_index("tp")
    y, c = lax.div(i, 2), lax.rem(i, 2)
    me = f * 4 + i
    half, width = wu.shape[0], up_ref.shape[1]
    sources, _, dh = r_ref.shape
    cap = 16
    n = sources * cap
    peers = group_peers(fs)
    across = (f, (1 - y) * 2 + c, z)

    own = pl.ds(pl.multiple_of(c * width, 64), width)
    other = pl.ds(pl.multiple_of((1 - c) * width, 64), width)
    mine = pl.ds(c * half, half)
    loads = [
        pltpu.make_async_copy(up_ref.at[mine], wu.at[:, own, :], wsem.at[0]),
        pltpu.make_async_copy(upx_ref, wu.at[:, other, :], wsem.at[1]),
        pltpu.make_async_copy(dn_ref.at[mine], wd.at[c], wsem.at[2]),
        pltpu.make_async_copy(dnx_ref, wd.at[1 - c], wsem.at[3]),
        pltpu.make_async_copy(s_ref.at[f, y, c], r_ref.at[me], wsem.at[4]),
    ]
    for cp in loads:
        cp.start()
    greet([p[3] for p in peers])
    out = []
    for k, (fp, yp, cp_, peer) in enumerate(peers):
        cp = remote(s_ref.at[fp, yp, cp_], r_ref.at[me], d_s.at[k], d_r.at[k], peer)
        cp.start()
        out.append(cp)
    stats = []
    if back:
        for k, (fp, yp, cp_, peer) in enumerate(peers):
            cp = remote(st_ref, stin.at[me], t_s.at[k], t_r.at[k], peer)
            cp.start()
            stats.append(cp)
    for cp in loads:
        cp.wait()
    for cp in out:
        cp.wait_recv()

    def cross(e):
        return remote(ps.at[e], pr.at[e], x_s.at[e], x_r.at[e], across)

    def rows_of(e):
        return r_ref[:, pl.ds(pl.multiple_of(e * cap, cap), cap), :].reshape(n, dh)

    @pl.loop(0, half)
    def _(e):
        rows = rows_of(e)
        if back:
            part = nt(rows[:, :width], wd[0, e]) + nt(rows[:, width:], wd[1, e])
        else:
            part = nn(rows, wu[e])
        ps[e] = part.astype(BF)
        cross(e).start()

    @pl.loop(0, half)
    def _(e):
        cross(e).wait_recv()
        total = ps[e].astype(F32) + pr[e].astype(F32)
        if back:
            grad = (total * gp_ref[e].astype(F32)).astype(BF)
            h_ref[e] = grad
            rows = nt(grad, wu[e])
        else:
            phi = 0.5 * (1.0 + lax.erf(total * math.sqrt(0.5)))
            act = (total * phi).astype(BF)
            h_ref[e] = act
            bell = jnp.exp(-0.5 * total * total) * (1.0 / math.sqrt(2.0 * math.pi))
            gp_ref[e] = (phi + total * bell).astype(BF)
            rows = jnp.concatenate([nn(act, wd[0, e]), nn(act, wd[1, e])], axis=1)
        ret[:, pl.ds(pl.multiple_of(e * cap, cap), cap), :] = rows.astype(BF).reshape(sources, cap, dh)

    keep = pltpu.make_async_copy(ret.at[me], rb_ref.at[me], wsem.at[5])
    keep.start()
    returns = []
    for k, (fp, yp, cp_, peer) in enumerate(peers):
        cp = remote(ret.at[fp * 4 + yp * 2 + cp_], rb_ref.at[me], b_s.at[k], b_r.at[k], peer)
        cp.start()
        returns.append(cp)
    if back:
        stin[me] = st_ref[...]
        for cp in stats:
            cp.wait_recv()
        total = stin[0]
        for k in range(1, sources):
            total = total + stin[k]
        sto_ref[...] = total
    keep.wait()
    for cp in returns:
        cp.wait_recv()
    for cp in out + returns + stats:
        cp.wait_send()

    @pl.loop(0, half)
    def _(e):
        cross(e).wait_send()


def expert_call(back, fs, s, up, upx, dn, dnx, extra, cid):
    experts, width, units = up.shape
    half = experts // 2
    sources = fs * 4
    cap = 16
    n = sources * cap
    dh = 2 * width
    row = (sources, half * cap, dh)
    hid = (half, n, units)
    outs = [sds(row, BF), sds(hid, BF), sds(row, BF)]
    outs.append(sds((8, 128), F32) if back else sds(hid, BF))
    peers = sources - 1
    dma = pltpu.SemaphoreType.DMA
    scratch = [
        VMEM((half, dh, units), BF),
        VMEM((2, half, units, width), BF),
        VMEM(hid, BF),
        VMEM(hid, BF),
        VMEM(row, BF),
    ]
    if back:
        scratch.append(VMEM((sources, 8, 128), F32))
    scratch += [dma((6,))] + [dma((peers,))] * 2 + [dma((half,))] * 2 + [dma((peers,))] * 2
    if back:
        scratch += [dma((peers,))] * 2
    anyspec = pl.BlockSpec(memory_space=ANY)
    return pl.pallas_call(
        partial(expert_body, back, fs),
        out_shape=outs,
        in_specs=[vspec()] + [anyspec] * 4 + [vspec()] * len(extra),
        out_specs=[vspec()] * len(outs),
        scratch_shapes=scratch,
        compiler_params=params(cid),
        name="experts_back" if back else "experts",
    )(s, up, upx, dn, dnx, *extra)


def per_device(tokens, mixing_weight, output_weight, first_gain, second_gain, centroids, expert_up,
               expert_down, prefix_length, assignment, validity, teacher, cotangent):
    fs, zs = lax.axis_size("fsdp"), lax.axis_size("tp")
    f, i = lax.axis_index("fsdp"), lax.axis_index("ctx")
    c = lax.rem(i, 2)
    y = lax.div(i, 2)
    n, d = tokens.shape[1], tokens.shape[2]
    rows = mixing_weight.shape[0]
    k = mixing_weight.shape[2]
    local_experts, width, units = expert_up.shape
    half = local_experts // 2
    experts = centroids.shape[0]
    cap = 2 * n // experts
    sources = fs * 4
    core_pairs = [(0, 1), (1, 0), (2, 3), (3, 2)]
    y_pairs = [(0, 2), (2, 0), (1, 3), (3, 1)]

    def core_swap(v):
        return lax.ppermute(v, "ctx", core_pairs)

    def y_swap(v):
        return lax.ppermute(v, "ctx", y_pairs)

    packed = jnp.zeros((rows, COLS), BF)
    packed = jnp.concatenate(
        [
            mixing_weight.reshape(rows, 3 * k),
            jnp.zeros((rows, OUT_AT - 3 * k), BF),
            output_weight.T,
            centroids.T,
            first_gain[:, None],
            second_gain[:, None],
            jnp.zeros((rows, COLS - CEN_AT - experts - 2), BF),
        ],
        axis=1,
    )
    pad_rows = -rows % 16 + 16
    last = jnp.pad(validity.astype(BF), ((0, pad_rows - 1), (0, COLS - n)))
    gathered = lax.all_gather(jnp.concatenate([packed, last], axis=0), ("fsdp", "ctx"), axis=0)
    weights = gathered[:, :rows].reshape(d, COLS)
    valid_all = gathered[:, rows, :n].astype(F32)
    table = weights[:, CEN_AT:].T
    table = jnp.pad(table, ((0, 0), (0, 0)))

    up_x = core_swap(lax.dynamic_slice_in_dim(expert_up, (1 - c) * half, half, 0))
    dn_x = core_swap(lax.dynamic_slice_in_dim(expert_down, (1 - c) * half, half, 0))

    tok = tokens[0]
    normed, qt, kv = pl.pallas_call(
        project_body,
        out_shape=[sds((n, d), BF), sds((k, n), BF), sds((n, 2 * k), BF)],
        in_specs=[vspec()] * 3,
        out_specs=[vspec()] * 3,
        compiler_params=params(),
        name="project",
    )(tok, weights, table)
    kv_far = y_swap(kv)
    kv_sib = core_swap(jnp.stack([kv, kv_far]))
    own_valid = lax.dynamic_slice_in_dim(valid_all, f * 4, 4, 0)
    far, sib = i + 2 - 4 * y, i + 1 - 2 * c
    sib_far = sib + 2 - 4 * y
    at = jnp.stack([i, prefix_length[0], i, far, sib, sib_far, f * 4 + i]).astype(jnp.int32)
    smem = pl.BlockSpec(memory_space=pltpu.SMEM)
    heads = k // HD
    pt, ctx, branch = pl.pallas_call(
        attend_body,
        out_shape=[sds((heads, 4, n, n), BF), sds((n, k), BF), sds((n, d), BF)],
        in_specs=[smem] + [vspec()] * 6,
        out_specs=[vspec()] * 3,
        compiler_params=params(),
        name="attend",
    )(at, qt, kv, kv_far, kv_sib, own_valid, weights)

    chosen = assignment[0]
    row_shape = (fs, 2, 2, half * cap, d // 2)
    summed = [VMEM((n, d), BF)] + sum_scratch(zs, n, d)
    residual, mixed_in, gate, slots = pl.pallas_call(
        partial(mix_body, zs, cap),
        out_shape=[sds((n, d), F32), sds((n, d), BF), sds((n, 1), F32), sds(row_shape, BF)],
        in_specs=[vspec()] * 4,
        out_specs=[vspec()] * 4,
        scratch_shapes=summed,
        compiler_params=params(1),
        name="mix",
    )(branch, tok, table, chosen)
    back_rows, act, received, gelu_slope = expert_call(
        False, fs, slots, expert_up, up_x, expert_down, dn_x, (), 2
    )
    activations, grad_mixed, grad_logit, stat, grad_slots = pl.pallas_call(
        partial(loss_body, zs, cap),
        out_shape=[sds((n, d), BF), sds((n, d), F32), sds((n, 1), F32), sds((8, 128), F32), sds(row_shape, BF)],
        in_specs=[vspec()] * 5 + [smem] + [vspec()] * 2,
        out_specs=[vspec()] * 5,
        scratch_shapes=[VMEM((n, d), BF)] + summed,
        compiler_params=params(3),
        name="losses",
    )(back_rows, residual, gate, chosen, valid_all, at, teacher[0], cotangent[0])
    back_grads, grad_hidden, grad_received, stats = expert_call(
        True, fs, grad_slots, expert_up, up_x, expert_down, dn_x, (gelu_slope, stat), 4
    )
    all_tokens = float(n * sources)
    share = stats[0, :experts] / all_tokens - 1.0 / experts
    balance = experts * experts * jnp.sum(share * stats[1, :experts] / all_tokens)
    distill = stats[2, 0]

    act_x, gh_x, rec_x, grec_x = (
        core_swap(act), core_swap(grad_hidden), core_swap(received), core_swap(grad_received)
    )
    grad_residual, grad_branch, centre_grad, g2 = pl.pallas_call(
        partial(norm2_body, zs, cap),
        out_shape=[sds((n, d), F32), sds((n, d), BF), sds((d, experts), F32), sds((8, d), F32)],
        in_specs=[vspec()] * 7,
        out_specs=[vspec()] * 4,
        scratch_shapes=[VMEM((n, d), BF)] + summed,
        compiler_params=params(5),
        name="norm_two",
    )(back_grads, residual, mixed_in, grad_mixed, grad_logit, chosen, table)
    dq, near, away, out_grad = pl.pallas_call(
        attend_back_body,
        out_shape=[sds((n, k), BF), sds((2, n, 2 * k), F32), sds((2, n, 2 * k), F32), sds((d, k), F32)],
        in_specs=[vspec()] * 8,
        out_specs=[vspec()] * 4,
        compiler_params=params(),
        name="attend_back",
    )(grad_branch, qt, kv, kv_far, kv_sib, pt, ctx, weights)
    near_sib = core_swap(away)
    near_far = y_swap((near[1] + near_sib[1]).astype(BF))
    mix_grad, gn = pl.pallas_call(
        mixing_back_body,
        out_shape=[sds((d, 3 * k), F32), sds((n, d), BF)],
        in_specs=[vspec()] * 6,
        out_specs=[vspec()] * 2,
        compiler_params=params(),
        name="mixing_back",
    )(normed, dq, near, near_sib, near_far, weights)

    sums = jnp.concatenate([mix_grad, out_grad, centre_grad], axis=1).reshape(fs, 2, 2, rows, 3 * k + k + experts)
    keep = lax.dynamic_index_in_dim(sums, c, 2, keepdims=False)
    give = lax.dynamic_index_in_dim(sums, 1 - c, 2, keepdims=False)
    sums = keep + core_swap(give)
    sums = lax.dynamic_index_in_dim(sums, y, 1, keepdims=False) + y_swap(
        lax.dynamic_index_in_dim(sums, 1 - y, 1, keepdims=False).astype(BF)
    ).astype(F32)
    total = lax.dynamic_index_in_dim(sums, f, 0, keepdims=False)
    for s in range(1, fs):
        piece = lax.dynamic_index_in_dim(sums, lax.rem(f + s, fs), 0, keepdims=False).astype(BF)
        total = total + lax.ppermute(piece, "fsdp", [(a, (a + s) % fs) for a in range(fs)]).astype(F32)

    tokens_gradient, g1 = pl.pallas_call(
        partial(norm1_body, zs),
        out_shape=[sds((n, d), BF), sds((8, d), F32)],
        in_specs=[vspec()] * 4,
        out_specs=[vspec()] * 2,
        scratch_shapes=summed,
        compiler_params=params(6),
        name="norm_one",
    )(gn, tok, table, grad_residual)
    gains = lax.psum_scatter(jnp.stack([g1[0], g2[0]]), ("fsdp", "ctx"), scatter_dimension=1, tiled=True)

    block = lambda e, *_: (e % half, 0, 0)
    slab = lambda e, *_: (0, e % half, 0)
    slots_in = sources * cap
    up_gradient, down_gradient = pl.pallas_call(
        lambda c_ref, *refs: expert_grad_body(c_ref, half, *refs),
        grid_spec=pltpu.PrefetchScalarGridSpec(
            num_scalar_prefetch=1,
            grid=(local_experts,),
            in_specs=[pl.BlockSpec((1, slots_in, units), block)] * 4
            + [pl.BlockSpec((sources, cap, 2 * width), slab)] * 4,
            out_specs=[
                pl.BlockSpec((1, width, units), lambda e, *_: (e, 0, 0)),
                pl.BlockSpec((1, units, width), lambda e, *_: (e, 0, 0)),
            ],
        ),
        out_shape=[sds(expert_up.shape, F32), sds(expert_down.shape, F32)],
        compiler_params=params(),
        name="expert_grads",
    )(c.reshape(1), act, act_x, grad_hidden, gh_x, received, rec_x, grad_received, grec_x)

    return (
        activations[None],
        tokens_gradient[None],
        total[:, : 3 * k].reshape(rows, 3, k),
        total[:, 3 * k : 4 * k].T,
        gains[0],
        gains[1],
        total[:, 4 * k :].T,
        up_gradient,
        down_gradient,
        balance,
        distill,
    )


def solution(mesh):
    in_specs = (
        P("fsdp", "ctx", None),
        P(("fsdp", "ctx"), None, "tp"),
        P("tp", ("fsdp", "ctx")),
        P(("fsdp", "ctx")),
        P(("fsdp", "ctx")),
        P(None, ("fsdp", "ctx")),
        P("fsdp", "ctx", "tp"),
        P("fsdp", "tp", "ctx"),
        P("fsdp"),
        P("fsdp", "ctx", None),
        P("fsdp", "ctx"),
        P("fsdp", "ctx", None),
        P("fsdp", "ctx", None),
    )
    out_specs = (
        P("fsdp", "ctx", None),
        P("fsdp", "ctx", None),
        P(("fsdp", "ctx"), None, "tp"),
        P("tp", ("fsdp", "ctx")),
        P(("fsdp", "ctx")),
        P(("fsdp", "ctx")),
        P(None, ("fsdp", "ctx")),
        P("fsdp", "ctx", "tp"),
        P("fsdp", "tp", "ctx"),
        P(),
        P(),
    )
    return jax.shard_map(
        per_device, mesh=mesh, in_specs=in_specs, out_specs=out_specs, check_vma=False
    )
```

```python
from functools import partial
import math

import jax
import jax.numpy as jnp
from jax import lax
from jax.experimental import pallas as pl
from jax.experimental.pallas import tpu as pltpu
from jax.sharding import PartitionSpec as P

HD = 64
EPSILON = 1e-05
BF = jnp.bfloat16
F32 = jnp.float32
MESH = pl.DeviceIdType.MESH
TOP = lax.Precision.HIGHEST
VMEM = pltpu.VMEM
ANY = pl.ANY
CAP = 16
EXP = 32
TAB = 48


def _dot(a, b, ca, cb, precision=None):
    return lax.dot_general(
        a, b, (((ca,), (cb,)), ((), ())), preferred_element_type=F32, precision=precision
    )


def nn(a, b):
    return _dot(a, b, 1, 0)


def nt(a, b):
    return _dot(a, b, 1, 1)


def tn(a, b):
    return _dot(a, b, 0, 0)


def vspec():
    return pl.BlockSpec(memory_space=VMEM)


def sds(shape, dtype):
    return jax.ShapeDtypeStruct(shape, dtype)


def params(cid=None, mib=56):
    if cid is None:
        return pltpu.CompilerParams(vmem_limit_bytes=mib * 2**20)
    return pltpu.CompilerParams(
        vmem_limit_bytes=mib * 2**20, collective_id=cid, has_side_effects=True
    )


def iota(shape, dim):
    return lax.broadcasted_iota(jnp.int32, shape, dim)


def to_col(row):
    n = row.shape[1]
    return jnp.sum(jnp.where(iota((n, n), 0) == iota((n, n), 1), row, 0.0), axis=1, keepdims=True)


def to_row(col):
    n = col.shape[0]
    return jnp.sum(jnp.where(iota((n, n), 0) == iota((n, n), 1), col, 0.0), axis=0, keepdims=True)


def norm_parts(x):
    c = x - jnp.mean(x, axis=-1, keepdims=True)
    inv = lax.rsqrt(jnp.mean(c * c, axis=-1, keepdims=True) + EPSILON)
    return c * inv, inv


def norm_back(grad, xhat, inv, gain):
    gx = grad * gain
    return inv * (
        gx
        - jnp.mean(gx, axis=-1, keepdims=True)
        - xhat * jnp.mean(gx * xhat, axis=-1, keepdims=True)
    )


def route(chosen):
    n = chosen.shape[1]
    chosen = to_col(chosen.astype(F32))
    hot = (chosen == iota((n, EXP), 1).astype(F32)).astype(F32)
    lower = (iota((n, n), 1) < iota((n, n), 0)).astype(BF)
    earlier = nn(lower, hot.astype(BF))
    rank = jnp.sum(earlier * hot, axis=1, keepdims=True)
    return hot, chosen * CAP + rank


def slot_rows(slot, rows, s_ref):
    n, d = rows.shape
    place = (iota((EXP * CAP, n), 0).astype(F32) == to_row(slot)).astype(BF)
    filled = nn(place, rows).astype(BF)
    fs, _, _, r, h = s_ref.shape
    for f in range(fs):
        for c in range(2):
            at = (f * 2 + c) * r
            for y in range(2):
                s_ref[f, y, c] = filled[at : at + r, y * h : (y + 1) * h]


def token_rows(slot, rb_ref):
    n = slot.shape[0]
    sources = rb_ref.shape[0]
    parts = []
    for f in range(sources // 4):
        for c in range(2):
            parts.append(
                jnp.concatenate([rb_ref[f * 4 + c], rb_ref[f * 4 + 2 + c]], axis=1)
            )
    rows = jnp.concatenate(parts, axis=0)
    place = (iota((n, EXP * CAP), 1).astype(F32) == slot).astype(BF)
    return nn(place, rows)


def z_peers(zs):
    f, i, z = lax.axis_index("fsdp"), lax.axis_index("ctx"), lax.axis_index("tp")
    return [(f, i, lax.rem(z + s, zs)) for s in range(1, zs)]


def greet(peers):
    barrier = pltpu.get_barrier_semaphore()
    for peer in peers:
        pl.semaphore_signal(barrier, inc=1, device_id=peer, device_id_type=MESH)
    pl.semaphore_wait(barrier, len(peers))


def remote(src, dst, send, recv, peer):
    return pltpu.make_async_remote_copy(
        src_ref=src, dst_ref=dst, send_sem=send, recv_sem=recv, device_id=peer, device_id_type=MESH
    )


def sum_over_z(zs, x_ref, o_ref, parts, send, recv):
    z = lax.axis_index("tp")
    n = x_ref.shape[0] // zs
    peers = z_peers(zs)

    def chunk(at):
        return pl.ds(pl.multiple_of(at * n, n), n)

    first = []
    for s in range(1, zs):
        to = lax.rem(z + s, zs)
        cp = remote(x_ref.at[chunk(to)], parts.at[s - 1], send.at[0, s - 1], recv.at[0, s - 1], peers[s - 1])
        cp.start()
        first.append(cp)
    total = x_ref[chunk(z), :].astype(F32)
    for s in range(1, zs):
        first[s - 1].wait_recv()
        total = total + parts[s - 1].astype(F32)
    o_ref[chunk(z), :] = total.astype(BF)
    second = []
    for s in range(1, zs):
        cp = remote(o_ref.at[chunk(z)], o_ref.at[chunk(z)], send.at[1, s - 1], recv.at[1, s - 1], peers[s - 1])
        cp.start()
        second.append(cp)
    for cp in second:
        cp.wait_recv()
    for cp in first + second:
        cp.wait_send()


def sum_scratch(zs, n, d):
    return [
        VMEM((zs - 1, n // zs, d), BF),
        pltpu.SemaphoreType.DMA((2, zs - 1)),
        pltpu.SemaphoreType.DMA((2, zs - 1)),
    ]


def group_peers(fs):
    f, i, z = lax.axis_index("fsdp"), lax.axis_index("ctx"), lax.axis_index("tp")
    y, c = lax.div(i, 2), lax.rem(i, 2)
    out = []
    for df in range(fs):
        for dy in range(2):
            for dc in range(2):
                if df or dy or dc:
                    fp = lax.rem(f + df, fs)
                    yp = y if dy == 0 else 1 - y
                    cp = c if dc == 0 else 1 - c
                    out.append((fp, yp, cp, (fp, yp * 2 + cp, z)))
    return out


def attend(mine, prefix, offsets, qt_ref, kv_ref, valid_ref, row0, pt_ref):
    k, n = qt_ref.shape
    query = iota((n, n), 1) + mine * n
    allowed = []
    for j in range(4):
        key = iota((n, n), 0) + offsets[j] * n
        col = to_col(valid_ref[pl.ds(row0 + offsets[j], 1), :])
        allowed.append(((key <= query) | (key < prefix)) & ((col > 0.5) | (key == query)))
    outs = []
    for h in range(k // HD):
        lo = h * HD
        qt = qt_ref[lo : lo + HD, :]
        scores = [
            jnp.where(allowed[j], nn(kv_ref[j, :, lo : lo + HD], qt) * (1.0 / math.sqrt(HD)), -1e30)
            for j in range(4)
        ]
        top = jnp.max(scores[0], axis=0, keepdims=True)
        for j in range(1, 4):
            top = jnp.maximum(top, jnp.max(scores[j], axis=0, keepdims=True))
        exps = [jnp.exp(s - top) for s in scores]
        share = 1.0 / sum(jnp.sum(e, axis=0, keepdims=True) for e in exps)
        acc = jnp.zeros((HD, n), F32)
        for j in range(4):
            w = (exps[j] * share).astype(BF)
            pt_ref[h, j] = w
            acc = acc + tn(kv_ref[j, :, k + lo : k + lo + HD], w)
        outs.append(acc)
    return jnp.transpose(jnp.concatenate(outs, axis=0)).astype(BF)


def attend_back(gct, qt_ref, kv_ref, pt_ref, near_ref, away_ref):
    k, n = qt_ref.shape
    scale = 1.0 / math.sqrt(HD)
    dqs = []
    for h in range(k // HD):
        lo = h * HD
        dot_ = gct[lo : lo + HD, :]
        qt = qt_ref[lo : lo + HD, :]
        ws = [pt_ref[h, j] for j in range(4)]
        dps = [nn(kv_ref[j, :, k + lo : k + lo + HD], dot_) for j in range(4)]
        mean = sum(jnp.sum(ws[j].astype(F32) * dps[j], axis=0, keepdims=True) for j in range(4))
        dq = jnp.zeros((HD, n), F32)
        for j in range(4):
            ds = (ws[j].astype(F32) * (dps[j] - mean)).astype(BF)
            dq = dq + tn(kv_ref[j, :, lo : lo + HD], ds)
            target = near_ref if j < 2 else away_ref
            target[j % 2, :, lo : lo + HD] = nt(ds, qt) * scale
            target[j % 2, :, k + lo : k + lo + HD] = nt(ws[j], dot_)
        dqs.append(dq * scale)
    return jnp.transpose(jnp.concatenate(dqs, axis=0)).astype(BF)


def expert_grad_body(c_ref, half, l_ref, lx_ref, r_ref, rx_ref, out_ref):
    e = pl.program_id(0)
    c = c_ref[0]
    q = out_ref.shape[1]

    def emit(left, right):
        left = left.reshape(right.shape[0], 2 * q)
        left = jnp.where(c == 0, left[:, :q], left[:, q:])
        out_ref[0] = tn(left, right)

    own = lax.div(e, half) == c

    @pl.when(own)
    def _():
        emit(l_ref[...], r_ref[0])

    @pl.when(jnp.logical_not(own))
    def _():
        emit(lx_ref[...], rx_ref[0])


def expert_grads(c, left, left_x, right, right_x, name):
    half, n, units = right.shape
    sources, _, dh = left.shape
    own = lambda e, c_ref: jnp.clip(e - c_ref[0] * half, 0, half - 1)
    sib = lambda e, c_ref: jnp.clip(e - (1 - c_ref[0]) * half, 0, half - 1)
    return pl.pallas_call(
        lambda c_ref, *refs: expert_grad_body(c_ref, half, *refs),
        grid_spec=pltpu.PrefetchScalarGridSpec(
            num_scalar_prefetch=1,
            grid=(2 * half,),
            in_specs=[
                pl.BlockSpec((sources, CAP, dh), lambda e, c_ref: (0, own(e, c_ref), 0)),
                pl.BlockSpec((sources, CAP, dh), lambda e, c_ref: (0, sib(e, c_ref), 0)),
                pl.BlockSpec((1, n, units), lambda e, c_ref: (own(e, c_ref), 0, 0)),
                pl.BlockSpec((1, n, units), lambda e, c_ref: (sib(e, c_ref), 0, 0)),
            ],
            out_specs=pl.BlockSpec((1, dh // 2, units), lambda e, c_ref: (e, 0, 0)),
        ),
        out_shape=sds((2 * half, dh // 2, units), F32),
        compiler_params=params(),
        cost_estimate=pl.CostEstimate(
            flops=4 * half * n * units * dh, bytes_accessed=2 * half * dh * units * 3, transcendentals=0
        ),
        name=name,
    )(c.reshape(1), left, left_x, right, right_x)


def reduce_body(zs, fs, rows, k, experts, *refs):
    own_ref, z_refs = refs[0], refs[1:zs]
    kept_ref, g_refs = refs[zs], refs[zs + 1 : zs + 2 * fs]
    chunk_ref, mix_ref, out_ref, cen_ref, g2_ref = refs[zs + 2 * fs :]
    total = own_ref[...].astype(F32)
    for r in z_refs:
        total = total + r[...].astype(F32)
    n, d = total.shape
    dense = kept_ref[...]
    for r in g_refs:
        dense = dense + r[...].astype(F32)
    for j in range(3):
        mix_ref[j] = dense[:rows, j * k : (j + 1) * k]
    out_ref[...] = jnp.transpose(dense[:rows, 3 * k : 4 * k])
    cen_ref[...] = jnp.transpose(dense[:rows, 4 * k :])[:experts, :]
    last = kept_ref.shape[0] - 16
    g2_ref[...] = dense[last + 1 : last + 2, :rows]
    chunk_ref[0:n, :] = total.astype(BF)
    chunk_ref[n : n + 16, :] = jnp.concatenate(
        [dense[last : last + 16, :rows], jnp.zeros((16, d - rows), F32)], axis=1
    ).astype(BF)


def finish_body(zs, at_ref, tok_ref, t_ref, gr_ref, *refs):
    chunks, (tg_ref, g1_ref, full) = refs[:zs], refs[zs:]
    n = chunks[0].shape[0] - 16
    z = at_ref[0]
    g1 = jnp.zeros((1, full.shape[1]), F32)
    for s in range(zs):
        at = lax.rem(z - s + zs, zs)
        full[pl.ds(pl.multiple_of(at * n, n), n), :] = chunks[s][0:n, :].astype(F32)
        g1 = g1 + chunks[s][n : n + 1, :].astype(F32)
    g1_ref[...] = g1[:, : g1_ref.shape[1]]
    grad = full[...]
    xhat, inv = norm_parts(tok_ref[...].astype(F32))
    tg_ref[...] = (gr_ref[...] + norm_back(grad, xhat, inv, t_ref[32:33, :].astype(F32))).astype(BF)


def whereabouts():
    f, i, z = lax.axis_index("fsdp"), lax.axis_index("ctx"), lax.axis_index("tp")
    return f, i, z, lax.div(i, 2), lax.rem(i, 2)


def head_body(fs, zs, gather, *refs):
    if gather:
        (prefix_ref, tok_ref, mix_ref, ow_ref, small_ref, as_ref, up_ref, dn_ref,
         w3_ref, wo_ref, t_ref, valid_ref, upx_ref, dnx_ref,
         normed_ref, qt_ref, kv_ref, pt_ref, ctx_ref, res_ref, mi_ref, gate_ref, s_ref,
         small_all, branch, summed, parts, send, recv, wx_s, wx_r, kv_s, kv_r, p_s, p_r, q_s, q_r) = refs
    else:
        (prefix_ref, tok_ref, w3_ref, wo_ref, t_ref, valid_ref, as_ref, up_ref, dn_ref,
         upx_ref, dnx_ref,
         normed_ref, qt_ref, kv_ref, pt_ref, ctx_ref, res_ref, mi_ref, gate_ref, s_ref,
         branch, summed, parts, send, recv, wx_s, wx_r, kv_s, kv_r) = refs
    f, i, z, y, c = whereabouts()
    me = f * 4 + i
    half = upx_ref.shape[0]
    k = qt_ref.shape[0]
    sibling = (f, y * 2 + 1 - c, z)
    across = (f, (1 - y) * 2 + c, z)
    same = []
    for df in range(fs):
        for dy in range(2):
            if df or dy:
                fp = lax.rem(f + df, fs)
                yp = y if dy == 0 else 1 - y
                same.append(((fp, yp * 2 + c, z), df, dy))
    greeted = same if gather else [s for s in same if s[1] == 0]
    greet([s[0] for s in greeted] + [sibling] + z_peers(zs))

    give = pl.ds((1 - c) * half, half)
    swaps = [
        remote(up_ref.at[give], upx_ref, wx_s.at[0], wx_r.at[0], sibling),
        remote(dn_ref.at[give], dnx_ref, wx_s.at[1], wx_r.at[1], sibling),
    ]
    waits = []
    xhat, _ = norm_parts(tok_ref[...].astype(F32))
    if gather:
        rows = mix_ref.shape[1]

        def places(at):
            span = pl.ds(pl.multiple_of(at * rows, rows), rows)
            return [w3_ref.at[:, span, :], wo_ref.at[span, :], small_all.at[at]]

        span = pl.ds(pl.multiple_of(me * rows, rows), rows)
        w3_ref[:, span, :] = mix_ref[...]
        wo_ref[span, :] = jnp.transpose(ow_ref[...].astype(F32)).astype(BF)
        small_all[me] = small_ref[...]
        sends, relays = [], []
        for n_, (peer, df, dy) in enumerate(same):
            for m, ref in enumerate(places(me)):
                cp = remote(ref, ref, p_s.at[n_, m], p_r.at[n_, m], peer)
                cp.start()
                sends.append(cp)
        for m, ref in enumerate(places(me)):
            cp = remote(ref, ref, q_s.at[0, m], q_r.at[0, m], sibling)
            cp.start()
            relays.append(cp)
        for n_, (peer, df, dy) in enumerate(same):
            fp = lax.rem(f - df + fs, fs)
            yp = y if dy == 0 else 1 - y
            for m, ref in enumerate(places(fp * 4 + yp * 2 + c)):
                sends[n_ * 3 + m].wait_recv()
                cp = remote(ref, ref, q_s.at[n_ + 1, m], q_r.at[n_ + 1, m], sibling)
                cp.start()
                relays.append(cp)
        for cp in relays:
            cp.wait_recv()
        sources = fs * 4
        t_ref[...] = jnp.concatenate([small_all[s, :, :rows] for s in range(sources)], axis=1)
        for s in range(sources):
            valid_ref[s : s + 1, :] = small_all[s, 34:35, :].astype(F32)
        waits += sends + relays
    for cp in swaps:
        cp.start()
    normed = (xhat * t_ref[32:33, :].astype(F32)).astype(BF)
    normed_ref[...] = normed
    kv_ref[0, :, :k] = nn(normed, w3_ref[1]).astype(BF)
    kv_ref[0, :, k:] = nn(normed, w3_ref[2]).astype(BF)
    far = remote(kv_ref.at[0], kv_ref.at[1], kv_s.at[0], kv_r.at[0], across)
    sib = remote(kv_ref.at[0], kv_ref.at[2], kv_s.at[1], kv_r.at[1], sibling)
    far.start()
    sib.start()
    qt_ref[...] = jnp.transpose(nn(normed, w3_ref[0])).astype(BF)
    far.wait_recv()
    relay = remote(kv_ref.at[1], kv_ref.at[3], kv_s.at[2], kv_r.at[2], sibling)
    relay.start()
    sib.wait_recv()
    relay.wait_recv()
    offsets = [i, (1 - y) * 2 + c, y * 2 + 1 - c, (1 - y) * 2 + 1 - c]
    ctx = attend(i, prefix_ref[0], offsets, qt_ref, kv_ref, valid_ref, f * 4, pt_ref)
    ctx_ref[...] = ctx
    branch[...] = nt(ctx, wo_ref[...]).astype(BF)
    sum_over_z(zs, branch, summed, parts, send, recv)
    residual = tok_ref[...].astype(F32) + summed[...].astype(F32)
    res_ref[...] = residual
    xhat, _ = norm_parts(residual)
    mixed_in = (xhat * t_ref[33:34, :].astype(F32)).astype(BF)
    mi_ref[...] = mixed_in
    hot, slot = route(as_ref[...])
    rows_ = nn(hot.astype(BF), t_ref[0:EXP, :])
    logit = jnp.sum(mixed_in.astype(F32) * rows_, axis=-1, keepdims=True)
    gate_ref[...] = jax.nn.sigmoid(logit)
    slot_rows(slot, mixed_in, s_ref)
    for cp in swaps:
        cp.wait_recv()
    for cp in waits + swaps + [far, sib, relay]:
        cp.wait_send()


def loss_body(zs, rb_ref, res_ref, gate_ref, as_ref, valid_ref, tea_ref, cot_ref,
              act_ref, gm_ref, gl_ref, stat_ref, s_ref, partial_rows, summed, parts, send, recv):
    greet(z_peers(zs))
    f, i, _, _, _ = whereabouts()
    hot, slot = route(as_ref[...])
    partial_rows[...] = token_rows(slot, rb_ref).astype(BF)
    sum_over_z(zs, partial_rows, summed, parts, send, recv)
    returned = summed[...].astype(F32)
    gate = gate_ref[...]
    d = returned.shape[1]
    mixed = res_ref[...] + gate * returned
    act_ref[...] = mixed.astype(BF)
    diff = mixed - tea_ref[...].astype(F32)
    valid = to_col(valid_ref[pl.ds(f * 4 + i, 1), :])
    scale = 1.0 / (jnp.sum(valid_ref[...]) * d)
    weighted = valid * diff
    grad = cot_ref[...].astype(F32) + 2.0 * weighted * scale
    gm_ref[...] = grad
    grad_gate = jnp.sum(grad * returned, axis=-1, keepdims=True)
    gl_ref[...] = grad_gate * gate * (1.0 - gate)
    stat_ref[...] = jnp.zeros_like(stat_ref)
    stat_ref[0:1, 0:EXP] = jnp.sum(hot, axis=0, keepdims=True)
    stat_ref[1:2, 0:EXP] = jnp.sum(hot * gate, axis=0, keepdims=True)
    stat_ref[2:3, :] = jnp.broadcast_to(jnp.sum(weighted * diff * scale), (1, 128))
    slot_rows(slot, (gate * grad).astype(BF), s_ref)


def back_body(fs, zs, rows, rb_ref, res_ref, mi_ref, gm_ref, gl_ref, as_ref, tok_ref, t_ref, w3_ref, wo_ref,
              normed_ref, qt_ref, kv_ref, pt_ref, ctx_ref, *refs):
    gr_ref, own_ref = refs[0:2]
    z_refs = refs[2 : 1 + zs]
    kept_ref = refs[1 + zs]
    g_refs = refs[2 + zs : 1 + zs + 2 * fs]
    (partial_rows, summed, parts, near, away, away_in, far_out, far_in, gn, dense, dense_in,
     send, recv, k_s, k_r) = refs[1 + zs + 2 * fs :]
    f, i, z, y, c = whereabouts()
    sibling = (f, y * 2 + 1 - c, z)
    across = (f, (1 - y) * 2 + c, z)
    greet(z_peers(zs) + [sibling, across])
    hot, slot = route(as_ref[...])
    partial_rows[...] = token_rows(slot, rb_ref).astype(BF)
    sum_over_z(zs, partial_rows, summed, parts, send, recv)
    n, d = res_ref.shape
    k = qt_ref.shape[0]
    gl = gl_ref[...]
    grad_in = summed[...].astype(F32) + gl * nn(hot.astype(BF), t_ref[0:EXP, :])
    xhat, inv = norm_parts(res_ref[...])
    g2 = jnp.sum(grad_in * xhat, axis=0, keepdims=True)
    grad = gm_ref[...] + norm_back(grad_in, xhat, inv, t_ref[33:34, :].astype(F32))
    gr_ref[...] = grad
    gb = grad.astype(BF)
    gct = jnp.transpose(nn(gb, wo_ref[...])).astype(BF)
    dq = attend_back(gct, qt_ref, kv_ref, pt_ref, near, away)
    swap = remote(away, away_in, k_s.at[0], k_r.at[0], sibling)
    swap.start()
    og = tn(gb, ctx_ref[...])
    cg = _dot(mi_ref[...].astype(F32), hot * gl, 0, 0, TOP)
    swap.wait_recv()
    far_out[...] = (near[1] + away_in[1]).astype(BF)
    cross = remote(far_out, far_in, k_s.at[1], k_r.at[1], across)
    cross.start()
    normed = normed_ref[...]
    mg = [tn(normed, dq), None, None]
    gq = nt(dq, w3_ref[0])
    cross.wait_recv()
    kvg = (near[0] + away_in[0] + far_in[...].astype(F32)).astype(BF)
    mg[1] = tn(normed, kvg[:, :k])
    mg[2] = tn(normed, kvg[:, k:])
    partial_normed = gq + nt(kvg[:, :k], w3_ref[1]) + nt(kvg[:, k:], w3_ref[2])
    gn[...] = partial_normed.astype(BF)
    xhat, _ = norm_parts(tok_ref[...].astype(F32))
    g1 = jnp.sum(partial_normed * xhat, axis=0, keepdims=True)
    last = dense.shape[3] - 16
    dense[:, :, :, last:, :] = jnp.zeros((fs, 2, 2, 16, dense.shape[4]), F32)
    for s in range(4 * fs):
        at = (s // 4, s % 4 // 2, s % 2)
        lo = s * rows
        for j in range(3):
            dense[at[0], at[1], at[2], 0:rows, j * k : (j + 1) * k] = mg[j][lo : lo + rows, :]
        dense[at[0], at[1], at[2], 0:rows, 3 * k : 4 * k] = og[lo : lo + rows, :]
        dense[at[0], at[1], at[2], 0:rows, 4 * k :] = cg[lo : lo + rows, :]
        dense[at[0], at[1], at[2], last : last + 1, 0:rows] = g1[:, lo : lo + rows]
        dense[at[0], at[1], at[2], last + 1 : last + 2, 0:rows] = g2[:, lo : lo + rows]
    pair = remote(dense.at[:, :, 1 - c], dense_in, k_s.at[2], k_r.at[2], sibling)
    pair.start()
    m = n // zs
    own_ref[...] = gn[pl.ds(pl.multiple_of(z * m, m), m), :]
    for s in range(1, zs):
        to = lax.rem(z + s, zs)
        z_refs[s - 1][...] = gn[pl.ds(pl.multiple_of(to * m, m), m), :]
    pair.wait_recv()
    kept_ref[...] = dense[f, y, c] + dense_in[f, y]
    at = 0
    for df in range(fs):
        for dy in range(2):
            if df or dy:
                fp = lax.rem(f + df, fs)
                yp = y if dy == 0 else 1 - y
                g_refs[at][...] = (dense[fp, yp, c] + dense_in[fp, yp]).astype(BF)
                at += 1
    for cp in (swap, cross, pair):
        cp.wait_send()


def expert_body(back, fs, *refs):
    if back:
        (s_ref, up_ref, upx_ref, dn_ref, dnx_ref, gp_ref, st_ref,
         rb_ref, h_ref, r_ref, sto_ref,
         wu, wd, ps, pr, ret, stin, wsem, d_s, d_r, x_s, x_r, b_s, b_r, t_s, t_r) = refs
    else:
        (s_ref, up_ref, upx_ref, dn_ref, dnx_ref,
         rb_ref, h_ref, r_ref, gp_ref,
         wu, wd, ps, pr, ret, wsem, d_s, d_r, x_s, x_r, b_s, b_r) = refs
    f, i, z = lax.axis_index("fsdp"), lax.axis_index("ctx"), lax.axis_index("tp")
    y, c = lax.div(i, 2), lax.rem(i, 2)
    me = f * 4 + i
    half, width = wu.shape[0], up_ref.shape[1]
    sources, _, dh = r_ref.shape
    cap = CAP
    n = sources * cap
    peers = group_peers(fs)
    across = (f, (1 - y) * 2 + c, z)

    own = pl.ds(pl.multiple_of(c * width, 64), width)
    other = pl.ds(pl.multiple_of((1 - c) * width, 64), width)
    mine = pl.ds(c * half, half)
    loads = [
        pltpu.make_async_copy(up_ref.at[mine], wu.at[:, own, :], wsem.at[0]),
        pltpu.make_async_copy(upx_ref, wu.at[:, other, :], wsem.at[1]),
        pltpu.make_async_copy(dn_ref.at[mine], wd.at[:, own, :], wsem.at[2]),
        pltpu.make_async_copy(dnx_ref, wd.at[:, other, :], wsem.at[3]),
        pltpu.make_async_copy(s_ref.at[f, y, c], r_ref.at[me], wsem.at[4]),
    ]
    for cp in loads:
        cp.start()
    greet([p[3] for p in peers])
    out = []
    for k, (fp, yp, cp_, peer) in enumerate(peers):
        cp = remote(s_ref.at[fp, yp, cp_], r_ref.at[me], d_s.at[k], d_r.at[k], peer)
        cp.start()
        out.append(cp)
    stats = []
    if back:
        for k, (fp, yp, cp_, peer) in enumerate(peers):
            cp = remote(st_ref, stin.at[me], t_s.at[k], t_r.at[k], peer)
            cp.start()
            stats.append(cp)
    for cp in loads:
        cp.wait()
    for cp in out:
        cp.wait_recv()

    def cross(e):
        return remote(ps.at[e], pr.at[e], x_s.at[e], x_r.at[e], across)

    def rows_of(e):
        return r_ref[:, pl.ds(pl.multiple_of(e * cap, cap), cap), :].reshape(n, dh)

    @pl.loop(0, half)
    def _(e):
        rows = rows_of(e)
        if back:
            part = nn(rows, wd[e])
        else:
            part = nn(rows, wu[e])
        ps[e] = part.astype(BF)
        cross(e).start()

    @pl.loop(0, half)
    def _(e):
        cross(e).wait_recv()
        total = ps[e].astype(F32) + pr[e].astype(F32)
        if back:
            grad = (total * gp_ref[e].astype(F32)).astype(BF)
            h_ref[e] = grad
            rows = nt(grad, wu[e])
        else:
            phi = 0.5 * (1.0 + lax.erf(total * math.sqrt(0.5)))
            act = (total * phi).astype(BF)
            h_ref[e] = act
            bell = jnp.exp(-0.5 * total * total) * (1.0 / math.sqrt(2.0 * math.pi))
            gp_ref[e] = (phi + total * bell).astype(BF)
            rows = nt(act, wd[e])
        ret[:, pl.ds(pl.multiple_of(e * cap, cap), cap), :] = rows.astype(BF).reshape(sources, cap, dh)

    keep = pltpu.make_async_copy(ret.at[me], rb_ref.at[me], wsem.at[5])
    keep.start()
    returns = []
    for k, (fp, yp, cp_, peer) in enumerate(peers):
        cp = remote(ret.at[fp * 4 + yp * 2 + cp_], rb_ref.at[me], b_s.at[k], b_r.at[k], peer)
        cp.start()
        returns.append(cp)
    if back:
        stin[me] = st_ref[...]
        for cp in stats:
            cp.wait_recv()
        total = stin[0]
        for k in range(1, sources):
            total = total + stin[k]
        sto_ref[...] = total
    keep.wait()
    for cp in returns:
        cp.wait_recv()
    for cp in out + returns + stats:
        cp.wait_send()

    @pl.loop(0, half)
    def _(e):
        cross(e).wait_send()


def expert_call(back, fs, s, up, upx, dn, dnx, extra, cid):
    experts, width, units = up.shape
    half = experts // 2
    sources = fs * 4
    cap = CAP
    n = sources * cap
    dh = 2 * width
    row = (sources, half * cap, dh)
    hid = (half, n, units)
    outs = [sds(row, BF), sds(hid, BF), sds(row, BF)]
    outs.append(sds((8, 128), F32) if back else sds(hid, BF))
    peers = sources - 1
    dma = pltpu.SemaphoreType.DMA
    scratch = [
        VMEM((half, dh, units), BF),
        VMEM((half, dh, units), BF),
        VMEM(hid, BF),
        VMEM(hid, BF),
        VMEM(row, BF),
    ]
    if back:
        scratch.append(VMEM((sources, 8, 128), F32))
    scratch += [dma((6,))] + [dma((peers,))] * 2 + [dma((half,))] * 2 + [dma((peers,))] * 2
    if back:
        scratch += [dma((peers,))] * 2
    anyspec = pl.BlockSpec(memory_space=ANY)
    return pl.pallas_call(
        partial(expert_body, back, fs),
        out_shape=outs,
        in_specs=[vspec()] + [anyspec] * 4 + [vspec()] * len(extra),
        out_specs=[vspec()] * len(outs),
        scratch_shapes=scratch,
        compiler_params=params(cid),
        name="experts_back" if back else "experts",
    )(s, up, upx, dn, dnx, *extra)


def per_device(tokens, mixing_weight, output_weight, first_gain, second_gain, centroids, expert_up,
               expert_down, prefix_length, assignment, validity, teacher, cotangent):
    fs, zs = lax.axis_size("fsdp"), lax.axis_size("tp")
    f, i, z = lax.axis_index("fsdp"), lax.axis_index("ctx"), lax.axis_index("tp")
    c = lax.rem(i, 2)
    n, d = tokens.shape[1], tokens.shape[2]
    rows, k = mixing_weight.shape[0], mixing_weight.shape[2]
    local_experts, width, units = expert_up.shape
    half = local_experts // 2
    experts = centroids.shape[0]
    sources = fs * 4
    heads = k // HD
    dma = pltpu.SemaphoreType.DMA
    smem = pl.BlockSpec(memory_space=pltpu.SMEM)
    anyspec = pl.BlockSpec(memory_space=ANY)
    core_pairs = [(0, 1), (1, 0), (2, 3), (3, 2)]

    def core_swap(v):
        return lax.ppermute(v, "ctx", core_pairs)

    down = expert_down.transpose(0, 2, 1)
    mixing = mixing_weight.transpose(1, 0, 2)
    tok = tokens[0]
    chosen = assignment.reshape(1, n)
    small = jnp.concatenate(
        [
            jnp.pad(jnp.concatenate([centroids, first_gain[None], second_gain[None]]), ((0, 0), (0, n - rows))),
            validity.astype(BF),
            jnp.zeros((TAB - experts - 3, n), BF),
        ]
    )
    swapped = (half, width, units)
    row_shape = (fs, 2, 2, half * CAP, d // 2)
    weight_shapes = [sds((3, d, k), BF), sds((d, k), BF), sds((TAB, d), BF), sds((sources, n), F32)]
    swap_shapes = [sds(swapped, BF)] * 2
    token_shapes = [
        sds((n, d), BF), sds((k, n), BF), sds((4, n, 2 * k), BF), sds((heads, 4, n, n), BF), sds((n, k), BF),
        sds((n, d), F32), sds((n, d), BF), sds((n, 1), F32), sds(row_shape, BF),
    ]
    summed = [VMEM((n, d), BF)] + sum_scratch(zs, n, d)
    exchange = [VMEM((n, d), BF)] + summed + [dma((2,))] * 2 + [dma((3,))] * 2
    gather = rows % 16 == 0
    if gather:
        head_in = (prefix_length, tok, mixing, output_weight, small, chosen, expert_up, down)
        out_shapes = weight_shapes + swap_shapes + token_shapes
        out_specs = [vspec()] * 4 + [anyspec] * 2 + [vspec()] * 9
        scratch = [VMEM((sources, TAB, n), BF)] + exchange + [dma((2 * fs - 1, 3))] * 2 + [dma((2 * fs, 3))] * 2
    else:
        everyone = ("fsdp", "ctx")
        w3 = lax.all_gather(mixing, everyone, axis=1, tiled=True)
        wo = lax.all_gather(output_weight, everyone, axis=1, tiled=True).T
        table = lax.all_gather(small, everyone, axis=0)
        valid_all = table[:, experts + 2, :].astype(F32)
        table = table[:, :, :rows].transpose(1, 0, 2).reshape(TAB, d)
        head_in = (prefix_length, tok, w3, wo, table, valid_all, chosen, expert_up, down)
        out_shapes = swap_shapes + token_shapes
        out_specs = [anyspec] * 2 + [vspec()] * 9
        scratch = exchange
    results = pl.pallas_call(
        partial(head_body, fs, zs, gather),
        out_shape=out_shapes,
        in_specs=[smem] + [vspec()] * (len(head_in) - 3) + [anyspec] * 2,
        out_specs=out_specs,
        scratch_shapes=scratch,
        compiler_params=params(1),
        name="head",
    )(*head_in)
    if gather:
        w3, wo, table, valid_all = results[:4]
        results = results[4:]
    up_x, dn_x, normed, qt, kv, pt, ctx, residual, mixed_in, gate, slots = results

    back_rows, act, received, gelu_slope = expert_call(False, fs, slots, expert_up, up_x, down, dn_x, (), 2)
    act_x, rec_x = core_swap(act), core_swap(received)
    activations, grad_mixed, grad_logit, stat, grad_slots = pl.pallas_call(
        partial(loss_body, zs),
        out_shape=[sds((n, d), BF), sds((n, d), F32), sds((n, 1), F32), sds((8, 128), F32), sds(row_shape, BF)],
        in_specs=[vspec()] * 7,
        out_specs=[vspec()] * 5,
        scratch_shapes=[VMEM((n, d), BF)] + summed,
        compiler_params=params(3),
        name="losses",
    )(back_rows, residual, gate, chosen, valid_all, teacher[0], cotangent[0])
    back_grads, grad_hidden, grad_received, stats = expert_call(
        True, fs, grad_slots, expert_up, up_x, down, dn_x, (gelu_slope, stat), 4
    )
    gh_x, grec_x = core_swap(grad_hidden), core_swap(grad_received)
    all_tokens = float(n * sources)
    share = stats[0, :experts] / all_tokens - 1.0 / experts
    balance = experts * experts * jnp.sum(share * stats[1, :experts] / all_tokens)
    distill = stats[2, 0]

    padded = rows + (-rows % 16) + 16
    columns = 4 * k + experts
    piece = (padded, columns)
    m = n // zs
    results = pl.pallas_call(
        partial(back_body, fs, zs, rows),
        out_shape=[sds((n, d), F32)] + [sds((m, d), BF)] * zs + [sds(piece, F32)] + [sds(piece, BF)] * (2 * fs - 1),
        in_specs=[vspec()] * 15,
        out_specs=[vspec()] * (1 + zs + 2 * fs),
        scratch_shapes=[
            VMEM((n, d), BF), VMEM((n, d), BF), VMEM((zs - 1, m, d), BF),
            VMEM((2, n, 2 * k), F32), VMEM((2, n, 2 * k), F32), VMEM((2, n, 2 * k), F32),
            VMEM((n, 2 * k), BF), VMEM((n, 2 * k), BF), VMEM((n, d), BF),
            VMEM((fs, 2, 2) + piece, F32), VMEM((fs, 2) + piece, F32),
            dma((2, zs - 1)), dma((2, zs - 1)), dma((3,)), dma((3,)),
        ],
        compiler_params=params(5),
        name="back",
    )(back_grads, residual, mixed_in, grad_mixed, grad_logit, chosen, tok, table, w3, wo, normed, qt, kv, pt, ctx)
    grad_residual, own, kept = results[0], results[1], results[1 + zs]
    z_out, g_out = results[2 : 1 + zs], results[2 + zs :]

    def z_shift(v, s):
        return lax.ppermute(v, "tp", [(a, (a + s) % zs) for a in range(zs)])

    z_in = [z_shift(v, s + 1) for s, v in enumerate(z_out)]
    g_in = []
    for df in range(fs):
        for dy in range(2):
            if df or dy:
                moves = [
                    (a * 4 + b, (a + df) % fs * 4 + (b + 2 * dy) % 4) for a in range(fs) for b in range(4)
                ]
                g_in.append(lax.ppermute(g_out[len(g_in)], ("fsdp", "ctx"), moves))
    up_gradient = expert_grads(c, received, rec_x, grad_hidden, gh_x, "up_grads")
    chunk, mix_part, out_part, cen_part, g2_part = pl.pallas_call(
        partial(reduce_body, zs, fs, rows, k, experts),
        out_shape=[
            sds((m + 16, d), BF), sds((3, rows, k), F32), sds((k, rows), F32), sds((experts, rows), F32),
            sds((1, rows), F32),
        ],
        in_specs=[vspec()] * (zs + 2 * fs),
        out_specs=[vspec()] * 5,
        compiler_params=params(),
        name="reduce",
    )(own, *z_in, kept, *g_in)
    chunks = [chunk] + [z_shift(chunk, s) for s in range(1, zs)]
    down_gradient = expert_grads(c, grad_received, grec_x, act, act_x, "down_grads")
    tokens_gradient, g1_part = pl.pallas_call(
        partial(finish_body, zs),
        out_shape=[sds((n, d), BF), sds((1, rows), F32)],
        in_specs=[smem] + [vspec()] * (3 + zs),
        out_specs=[vspec()] * 2,
        scratch_shapes=[VMEM((n, d), F32)],
        compiler_params=params(),
        name="finish",
    )(z.reshape(1), tok, table, grad_residual, *chunks)

    return (
        activations[None],
        tokens_gradient[None],
        mix_part.transpose(1, 0, 2),
        out_part,
        g1_part[0],
        g2_part[0],
        cen_part,
        up_gradient,
        down_gradient.transpose(0, 2, 1),
        balance,
        distill,
    )


def solution(mesh):
    in_specs = (
        P("fsdp", "ctx", None),
        P(("fsdp", "ctx"), None, "tp"),
        P("tp", ("fsdp", "ctx")),
        P(("fsdp", "ctx")),
        P(("fsdp", "ctx")),
        P(None, ("fsdp", "ctx")),
        P("fsdp", "ctx", "tp"),
        P("fsdp", "tp", "ctx"),
        P("fsdp"),
        P("fsdp", "ctx", None),
        P("fsdp", "ctx"),
        P("fsdp", "ctx", None),
        P("fsdp", "ctx", None),
    )
    out_specs = (
        P("fsdp", "ctx", None),
        P("fsdp", "ctx", None),
        P(("fsdp", "ctx"), None, "tp"),
        P("tp", ("fsdp", "ctx")),
        P(("fsdp", "ctx")),
        P(("fsdp", "ctx")),
        P(None, ("fsdp", "ctx")),
        P("fsdp", "ctx", "tp"),
        P("fsdp", "tp", "ctx"),
        P(),
        P(),
    )
    return jax.shard_map(
        per_device, mesh=mesh, in_specs=in_specs, out_specs=out_specs, check_vma=False
    )
```

```python
from functools import partial
import math

import jax
import jax.numpy as jnp
from jax import lax
from jax.experimental import pallas as pl
from jax.experimental.pallas import tpu as pltpu
from jax.sharding import PartitionSpec as P

HD = 64
EPSILON = 1e-05
BF = jnp.bfloat16
F32 = jnp.float32
MESH = pl.DeviceIdType.MESH
TOP = lax.Precision.HIGHEST
VMEM = pltpu.VMEM
ANY = pl.ANY
CAP = 16
EXP = 32
TAB = 48


def _dot(a, b, ca, cb, precision=None):
    return lax.dot_general(
        a, b, (((ca,), (cb,)), ((), ())), preferred_element_type=F32, precision=precision
    )


def nn(a, b):
    return _dot(a, b, 1, 0)


def nt(a, b):
    return _dot(a, b, 1, 1)


def tn(a, b):
    return _dot(a, b, 0, 0)


def vspec():
    return pl.BlockSpec(memory_space=VMEM)


def sds(shape, dtype):
    return jax.ShapeDtypeStruct(shape, dtype)


def params(cid=None, mib=56):
    if cid is None:
        return pltpu.CompilerParams(vmem_limit_bytes=mib * 2**20)
    return pltpu.CompilerParams(
        vmem_limit_bytes=mib * 2**20, collective_id=cid, has_side_effects=True
    )


def iota(shape, dim):
    return lax.broadcasted_iota(jnp.int32, shape, dim)


def to_col(row):
    n = row.shape[1]
    return jnp.sum(jnp.where(iota((n, n), 0) == iota((n, n), 1), row, 0.0), axis=1, keepdims=True)


def to_row(col):
    n = col.shape[0]
    return jnp.sum(jnp.where(iota((n, n), 0) == iota((n, n), 1), col, 0.0), axis=0, keepdims=True)


def norm_parts(x):
    c = x - jnp.mean(x, axis=-1, keepdims=True)
    inv = lax.rsqrt(jnp.mean(c * c, axis=-1, keepdims=True) + EPSILON)
    return c * inv, inv


def norm_back(grad, xhat, inv, gain):
    gx = grad * gain
    return inv * (
        gx
        - jnp.mean(gx, axis=-1, keepdims=True)
        - xhat * jnp.mean(gx * xhat, axis=-1, keepdims=True)
    )


def shifted(v, by):
    return lax.shift_right_logical(v, by)


class Route:
    def __init__(self, chosen, zs, z):
        n = chosen.shape[1]
        m = n // zs
        per = CAP // zs
        chosen = to_col(chosen.astype(F32))
        self.hot = (chosen == iota((n, EXP), 1).astype(F32)).astype(BF)
        lower = (iota((n, n), 1) < iota((n, n), 0)).astype(BF)
        rank = jnp.sum(nn(lower, self.hot) * self.hot.astype(F32), axis=1, keepdims=True)
        turn = jnp.floor(rank * (1.0 / zs))
        owner = rank - zs * turn
        owned = (owner == iota((n, zs), 1).astype(F32)).astype(BF)
        place = jnp.sum(nn(lower, owned) * owned.astype(F32), axis=1, keepdims=True)
        self.at = owner * m + place
        self.at_row = to_row(self.at)
        mine = iota((m, n), 0).astype(F32) + lax.convert_element_type(z * m, F32) == self.at_row
        self.mine = mine.astype(BF)
        self.mine_mask = mine
        self.slot = self.own_col(to_row(chosen * per + turn))
        self.own_hot = nn(self.mine, self.hot).astype(BF)
        self.slots = EXP * per
        self.n, self.m = n, m

    def own_col(self, row):
        return jnp.sum(jnp.where(self.mine_mask, row, 0.0), axis=1, keepdims=True)

    def own(self, rows):
        return nn(self.mine, rows)

    def sort(self, rows):
        return nn((iota((self.n, self.n), 0).astype(F32) == self.at_row).astype(BF), rows).astype(BF)

    def unsort(self, rows):
        return nn((iota((self.n, self.n), 1).astype(F32) == self.at).astype(BF), rows).astype(BF)

    def fill(self, rows, s_ref):
        place = (iota((self.slots, self.m), 0).astype(F32) == to_row(self.slot)).astype(BF)
        filled = nn(place, rows).astype(BF)
        fs, _, _, r, h = s_ref.shape
        for f in range(fs):
            for c in range(2):
                at = (f * 2 + c) * r
                for y in range(2):
                    s_ref[f, y, c] = filled[at : at + r, y * h : (y + 1) * h]

    def collect(self, rb_ref):
        parts = []
        for f in range(rb_ref.shape[0] // 4):
            for c in range(2):
                parts.append(jnp.concatenate([rb_ref[f * 4 + c], rb_ref[f * 4 + 2 + c]], axis=1))
        rows = jnp.concatenate(parts, axis=0)
        place = (iota((self.m, self.slots), 1).astype(F32) == self.slot).astype(BF)
        return nn(place, rows)


def z_peers(zs):
    f, i, z = lax.axis_index("fsdp"), lax.axis_index("ctx"), lax.axis_index("tp")
    return [(f, i, lax.rem(z + s, zs)) for s in range(1, zs)]


def greet(peers):
    barrier = pltpu.get_barrier_semaphore()
    for peer in peers:
        pl.semaphore_signal(barrier, inc=1, device_id=peer, device_id_type=MESH)
    pl.semaphore_wait(barrier, len(peers))


def remote(src, dst, send, recv, peer):
    return pltpu.make_async_remote_copy(
        src_ref=src, dst_ref=dst, send_sem=send, recv_sem=recv, device_id=peer, device_id_type=MESH
    )


def scatter_z(zs, x_ref, parts, send, recv):
    z = lax.axis_index("tp")
    n = x_ref.shape[0] // zs
    copies = []
    for s, peer in enumerate(z_peers(zs)):
        to = lax.rem(z + s + 1, zs)
        cp = remote(x_ref.at[span(to, n)], parts.at[s], send.at[s], recv.at[s], peer)
        cp.start()
        copies.append(cp)
    total = x_ref[span(z, n), :].astype(F32)
    for s, cp in enumerate(copies):
        cp.wait_recv()
        total = total + parts[s].astype(F32)
    return total, copies


def gather_z(zs, x_ref, n, send, recv):
    z = lax.axis_index("tp")
    copies = []
    for s, peer in enumerate(z_peers(zs)):
        cp = remote(x_ref.at[span(z, n)], x_ref.at[span(z, n)], send.at[s], recv.at[s], peer)
        cp.start()
        copies.append(cp)
    return copies


def span(at, n):
    return pl.ds(pl.multiple_of(at * n, n), n)


def group_peers(fs):
    f, i, z = lax.axis_index("fsdp"), lax.axis_index("ctx"), lax.axis_index("tp")
    y, c = lax.div(i, 2), lax.rem(i, 2)
    out = []
    for df in range(fs):
        for dy in range(2):
            for dc in range(2):
                if df or dy or dc:
                    fp = lax.rem(f + df, fs)
                    yp = y if dy == 0 else 1 - y
                    cp = c if dc == 0 else 1 - c
                    out.append((fp, yp, cp, (fp, yp * 2 + cp, z)))
    return out


def attend(mine, prefix, offsets, qt_ref, kv_ref, valid_ref, row0, pt_ref):
    k, n = qt_ref.shape
    query = iota((n, n), 1) + mine * n
    allowed = []
    for j in range(4):
        key = iota((n, n), 0) + offsets[j] * n
        col = to_col(valid_ref[pl.ds(row0 + offsets[j], 1), :])
        allowed.append(((key <= query) | (key < prefix)) & ((col > 0.5) | (key == query)))
    outs = []
    for h in range(k // HD):
        lo = h * HD
        qt = qt_ref[lo : lo + HD, :]
        scores = [
            jnp.where(allowed[j], nn(kv_ref[j, :, lo : lo + HD], qt) * (1.0 / math.sqrt(HD)), -1e30)
            for j in range(4)
        ]
        top = jnp.max(scores[0], axis=0, keepdims=True)
        for j in range(1, 4):
            top = jnp.maximum(top, jnp.max(scores[j], axis=0, keepdims=True))
        exps = [jnp.exp(s - top) for s in scores]
        share = 1.0 / sum(jnp.sum(e, axis=0, keepdims=True) for e in exps)
        acc = jnp.zeros((HD, n), F32)
        for j in range(4):
            w = (exps[j] * share).astype(BF)
            pt_ref[h, j] = w
            acc = acc + tn(kv_ref[j, :, k + lo : k + lo + HD], w)
        outs.append(acc)
    return jnp.transpose(jnp.concatenate(outs, axis=0)).astype(BF)


def attend_back(gct, qt_ref, kv_ref, pt_ref, near_ref, away_ref):
    k, n = qt_ref.shape
    scale = 1.0 / math.sqrt(HD)
    dqs = []
    for h in range(k // HD):
        lo = h * HD
        dot_ = gct[lo : lo + HD, :]
        qt = qt_ref[lo : lo + HD, :]
        ws = [pt_ref[h, j] for j in range(4)]
        dps = [nn(kv_ref[j, :, k + lo : k + lo + HD], dot_) for j in range(4)]
        mean = sum(jnp.sum(ws[j].astype(F32) * dps[j], axis=0, keepdims=True) for j in range(4))
        dq = jnp.zeros((HD, n), F32)
        for j in range(4):
            ds = (ws[j].astype(F32) * (dps[j] - mean)).astype(BF)
            dq = dq + tn(kv_ref[j, :, lo : lo + HD], ds)
            target = near_ref if j < 2 else away_ref
            target[j % 2, :, lo : lo + HD] = nt(ds, qt) * scale
            target[j % 2, :, k + lo : k + lo + HD] = nt(ws[j], dot_)
        dqs.append(dq * scale)
    return jnp.transpose(jnp.concatenate(dqs, axis=0)).astype(BF)


def expert_grads_body(c_ref, *refs):
    ins, outs = refs[:8], refs[8:]
    c = c_ref[0]
    for out_ref, at in zip(outs, (0, 4)):
        q = out_ref.shape[2]
        for core, (left_ref, right_ref) in ((c, ins[at : at + 2]), (1 - c, ins[at + 2 : at + 4])):
            for e in range(left_ref.shape[0]):
                left = jnp.where(c == 0, left_ref[e, :, :q], left_ref[e, :, q:])
                out_ref[core, e] = tn(left, right_ref[e])


def expert_grads(c, *pairs):
    half, n, dh = pairs[0].shape
    units = pairs[1].shape[2]
    step = 2 if half % 2 == 0 else 1
    block = lambda e, c_ref: (e, 0, 0)
    out = sds((2, half, dh // 2, units), F32)
    up, down = pl.pallas_call(
        expert_grads_body,
        grid_spec=pltpu.PrefetchScalarGridSpec(
            num_scalar_prefetch=1,
            grid=(half // step,),
            in_specs=[pl.BlockSpec((step, n, dh), block), pl.BlockSpec((step, n, units), block)] * 4,
            out_specs=[pl.BlockSpec((2, step, dh // 2, units), lambda e, c_ref: (0, e, 0, 0))] * 2,
        ),
        out_shape=[out, out],
        compiler_params=params(),
        name="expert_grads",
    )(c.reshape(1), *pairs)
    return up.reshape(2 * half, dh // 2, units), down.reshape(2 * half, dh // 2, units)


def whereabouts():
    f, i, z = lax.axis_index("fsdp"), lax.axis_index("ctx"), lax.axis_index("tp")
    return f, i, z, lax.div(i, 2), lax.rem(i, 2)


def head_body(fs, zs, gather, *refs):
    if gather:
        (prefix_ref, tok_ref, mix_ref, ow_ref, small_ref, as_ref, up_ref, dn_ref,
         w3_ref, wo_ref, t_ref, valid_ref, upx_ref, dnx_ref,
         normed_ref, qt_ref, kv_ref, pt_ref, ctx_ref, res_ref, mi_ref, gate_ref, s_ref,
         small_all, branch, parts, send, recv, wx_s, wx_r, kv_s, kv_r, p_s, p_r, q_s, q_r) = refs
    else:
        (prefix_ref, tok_ref, w3_ref, wo_ref, t_ref, valid_ref, as_ref, up_ref, dn_ref,
         upx_ref, dnx_ref,
         normed_ref, qt_ref, kv_ref, pt_ref, ctx_ref, res_ref, mi_ref, gate_ref, s_ref,
         branch, parts, send, recv, wx_s, wx_r, kv_s, kv_r) = refs
    f, i, z, y, c = whereabouts()
    me = f * 4 + i
    half = upx_ref.shape[0]
    k = qt_ref.shape[0]
    sibling = (f, y * 2 + 1 - c, z)
    across = (f, (1 - y) * 2 + c, z)
    same = []
    for df in range(fs):
        for dy in range(2):
            if df or dy:
                fp = lax.rem(f + df, fs)
                yp = y if dy == 0 else 1 - y
                same.append(((fp, yp * 2 + c, z), df, dy))
    greeted = same if gather else [s for s in same if s[1] == 0]
    greet([s[0] for s in greeted] + [sibling] + z_peers(zs))

    give = pl.ds((1 - c) * half, half)
    swaps = [
        remote(up_ref.at[give], upx_ref, wx_s.at[0], wx_r.at[0], sibling),
        remote(dn_ref.at[give], dnx_ref, wx_s.at[1], wx_r.at[1], sibling),
    ]
    waits = []
    xhat, _ = norm_parts(tok_ref[...].astype(F32))
    if gather:
        rows = mix_ref.shape[1]

        def places(at):
            return [w3_ref.at[:, span(at, rows), :], wo_ref.at[span(at, rows), :], small_all.at[at]]

        w3_ref[:, span(me, rows), :] = mix_ref[...]
        wo_ref[span(me, rows), :] = jnp.transpose(ow_ref[...].astype(F32)).astype(BF)
        small_all[me] = small_ref[...]
        sends, relays = [], []
        for n_, (peer, df, dy) in enumerate(same):
            for m, ref in enumerate(places(me)):
                cp = remote(ref, ref, p_s.at[n_, m], p_r.at[n_, m], peer)
                cp.start()
                sends.append(cp)
        for m, ref in enumerate(places(me)):
            cp = remote(ref, ref, q_s.at[0, m], q_r.at[0, m], sibling)
            cp.start()
            relays.append(cp)
        for n_, (peer, df, dy) in enumerate(same):
            fp = lax.rem(f - df + fs, fs)
            yp = y if dy == 0 else 1 - y
            for m, ref in enumerate(places(fp * 4 + yp * 2 + c)):
                sends[n_ * 3 + m].wait_recv()
                cp = remote(ref, ref, q_s.at[n_ + 1, m], q_r.at[n_ + 1, m], sibling)
                cp.start()
                relays.append(cp)
        for cp in relays:
            cp.wait_recv()
        sources = fs * 4
        t_ref[...] = jnp.concatenate([small_all[s, :, :rows] for s in range(sources)], axis=1)
        for s in range(sources):
            valid_ref[s : s + 1, :] = small_all[s, 34:35, :].astype(F32)
        waits += sends + relays
    for cp in swaps:
        cp.start()
    normed = (xhat * t_ref[32:33, :].astype(F32)).astype(BF)
    normed_ref[...] = normed
    kv_ref[0, :, :k] = nn(normed, w3_ref[1]).astype(BF)
    kv_ref[0, :, k:] = nn(normed, w3_ref[2]).astype(BF)
    far = remote(kv_ref.at[0], kv_ref.at[1], kv_s.at[0], kv_r.at[0], across)
    sib = remote(kv_ref.at[0], kv_ref.at[2], kv_s.at[1], kv_r.at[1], sibling)
    far.start()
    sib.start()
    qt_ref[...] = jnp.transpose(nn(normed, w3_ref[0])).astype(BF)
    far.wait_recv()
    relay = remote(kv_ref.at[1], kv_ref.at[3], kv_s.at[2], kv_r.at[2], sibling)
    relay.start()
    sib.wait_recv()
    relay.wait_recv()
    offsets = [i, (1 - y) * 2 + c, y * 2 + 1 - c, (1 - y) * 2 + 1 - c]
    ctx = attend(i, prefix_ref[0], offsets, qt_ref, kv_ref, valid_ref, f * 4, pt_ref)
    ctx_ref[...] = ctx
    route = Route(as_ref[...], zs, z)
    branch[...] = route.sort(nt(ctx, wo_ref[...]).astype(BF))
    total, sums = scatter_z(zs, branch, parts, send, recv)
    residual = route.own(tok_ref[...]) + total
    res_ref[...] = residual
    xhat, _ = norm_parts(residual)
    mixed_in = (xhat * t_ref[33:34, :].astype(F32)).astype(BF)
    mi_ref[...] = mixed_in
    logit = jnp.sum(mixed_in.astype(F32) * nn(route.own_hot, t_ref[0:EXP, :]), axis=-1, keepdims=True)
    gate_ref[...] = jax.nn.sigmoid(logit)
    route.fill(mixed_in, s_ref)
    for cp in swaps:
        cp.wait_recv()
    for cp in waits + swaps + sums + [far, sib, relay]:
        cp.wait_send()


def log2(v):
    return v.bit_length() - 1


def reorder(sources, half, per, inverse):
    n = sources * half * per
    i, o = iota((n, n), 1), iota((n, n), 0)
    if inverse:
        i, o = o, i
    ls, lh, lp = log2(sources), log2(half), log2(per)
    slot = o & (per - 1)
    source = shifted(o, lp) & (sources - 1)
    expert = shifted(o, lp + ls)
    return (i == source * (half * per) + expert * per + slot).astype(BF)


def expert_pass(back, fs, zs, s_ref, w_in, w_out, x_ref, h_ref, gp_ref, rb_ref, buffers, sems, waiting):
    rq, xg, ps, pr, res, rin, ret = buffers
    d_s, d_r, a_s, a_r, x_s, x_r, r_s, r_r, b_s, b_r, own_sem = sems
    f, i, z, y, c = whereabouts()
    me = f * 4 + i
    sources, r, dh = rq.shape
    half, n, _ = x_ref.shape
    per = r // half
    m = sources * per
    across = (f, (1 - y) * 2 + c, z)
    peers = group_peers(fs)
    zp = z_peers(zs)

    keep = pltpu.make_async_copy(s_ref.at[f, y, c], rq.at[me], own_sem.at[0])
    keep.start()
    copies = []
    for k, (fp, yp, cp_, peer) in enumerate(peers):
        cp = remote(s_ref.at[fp, yp, cp_], rq.at[me], d_s.at[k], d_r.at[k], peer)
        cp.start()
        copies.append(cp)
    for cp in waiting:
        cp.wait()
    keep.wait()
    for cp in copies:
        cp.wait_recv()
    rows = rq[...].reshape(sources * r, dh)
    xg[...] = nn(reorder(sources, half, per, False), rows).astype(BF).reshape(half, m, dh)

    def share(e, s):
        return remote(xg.at[e], x_ref.at[e, span(z, m), :], a_s.at[e, s], a_r.at[e, s], zp[s])

    def cross(e):
        return remote(ps.at[e], pr.at[e], x_s.at[e], x_r.at[e], across)

    def scatter(e, s):
        to = lax.rem(z + s + 1, zs)
        return remote(res.at[e, span(to, m), :], rin.at[e, s], r_s.at[e, s], r_r.at[e, s], zp[s])

    @pl.loop(0, half)
    def _(e):
        for s in range(zs - 1):
            share(e, s).start()
        x_ref[e, span(z, m), :] = xg[e]

    @pl.loop(0, half)
    def _(e):
        for s in range(zs - 1):
            share(e, s).wait_recv()
        ps[e] = nn(x_ref[e], w_in[e]).astype(BF)
        cross(e).start()

    @pl.loop(0, half)
    def _(e):
        cross(e).wait_recv()
        total = ps[e].astype(F32) + pr[e].astype(F32)
        if back:
            h_ref[e] = (total * gp_ref[e].astype(F32)).astype(BF)
        else:
            phi = 0.5 * (1.0 + lax.erf(total * math.sqrt(0.5)))
            h_ref[e] = (total * phi).astype(BF)
            bell = jnp.exp(-0.5 * total * total) * (1.0 / math.sqrt(2.0 * math.pi))
            gp_ref[e] = (phi + total * bell).astype(BF)
        res[e] = nt(h_ref[e], w_out[e]).astype(BF)
        for s in range(zs - 1):
            scatter(e, s).start()

    @pl.loop(0, half)
    def _(e):
        total = res[e, span(z, m), :].astype(F32)
        for s in range(zs - 1):
            scatter(e, s).wait_recv()
            total = total + rin[e, s].astype(F32)
            share(e, s).wait_send()
        xg[e] = total.astype(BF)

    rows = nn(reorder(sources, half, per, True), xg[...].reshape(half * m, dh))
    ret[...] = rows.astype(BF).reshape(sources, r, dh)
    keep = pltpu.make_async_copy(ret.at[me], rb_ref.at[me], own_sem.at[1])
    keep.start()
    for k, (fp, yp, cp_, peer) in enumerate(peers):
        cp = remote(ret.at[fp * 4 + yp * 2 + cp_], rb_ref.at[me], b_s.at[k], b_r.at[k], peer)
        cp.start()
        copies.append(cp)
    keep.wait()
    for cp in copies[len(peers) :]:
        cp.wait_recv()
    for cp in copies:
        cp.wait_send()

    @pl.loop(0, half)
    def _(e):
        cross(e).wait_send()
        for s in range(zs - 1):
            scatter(e, s).wait_send()


def pass_sems(fs, zs, half):
    dma = pltpu.SemaphoreType.DMA
    peers = 4 * fs - 1
    out = []
    for shape in ((peers,), (half, zs - 1), (half,), (half, zs - 1), (peers,)):
        out += [dma(shape)] * 2
    return out + [dma((2,))]


def middle_body(fs, zs, s_ref, res_ref, gate_ref, as_ref, valid_ref, tea_ref, cot_ref, up_ref, upx_ref, dn_ref, dnx_ref,
                x_ref, act_ref, gx_ref, gh_ref, out_ref, gm_ref, gl_ref, gb_ref, stat_ref, *refs):
    wu, wd, gp, gs, rb, rb_back, sorted_out, stat_in, stat_all = refs[:9]
    buffers = refs[9:16]
    sems = refs[16:27], refs[27:38]
    wsem, o_s, o_r, t_s, t_r, u_s, u_r = refs[38:]
    f, i, z, y, c = whereabouts()
    me = f * 4 + i
    half, width = wu.shape[0], up_ref.shape[1]
    group = group_peers(fs)
    own = pl.ds(pl.multiple_of(c * width, 64), width)
    other = pl.ds(pl.multiple_of((1 - c) * width, 64), width)
    mine = pl.ds(c * half, half)
    loads = [
        pltpu.make_async_copy(up_ref.at[mine], wu.at[:, own, :], wsem.at[0]),
        pltpu.make_async_copy(upx_ref, wu.at[:, other, :], wsem.at[1]),
        pltpu.make_async_copy(dn_ref.at[mine], wd.at[:, own, :], wsem.at[2]),
        pltpu.make_async_copy(dnx_ref, wd.at[:, other, :], wsem.at[3]),
    ]
    for cp in loads:
        cp.start()
    greet([p[3] for p in group] + z_peers(zs))
    expert_pass(False, fs, zs, s_ref, wu, wd, x_ref, act_ref, gp, rb, buffers, sems[0], loads)

    route = Route(as_ref[...], zs, z)
    returned = route.collect(rb)
    gate = gate_ref[...]
    m, d = returned.shape
    mixed = res_ref[...] + gate * returned
    diff = mixed - route.own(tea_ref[...])
    valid = route.own_col(valid_ref[pl.ds(me, 1), :])
    scale = 1.0 / (jnp.sum(valid_ref[...]) * d)
    weighted = valid * diff
    grad = route.own(cot_ref[...]) + 2.0 * weighted * scale
    route.fill((gate * grad).astype(BF), gs)
    sorted_out[span(z, m), :] = mixed.astype(BF)
    hot = route.own_hot.astype(F32)
    stat_ref[...] = jnp.zeros_like(stat_ref)
    stat_ref[0:1, 0:EXP] = jnp.sum(hot, axis=0, keepdims=True)
    stat_ref[1:2, 0:EXP] = jnp.sum(hot * gate, axis=0, keepdims=True)
    stat_ref[2:3, :] = jnp.broadcast_to(jnp.sum(weighted * diff * scale), (1, 128))
    stats = []
    for s, peer in enumerate(z_peers(zs)):
        cp = remote(stat_ref, stat_in.at[s], t_s.at[s], t_r.at[s], peer)
        cp.start()
        stats.append(cp)
    outs = gather_z(zs, sorted_out, m, o_s, o_r)
    gm_ref[...] = grad
    grad_gate = jnp.sum(grad * returned, axis=-1, keepdims=True)
    gl_ref[...] = grad_gate * gate * (1.0 - gate)
    total = stat_ref[...]
    for s, cp in enumerate(stats):
        cp.wait_recv()
        total = total + stat_in[s]
    stat_all[me] = total
    for k, (_, _, _, peer) in enumerate(group):
        cp = remote(stat_all.at[me], stat_all.at[me], u_s.at[k], u_r.at[k], peer)
        cp.start()
        stats.append(cp)

    expert_pass(True, fs, zs, gs, wd, wu, gx_ref, gh_ref, gp, rb_back, buffers, sems[1], [])
    gb_ref[...] = route.collect(rb_back)
    for cp in outs:
        cp.wait_recv()
    out_ref[...] = route.unsort(sorted_out[...])
    for cp in stats[zs - 1 :]:
        cp.wait_recv()
    for cp in outs + stats:
        cp.wait_send()
    total = stat_all[0]
    for k in range(1, fs * 4):
        total = total + stat_all[k]
    stat_ref[...] = total


def back_body(fs, zs, rows, gb_ref, res_ref, mi_ref, gm_ref, gl_ref, as_ref, tok_ref, t_ref, w3_ref, wo_ref,
              normed_ref, qt_ref, kv_ref, pt_ref, ctx_ref,
              tg_ref, mix_ref, og_ref, sm_ref,
              sorted_gb, near, away, away_in, far_out, far_in, gn, parts, sorted_tg, dense, dense_in, give, taken, sm_in,
              a_s, a_r, s_s, s_r, t_s, t_r, v_s, v_r, k_s, k_r, g_s, g_r):
    f, i, z, y, c = whereabouts()
    sibling = (f, y * 2 + 1 - c, z)
    across = (f, (1 - y) * 2 + c, z)
    same = []
    for df in range(fs):
        for dy in range(2):
            if df or dy:
                fp = lax.rem(f + df, fs)
                yp = y if dy == 0 else 1 - y
                same.append((fp, yp, (fp, yp * 2 + c, z)))
    greet(z_peers(zs) + [sibling] + [s[2] for s in same])
    route = Route(as_ref[...], zs, z)
    k = qt_ref.shape[0]
    gl = gl_ref[...]
    grad_in = gb_ref[...] + gl * nn(route.own_hot, t_ref[0:EXP, :])
    m, d = grad_in.shape
    xhat, inv = norm_parts(res_ref[...])
    grad = gm_ref[...] + norm_back(grad_in, xhat, inv, t_ref[33:34, :].astype(F32))
    sorted_gb[span(z, m), :] = grad.astype(BF)
    gathers = gather_z(zs, sorted_gb, m, a_s, a_r)
    g2 = jnp.sum(grad_in * xhat, axis=0, keepdims=True)
    cg = _dot(route.own_hot.astype(F32) * gl, mi_ref[...].astype(F32), 0, 0, TOP)
    all_tok = norm_parts(tok_ref[...].astype(F32))[0]
    own_tok, own_inv = norm_parts(route.own(tok_ref[...]))
    for cp in gathers:
        cp.wait_recv()
    gb = route.unsort(sorted_gb[...])
    gct = jnp.transpose(nn(gb, wo_ref[...])).astype(BF)
    dq = attend_back(gct, qt_ref, kv_ref, pt_ref, near, away)
    swap = remote(away, away_in, k_s.at[0], k_r.at[0], sibling)
    swap.start()
    og = tn(gb, ctx_ref[...])
    swap.wait_recv()
    far_out[...] = (near[1] + away_in[1]).astype(BF)
    cross = remote(far_out, far_in, k_s.at[1], k_r.at[1], across)
    cross.start()
    normed = normed_ref[...]
    mg = [tn(normed, dq), None, None]
    gq = nt(dq, w3_ref[0])
    cross.wait_recv()
    kvg = (near[0] + away_in[0] + far_in[...].astype(F32)).astype(BF)
    partial_normed = gq + nt(kvg[:, :k], w3_ref[1]) + nt(kvg[:, k:], w3_ref[2])
    gn[...] = route.sort(partial_normed.astype(BF))
    n = gn.shape[0]
    scat = []
    for s, peer in enumerate(z_peers(zs)):
        cp = remote(gn.at[span(lax.rem(z + s + 1, zs), m)], parts.at[s], s_s.at[s], s_r.at[s], peer)
        cp.start()
        scat.append(cp)
    mg[1] = tn(normed, kvg[:, :k])
    mg[2] = tn(normed, kvg[:, k:])
    g1 = jnp.sum(partial_normed * all_tok, axis=0, keepdims=True)
    last = dense.shape[3] - TAB
    small = jnp.concatenate([cg, g1, g2, jnp.zeros((TAB - EXP - 2, d), F32)], axis=0)
    for s in range(4 * fs):
        at = (s // 4, s % 4 // 2, s % 2)
        lo = s * rows
        for j in range(3):
            dense[at[0], at[1], at[2], 0:rows, j * k : (j + 1) * k] = mg[j][lo : lo + rows, :]
        dense[at[0], at[1], at[2], 0:rows, 3 * k : 4 * k] = og[lo : lo + rows, :]
        dense[at[0], at[1], at[2], last : last + TAB, 0:rows] = small[:, lo : lo + rows]
    pair = remote(dense.at[:, :, 1 - c], dense_in, k_s.at[2], k_r.at[2], sibling)
    pair.start()
    pair.wait_recv()
    shares = []
    for s, (fp, yp, peer) in enumerate(same):
        give[s] = (dense[fp, yp, c] + dense_in[fp, yp]).astype(BF)
        cp = remote(give.at[s], taken.at[s], g_s.at[s], g_r.at[s], peer)
        cp.start()
        shares.append(cp)
    total = gn[span(z, m), :].astype(F32)
    for s, cp in enumerate(scat):
        cp.wait_recv()
        total = total + parts[s].astype(F32)
    tg = grad + norm_back(total, own_tok, own_inv, t_ref[32:33, :].astype(F32))
    sorted_tg[span(z, m), :] = tg.astype(BF)
    ends = gather_z(zs, sorted_tg, m, t_s, t_r)
    kept = dense[f, y, c] + dense_in[f, y]
    for s, cp in enumerate(shares):
        cp.wait_recv()
        kept = kept + taken[s].astype(F32)
    sm_ref[...] = kept[last:, :128]
    smalls = []
    for s, peer in enumerate(z_peers(zs)):
        cp = remote(sm_ref, sm_in.at[s], v_s.at[s], v_r.at[s], peer)
        cp.start()
        smalls.append(cp)
    for j in range(3):
        mix_ref[j] = kept[:rows, j * k : (j + 1) * k]
    og_ref[...] = jnp.transpose(kept[:rows, 3 * k :])
    for cp in ends:
        cp.wait_recv()
    tg_ref[...] = route.unsort(sorted_tg[...])
    for cp in smalls:
        cp.wait()
    total = sm_ref[...]
    for s in range(zs - 1):
        total = total + sm_in[s]
    sm_ref[...] = total
    for cp in gathers + [swap, cross, pair] + scat + shares + ends:
        cp.wait_send()


def per_device(tokens, mixing_weight, output_weight, first_gain, second_gain, centroids, expert_up,
               expert_down, prefix_length, assignment, validity, teacher, cotangent):
    fs, zs = lax.axis_size("fsdp"), lax.axis_size("tp")
    f, i, z = lax.axis_index("fsdp"), lax.axis_index("ctx"), lax.axis_index("tp")
    c = lax.rem(i, 2)
    n, d = tokens.shape[1], tokens.shape[2]
    rows, k = mixing_weight.shape[0], mixing_weight.shape[2]
    local_experts, width, units = expert_up.shape
    half = local_experts // 2
    experts = centroids.shape[0]
    sources = fs * 4
    heads = k // HD
    dma = pltpu.SemaphoreType.DMA
    smem = pl.BlockSpec(memory_space=pltpu.SMEM)
    anyspec = pl.BlockSpec(memory_space=ANY)
    core_pairs = [(0, 1), (1, 0), (2, 3), (3, 2)]

    def core_swap(v):
        return lax.ppermute(v, "ctx", core_pairs)

    down = expert_down.transpose(0, 2, 1)
    mixing = mixing_weight.transpose(1, 0, 2)
    tok = tokens[0]
    chosen = assignment.reshape(1, n)
    small = jnp.concatenate(
        [
            jnp.pad(jnp.concatenate([centroids, first_gain[None], second_gain[None]]), ((0, 0), (0, n - rows))),
            validity.astype(BF),
            jnp.zeros((TAB - experts - 3, n), BF),
        ]
    )
    swapped = (half, width, units)
    per = CAP // zs
    m = n // zs
    r = half * per
    row_shape = (fs, 2, 2, r, d // 2)
    weight_shapes = [sds((3, d, k), BF), sds((d, k), BF), sds((TAB, d), BF), sds((sources, n), F32)]
    swap_shapes = [sds(swapped, BF)] * 2
    token_shapes = [
        sds((n, d), BF), sds((k, n), BF), sds((4, n, 2 * k), BF), sds((heads, 4, n, n), BF), sds((n, k), BF),
        sds((m, d), F32), sds((m, d), BF), sds((m, 1), F32), sds(row_shape, BF),
    ]
    scattered = [VMEM((n, d), BF), VMEM((zs - 1, m, d), BF)]
    exchange = scattered + [dma((zs - 1,))] * 2 + [dma((2,))] * 2 + [dma((3,))] * 2
    gather = rows % 16 == 0
    if gather:
        head_in = (prefix_length, tok, mixing, output_weight, small, chosen, expert_up, down)
        out_shapes = weight_shapes + swap_shapes + token_shapes
        out_specs = [vspec()] * 4 + [anyspec] * 2 + [vspec()] * 9
        scratch = [VMEM((sources, TAB, n), BF)] + exchange + [dma((2 * fs - 1, 3))] * 2 + [dma((2 * fs, 3))] * 2
    else:
        everyone = ("fsdp", "ctx")
        w3 = lax.all_gather(mixing, everyone, axis=1, tiled=True)
        wo = lax.all_gather(output_weight, everyone, axis=1, tiled=True).T
        table = lax.all_gather(small, everyone, axis=0)
        valid_all = table[:, experts + 2, :].astype(F32)
        table = table[:, :, :rows].transpose(1, 0, 2).reshape(TAB, d)
        head_in = (prefix_length, tok, w3, wo, table, valid_all, chosen, expert_up, down)
        out_shapes = swap_shapes + token_shapes
        out_specs = [anyspec] * 2 + [vspec()] * 9
        scratch = exchange
    results = pl.pallas_call(
        partial(head_body, fs, zs, gather),
        out_shape=out_shapes,
        in_specs=[smem] + [vspec()] * (len(head_in) - 3) + [anyspec] * 2,
        out_specs=out_specs,
        scratch_shapes=scratch,
        compiler_params=params(1),
        name="head",
    )(*head_in)
    if gather:
        w3, wo, table, valid_all = results[:4]
        results = results[4:]
    up_x, dn_x, normed, qt, kv, pt, ctx, residual, mixed_in, gate, slots = results

    slots_in = sources * CAP
    dh = d // 2
    hidden = (half, slots_in, units)
    received = (half, slots_in, dh)
    x, act, gx, gh, activations, grad_mixed, grad_logit, grad_back, stats = pl.pallas_call(
        partial(middle_body, fs, zs),
        out_shape=[
            sds(received, BF), sds(hidden, BF), sds(received, BF), sds(hidden, BF), sds((n, d), BF),
            sds((m, d), F32), sds((m, 1), F32), sds((m, d), F32), sds((8, 128), F32),
        ],
        in_specs=[vspec()] * 7 + [anyspec] * 4,
        out_specs=[vspec()] * 9,
        scratch_shapes=[
            VMEM((half, dh, units), BF), VMEM((half, dh, units), BF), VMEM(hidden, BF), VMEM(row_shape, BF),
            VMEM((sources, r, dh), BF), VMEM((sources, r, dh), BF), VMEM((n, d), BF),
            VMEM((zs - 1, 8, 128), F32), VMEM((sources, 8, 128), F32),
            VMEM((sources, r, dh), BF), VMEM((half, sources * per, dh), BF), VMEM(hidden, BF), VMEM(hidden, BF),
            VMEM(received, BF), VMEM((half, zs - 1, sources * per, dh), BF), VMEM((sources, r, dh), BF),
        ]
        + pass_sems(fs, zs, half) * 2
        + [dma((4,))] + [dma((zs - 1,))] * 4 + [dma((sources - 1,))] * 2,
        compiler_params=params(2),
        name="middle",
    )(slots, residual, gate, chosen, valid_all, teacher[0], cotangent[0], expert_up, up_x, down, dn_x)
    x_x, act_x, gx_x, gh_x = core_swap(x), core_swap(act), core_swap(gx), core_swap(gh)
    all_tokens = float(n * sources)
    share = stats[0, :experts] / all_tokens - 1.0 / experts
    balance = experts * experts * jnp.sum(share * stats[1, :experts] / all_tokens)
    distill = stats[2, 0]

    piece = (rows + (-rows % 16) + TAB, 4 * k)
    others = 2 * fs - 1
    tokens_gradient, mix_part, out_part, small_part = pl.pallas_call(
        partial(back_body, fs, zs, rows),
        out_shape=[sds((n, d), BF), sds((3, rows, k), F32), sds((k, rows), F32), sds((TAB, 128), F32)],
        in_specs=[vspec()] * 15,
        out_specs=[vspec()] * 4,
        scratch_shapes=[
            VMEM((n, d), BF), VMEM((2, n, 2 * k), F32), VMEM((2, n, 2 * k), F32), VMEM((2, n, 2 * k), F32),
            VMEM((n, 2 * k), BF), VMEM((n, 2 * k), BF), VMEM((n, d), BF), VMEM((zs - 1, m, d), BF), VMEM((n, d), BF),
            VMEM((fs, 2, 2) + piece, F32), VMEM((fs, 2) + piece, F32),
            VMEM((others,) + piece, BF), VMEM((others,) + piece, BF), VMEM((zs - 1, TAB, 128), F32),
        ]
        + [dma((zs - 1,))] * 8 + [dma((3,))] * 2 + [dma((others,))] * 2,
        compiler_params=params(3),
        name="back",
    )(grad_back, residual, mixed_in, grad_mixed, grad_logit, chosen, tok, table, w3, wo, normed, qt, kv, pt, ctx)
    up_gradient, down_gradient = expert_grads(c, x, gh, x_x, gh_x, gx, act, gx_x, act_x)

    return (
        activations[None],
        tokens_gradient[None],
        mix_part.transpose(1, 0, 2),
        out_part,
        small_part[experts, :rows],
        small_part[experts + 1, :rows],
        small_part[:experts, :rows],
        up_gradient,
        down_gradient.transpose(0, 2, 1),
        balance,
        distill,
    )


def solution(mesh):
    in_specs = (
        P("fsdp", "ctx", None),
        P(("fsdp", "ctx"), None, "tp"),
        P("tp", ("fsdp", "ctx")),
        P(("fsdp", "ctx")),
        P(("fsdp", "ctx")),
        P(None, ("fsdp", "ctx")),
        P("fsdp", "ctx", "tp"),
        P("fsdp", "tp", "ctx"),
        P("fsdp"),
        P("fsdp", "ctx", None),
        P("fsdp", "ctx"),
        P("fsdp", "ctx", None),
        P("fsdp", "ctx", None),
    )
    out_specs = (
        P("fsdp", "ctx", None),
        P("fsdp", "ctx", None),
        P(("fsdp", "ctx"), None, "tp"),
        P("tp", ("fsdp", "ctx")),
        P(("fsdp", "ctx")),
        P(("fsdp", "ctx")),
        P(None, ("fsdp", "ctx")),
        P("fsdp", "ctx", "tp"),
        P("fsdp", "tp", "ctx"),
        P(),
        P(),
    )
    return jax.shard_map(
        per_device, mesh=mesh, in_specs=in_specs, out_specs=out_specs, check_vma=False
    )
```

```python
from functools import partial
import math

import jax
import jax.numpy as jnp
from jax import lax
from jax.experimental import pallas as pl
from jax.experimental.pallas import tpu as pltpu
from jax.sharding import PartitionSpec as P

HD = 64
EPSILON = 1e-05
BF = jnp.bfloat16
F32 = jnp.float32
MESH = pl.DeviceIdType.MESH
TOP = lax.Precision.HIGHEST
VMEM = pltpu.VMEM
ANY = pl.ANY
CAP = 16
EXP = 32
TAB = 48


def _dot(a, b, ca, cb, precision=None):
    return lax.dot_general(
        a, b, (((ca,), (cb,)), ((), ())), preferred_element_type=F32, precision=precision
    )


def nn(a, b):
    return _dot(a, b, 1, 0)


def nt(a, b):
    return _dot(a, b, 1, 1)


def tn(a, b):
    return _dot(a, b, 0, 0)


def vspec():
    return pl.BlockSpec(memory_space=VMEM)


def sds(shape, dtype):
    return jax.ShapeDtypeStruct(shape, dtype)


def params(cid=None, mib=56):
    if cid is None:
        return pltpu.CompilerParams(vmem_limit_bytes=mib * 2**20)
    return pltpu.CompilerParams(
        vmem_limit_bytes=mib * 2**20, collective_id=cid, has_side_effects=True
    )


def iota(shape, dim):
    return lax.broadcasted_iota(jnp.int32, shape, dim)


def to_col(row):
    n = row.shape[1]
    return jnp.sum(jnp.where(iota((n, n), 0) == iota((n, n), 1), row, 0.0), axis=1, keepdims=True)


def to_row(col):
    n = col.shape[0]
    return jnp.sum(jnp.where(iota((n, n), 0) == iota((n, n), 1), col, 0.0), axis=0, keepdims=True)


def norm_parts(x):
    c = x - jnp.mean(x, axis=-1, keepdims=True)
    inv = lax.rsqrt(jnp.mean(c * c, axis=-1, keepdims=True) + EPSILON)
    return c * inv, inv


def norm_back(grad, xhat, inv, gain):
    gx = grad * gain
    return inv * (
        gx
        - jnp.mean(gx, axis=-1, keepdims=True)
        - xhat * jnp.mean(gx * xhat, axis=-1, keepdims=True)
    )


def log2(v):
    return v.bit_length() - 1


def shifted(v, by):
    return lax.shift_right_logical(v, by)


class Route:
    def __init__(self, chosen, zs, z, width=0):
        n = chosen.shape[1]
        m = n // zs
        per = CAP // zs
        chosen = to_col(chosen.astype(F32))
        self.hot = (chosen == iota((n, EXP), 1).astype(F32)).astype(BF)
        lower = (iota((n, n), 1) < iota((n, n), 0)).astype(BF)
        rank = jnp.sum(nn(lower, self.hot) * self.hot.astype(F32), axis=1, keepdims=True)
        turn = jnp.floor(rank * (1.0 / zs))
        owner = rank - zs * turn
        owned = (owner == iota((n, zs), 1).astype(F32)).astype(BF)
        place = jnp.sum(nn(lower, owned) * owned.astype(F32), axis=1, keepdims=True)
        self.at = owner * m + place
        self.at_row = to_row(self.at)
        mine = iota((m, n), 0).astype(F32) + lax.convert_element_type(z * m, F32) == self.at_row
        self.mine = mine.astype(BF)
        self.mine_mask = mine
        self.slot = self.own_col(to_row(chosen * per + turn))
        self.own_hot = nn(self.mine, self.hot).astype(BF)
        self.slots = EXP * per
        self.n, self.m, self.width = n, m, width

    def own_col(self, row):
        return jnp.sum(jnp.where(self.mine_mask, row, 0.0), axis=1, keepdims=True)

    def own(self, rows):
        return nn(self.mine, rows)

    def sort(self, rows):
        return nn((iota((self.n, self.n), 0).astype(F32) == self.at_row).astype(BF), rows).astype(BF)

    def unsort(self, rows):
        return nn((iota((self.n, self.n), 1).astype(F32) == self.at).astype(BF), rows).astype(BF)

    def fill(self, rows, s_ref):
        place = (iota((self.slots, self.m), 0).astype(F32) == to_row(self.slot)).astype(BF)
        filled = nn(place, rows).astype(BF)
        fs, _, _, r, _ = s_ref.shape
        h = self.width // 2
        for f in range(fs):
            for c in range(2):
                at = (f * 2 + c) * r
                for y in range(2):
                    s_ref[f, y, c, :, :h] = filled[at : at + r, y * h : (y + 1) * h]
                    if rows.shape[1] > self.width:
                        s_ref[f, y, c, :, h:] = filled[at : at + r, self.width :]

    def collect(self, rb_ref):
        parts = []
        for f in range(rb_ref.shape[0] // 4):
            for c in range(2):
                parts.append(jnp.concatenate([rb_ref[f * 4 + c], rb_ref[f * 4 + 2 + c]], axis=1))
        rows = jnp.concatenate(parts, axis=0)
        place = (iota((self.m, self.slots), 1).astype(F32) == self.slot).astype(BF)
        return nn(place, rows)


def z_peers(zs):
    f, i, z = lax.axis_index("fsdp"), lax.axis_index("ctx"), lax.axis_index("tp")
    return [(f, i, lax.rem(z + s, zs)) for s in range(1, zs)]


def greet(peers):
    barrier = pltpu.get_barrier_semaphore()
    for peer in peers:
        pl.semaphore_signal(barrier, inc=1, device_id=peer, device_id_type=MESH)
    pl.semaphore_wait(barrier, len(peers))


def remote(src, dst, send, recv, peer):
    return pltpu.make_async_remote_copy(
        src_ref=src, dst_ref=dst, send_sem=send, recv_sem=recv, device_id=peer, device_id_type=MESH
    )


def scatter_z(zs, x_ref, parts, send, recv):
    z = lax.axis_index("tp")
    n = x_ref.shape[0] // zs
    copies = []
    for s, peer in enumerate(z_peers(zs)):
        to = lax.rem(z + s + 1, zs)
        cp = remote(x_ref.at[span(to, n)], parts.at[s], send.at[s], recv.at[s], peer)
        cp.start()
        copies.append(cp)
    total = x_ref[span(z, n), :].astype(F32)
    for s, cp in enumerate(copies):
        cp.wait_recv()
        total = total + parts[s].astype(F32)
    return total, copies


def gather_z(zs, x_ref, n, send, recv):
    z = lax.axis_index("tp")
    copies = []
    for s, peer in enumerate(z_peers(zs)):
        cp = remote(x_ref.at[span(z, n)], x_ref.at[span(z, n)], send.at[s], recv.at[s], peer)
        cp.start()
        copies.append(cp)
    return copies


def span(at, n):
    return pl.ds(pl.multiple_of(at * n, n), n)


def group_peers(fs):
    f, i, z = lax.axis_index("fsdp"), lax.axis_index("ctx"), lax.axis_index("tp")
    y, c = lax.div(i, 2), lax.rem(i, 2)
    out = []
    for df in range(fs):
        for dy in range(2):
            for dc in range(2):
                if df or dy or dc:
                    fp = lax.rem(f + df, fs)
                    yp = y if dy == 0 else 1 - y
                    cp = c if dc == 0 else 1 - c
                    out.append((fp, yp, cp, (fp, yp * 2 + cp, z)))
    return out


def attend(mine, prefix, offsets, qt_ref, kv_ref, valid_ref, row0, pt_ref):
    k, n = qt_ref.shape
    query = iota((n, n), 1) + mine * n
    allowed = []
    for j in range(4):
        key = iota((n, n), 0) + offsets[j] * n
        col = to_col(valid_ref[pl.ds(row0 + offsets[j], 1), :])
        allowed.append(((key <= query) | (key < prefix)) & ((col > 0.5) | (key == query)))
    outs = []
    for h in range(k // HD):
        lo = h * HD
        qt = qt_ref[lo : lo + HD, :]
        scores = [
            jnp.where(allowed[j], nn(kv_ref[j, :, lo : lo + HD], qt) * (1.0 / math.sqrt(HD)), -1e30)
            for j in range(4)
        ]
        top = jnp.max(scores[0], axis=0, keepdims=True)
        for j in range(1, 4):
            top = jnp.maximum(top, jnp.max(scores[j], axis=0, keepdims=True))
        exps = [jnp.exp(s - top) for s in scores]
        share = 1.0 / sum(jnp.sum(e, axis=0, keepdims=True) for e in exps)
        acc = jnp.zeros((HD, n), F32)
        for j in range(4):
            w = (exps[j] * share).astype(BF)
            pt_ref[h, j] = w
            acc = acc + tn(kv_ref[j, :, k + lo : k + lo + HD], w)
        outs.append(acc)
    return jnp.transpose(jnp.concatenate(outs, axis=0)).astype(BF)


def attend_back(gct, qt_ref, kv_ref, pt_ref, near_ref, away_ref):
    k, n = qt_ref.shape
    scale = 1.0 / math.sqrt(HD)
    dqs = []
    for h in range(k // HD):
        lo = h * HD
        dot_ = gct[lo : lo + HD, :]
        qt = qt_ref[lo : lo + HD, :]
        ws = [pt_ref[h, j] for j in range(4)]
        dps = [nn(kv_ref[j, :, k + lo : k + lo + HD], dot_) for j in range(4)]
        mean = sum(jnp.sum(ws[j].astype(F32) * dps[j], axis=0, keepdims=True) for j in range(4))
        dq = jnp.zeros((HD, n), F32)
        for j in range(4):
            ds = (ws[j].astype(F32) * (dps[j] - mean)).astype(BF)
            dq = dq + tn(kv_ref[j, :, lo : lo + HD], ds)
            target = near_ref if j < 2 else away_ref
            target[j % 2, :, lo : lo + HD] = nt(ds, qt) * scale
            target[j % 2, :, k + lo : k + lo + HD] = nt(ws[j], dot_)
        dqs.append(dq * scale)
    return jnp.transpose(jnp.concatenate(dqs, axis=0)).astype(BF)


def expert_grads_body(c_ref, *refs):
    ins, outs = refs[:8], refs[8:]
    c = c_ref[0]
    for out_ref, at in zip(outs, (0, 4)):
        q = out_ref.shape[2]
        for core, (left_ref, right_ref) in ((c, ins[at : at + 2]), (1 - c, ins[at + 2 : at + 4])):
            for e in range(left_ref.shape[0]):
                left = jnp.where(c == 0, left_ref[e, :, :q], left_ref[e, :, q:])
                out_ref[core, e] = tn(left, right_ref[e])


def expert_grads(c, *pairs):
    half, n, dh = pairs[0].shape
    units = pairs[1].shape[2]
    step = 2 if half % 2 == 0 else 1
    block = lambda e, c_ref: (e, 0, 0)
    out = sds((2, half, dh // 2, units), F32)
    up, down = pl.pallas_call(
        expert_grads_body,
        grid_spec=pltpu.PrefetchScalarGridSpec(
            num_scalar_prefetch=1,
            grid=(half // step,),
            in_specs=[pl.BlockSpec((step, n, dh), block), pl.BlockSpec((step, n, units), block)] * 4,
            out_specs=[pl.BlockSpec((2, step, dh // 2, units), lambda e, c_ref: (0, e, 0, 0))] * 2,
        ),
        out_shape=[out, out],
        compiler_params=params(),
        name="expert_grads",
    )(c.reshape(1), *pairs)
    return up.reshape(2 * half, dh // 2, units), down.reshape(2 * half, dh // 2, units)


def whereabouts():
    f, i, z = lax.axis_index("fsdp"), lax.axis_index("ctx"), lax.axis_index("tp")
    return f, i, z, lax.div(i, 2), lax.rem(i, 2)


def head_body(fs, zs, gather, *refs):
    if gather:
        (prefix_ref, tok_ref, mix_ref, ow_ref, small_ref, as_ref, tea_ref, cot_ref, up_ref, dn_ref,
         w3_ref, wo_ref, t_ref, valid_ref, upx_ref, dnx_ref,
         normed_ref, qt_ref, kv_ref, pt_ref, ctx_ref, res_ref, mi_ref, gate_ref, s_ref, sg_ref,
         small_all, branch, parts, send, recv, wx_s, wx_r, kv_s, kv_r, p_s, p_r, q_s, q_r) = refs
    else:
        (prefix_ref, tok_ref, w3_ref, wo_ref, t_ref, valid_ref, as_ref, tea_ref, cot_ref, up_ref, dn_ref,
         upx_ref, dnx_ref,
         normed_ref, qt_ref, kv_ref, pt_ref, ctx_ref, res_ref, mi_ref, gate_ref, s_ref, sg_ref,
         branch, parts, send, recv, wx_s, wx_r, kv_s, kv_r) = refs
    f, i, z, y, c = whereabouts()
    me = f * 4 + i
    half = upx_ref.shape[0]
    k = qt_ref.shape[0]
    sibling = (f, y * 2 + 1 - c, z)
    across = (f, (1 - y) * 2 + c, z)
    same = []
    for df in range(fs):
        for dy in range(2):
            if df or dy:
                fp = lax.rem(f + df, fs)
                yp = y if dy == 0 else 1 - y
                same.append(((fp, yp * 2 + c, z), df, dy))
    greeted = same if gather else [s for s in same if s[1] == 0]
    greet([s[0] for s in greeted] + [sibling] + z_peers(zs))

    give = pl.ds((1 - c) * half, half)
    swaps = [
        remote(up_ref.at[give], upx_ref, wx_s.at[0], wx_r.at[0], sibling),
        remote(dn_ref.at[give], dnx_ref, wx_s.at[1], wx_r.at[1], sibling),
    ]
    waits = []
    xhat, _ = norm_parts(tok_ref[...].astype(F32))
    if gather:
        rows = mix_ref.shape[1]

        def places(at):
            return [w3_ref.at[:, span(at, rows), :], wo_ref.at[span(at, rows), :], small_all.at[at]]

        w3_ref[:, span(me, rows), :] = mix_ref[...]
        wo_ref[span(me, rows), :] = jnp.transpose(ow_ref[...].astype(F32)).astype(BF)
        small_all[me] = small_ref[...]
        sends, relays = [], []
        for n_, (peer, df, dy) in enumerate(same):
            for m, ref in enumerate(places(me)):
                cp = remote(ref, ref, p_s.at[n_, m], p_r.at[n_, m], peer)
                cp.start()
                sends.append(cp)
        for m, ref in enumerate(places(me)):
            cp = remote(ref, ref, q_s.at[0, m], q_r.at[0, m], sibling)
            cp.start()
            relays.append(cp)
        for n_, (peer, df, dy) in enumerate(same):
            fp = lax.rem(f - df + fs, fs)
            yp = y if dy == 0 else 1 - y
            for m, ref in enumerate(places(fp * 4 + yp * 2 + c)):
                sends[n_ * 3 + m].wait_recv()
                cp = remote(ref, ref, q_s.at[n_ + 1, m], q_r.at[n_ + 1, m], sibling)
                cp.start()
                relays.append(cp)
        for cp in relays:
            cp.wait_recv()
        sources = fs * 4
        t_ref[...] = jnp.concatenate([small_all[s, :, :rows] for s in range(sources)], axis=1)
        for s in range(sources):
            valid_ref[s : s + 1, :] = small_all[s, 34:35, :].astype(F32)
        waits += sends + relays
    for cp in swaps:
        cp.start()
    normed = (xhat * t_ref[32:33, :].astype(F32)).astype(BF)
    normed_ref[...] = normed
    kv_ref[0, :, :k] = nn(normed, w3_ref[1]).astype(BF)
    kv_ref[0, :, k:] = nn(normed, w3_ref[2]).astype(BF)
    far = remote(kv_ref.at[0], kv_ref.at[1], kv_s.at[0], kv_r.at[0], across)
    sib = remote(kv_ref.at[0], kv_ref.at[2], kv_s.at[1], kv_r.at[1], sibling)
    far.start()
    sib.start()
    qt_ref[...] = jnp.transpose(nn(normed, w3_ref[0])).astype(BF)
    far.wait_recv()
    relay = remote(kv_ref.at[1], kv_ref.at[3], kv_s.at[2], kv_r.at[2], sibling)
    relay.start()
    sib.wait_recv()
    relay.wait_recv()
    offsets = [i, (1 - y) * 2 + c, y * 2 + 1 - c, (1 - y) * 2 + 1 - c]
    ctx = attend(i, prefix_ref[0], offsets, qt_ref, kv_ref, valid_ref, f * 4, pt_ref)
    ctx_ref[...] = ctx
    d = tok_ref.shape[1]
    route = Route(as_ref[...], zs, z, d)
    branch[...] = route.sort(nt(ctx, wo_ref[...]).astype(BF))
    teacher, cotangent = route.own(tea_ref[...]), route.own(cot_ref[...])
    valid = route.own_col(valid_ref[pl.ds(me, 1), :])
    weight = 2.0 * valid / (jnp.sum(valid_ref[...]) * d)
    total, sums = scatter_z(zs, branch, parts, send, recv)
    residual = route.own(tok_ref[...]) + total
    res_ref[...] = residual
    xhat, _ = norm_parts(residual)
    mixed_in = (xhat * t_ref[33:34, :].astype(F32)).astype(BF)
    mi_ref[...] = mixed_in
    logit = jnp.sum(mixed_in.astype(F32) * nn(route.own_hot, t_ref[0:EXP, :]), axis=-1, keepdims=True)
    gate = jax.nn.sigmoid(logit)
    gate_ref[...] = gate
    route.fill(mixed_in, s_ref)
    known = gate * (cotangent + weight * (residual - teacher))
    slope = jnp.broadcast_to(gate * gate * weight, (known.shape[0], 128))
    route.fill(jnp.concatenate([known, slope], axis=1).astype(BF), sg_ref)
    for cp in swaps:
        cp.wait_recv()
    for cp in waits + swaps + sums + [far, sib, relay]:
        cp.wait_send()


def reorder(sources, half, per, inverse):
    n = sources * half * per
    i, o = iota((n, n), 1), iota((n, n), 0)
    if inverse:
        i, o = o, i
    ls, lh, lp = log2(sources), log2(half), log2(per)
    slot = o & (per - 1)
    source = shifted(o, lp) & (sources - 1)
    expert = shifted(o, lp + ls)
    return (i == source * (half * per) + expert * per + slot).astype(BF)


class Pass:
    def __init__(self, back, zs, w_in, w_out, xg, x_ref, ps, pr, h_ref, gp_ref, res, rin, sems):
        self.back, self.zs, self.w_in, self.w_out = back, zs, w_in, w_out
        self.xg, self.x_ref, self.ps, self.pr = xg, x_ref, ps, pr
        self.h_ref, self.gp_ref, self.res, self.rin = h_ref, gp_ref, res, rin
        self.a_s, self.a_r, self.x_s, self.x_r, self.r_s, self.r_r = sems
        f, i, z, y, c = whereabouts()
        self.z = z
        self.m = xg.shape[1]
        self.across = (f, (1 - y) * 2 + c, z)
        self.peers = z_peers(zs)

    def share(self, e, s):
        to = self.x_ref.at[e, span(self.z, self.m), :]
        return remote(self.xg.at[e], to, self.a_s.at[e, s], self.a_r.at[e, s], self.peers[s])

    def cross(self, e):
        return remote(self.ps.at[e], self.pr.at[e], self.x_s.at[e], self.x_r.at[e], self.across)

    def scatter(self, e, s):
        to = lax.rem(self.z + s + 1, self.zs)
        return remote(
            self.res.at[e, span(to, self.m), :], self.rin.at[e, s], self.r_s.at[e, s], self.r_r.at[e, s], self.peers[s]
        )

    def spread(self, e, rows):
        self.xg[e] = rows
        for s in range(self.zs - 1):
            self.share(e, s).start()
        self.x_ref[e, span(self.z, self.m), :] = rows

    def first(self, e):
        for s in range(self.zs - 1):
            self.share(e, s).wait_recv()
        self.ps[e] = nn(self.x_ref[e], self.w_in[e]).astype(BF)

    def second(self, e):
        self.cross(e).wait_recv()
        total = self.ps[e].astype(F32) + self.pr[e].astype(F32)
        if self.back:
            self.h_ref[e] = (total * self.gp_ref[e].astype(F32)).astype(BF)
        else:
            phi = 0.5 * (1.0 + lax.erf(total * math.sqrt(0.5)))
            self.h_ref[e] = (total * phi).astype(BF)
            bell = jnp.exp(-0.5 * total * total) * (1.0 / math.sqrt(2.0 * math.pi))
            self.gp_ref[e] = (phi + total * bell).astype(BF)
        self.res[e] = nt(self.h_ref[e], self.w_out[e]).astype(BF)
        for s in range(self.zs - 1):
            self.scatter(e, s).start()

    def total(self, e):
        total = self.res[e, span(self.z, self.m), :].astype(F32)
        for s in range(self.zs - 1):
            self.scatter(e, s).wait_recv()
            total = total + self.rin[e, s].astype(F32)
        return total.astype(BF)

    def settle(self, e):
        self.cross(e).wait_send()
        for s in range(self.zs - 1):
            self.share(e, s).wait_send()
            self.scatter(e, s).wait_send()


def give_back(fs, total, ret, rb_ref, own_sem, send, recv):
    f, i, z, y, c = whereabouts()
    me = f * 4 + i
    sources, r, dh = ret.shape
    half = total.shape[0]
    rows = total[...].reshape(sources * r, dh)
    ret[...] = nn(reorder(sources, half, r // half, True), rows).astype(BF).reshape(sources, r, dh)
    keep = pltpu.make_async_copy(ret.at[me], rb_ref.at[me], own_sem)
    keep.start()
    copies = []
    for k, (fp, yp, cp_, peer) in enumerate(group_peers(fs)):
        cp = remote(ret.at[fp * 4 + yp * 2 + cp_], rb_ref.at[me], send.at[k], recv.at[k], peer)
        cp.start()
        copies.append(cp)
    return keep, copies


def arrived(given):
    keep, copies = given
    keep.wait()
    for cp in copies:
        cp.wait_recv()


def pass_sems(zs, half):
    dma = pltpu.SemaphoreType.DMA
    return [dma((half, zs - 1))] * 2 + [dma((half,))] * 2 + [dma((half, zs - 1))] * 2


def middle_body(fs, zs, s_ref, sg_ref, res_ref, gate_ref, as_ref, valid_ref, tea_ref, cot_ref,
                up_ref, upx_ref, dn_ref, dnx_ref,
                x_ref, act_ref, gx_ref, gh_ref, out_ref, gm_ref, gl_ref, gb_ref, stat_ref, *refs):
    (wu, wd, gp, rq, rg, grads, results, ret, ret_back, rb, rb_back, sorted_out, stat_in, stat_all,
     xg, xg_back, ps, pr, pr_back, res, rin) = refs[:21]
    sems = refs[21:27], refs[27:33]
    wsem, d_s, d_r, g_s, g_r, b_s, b_r, c_s, c_r, o_s, o_r, t_s, t_r, u_s, u_r = refs[33:]
    f, i, z, y, c = whereabouts()
    me = f * 4 + i
    half, width = wu.shape[0], up_ref.shape[1]
    sources, r, dh = rq.shape
    m = sources * r // half
    group = group_peers(fs)
    own = pl.ds(pl.multiple_of(c * width, 64), width)
    other = pl.ds(pl.multiple_of((1 - c) * width, 64), width)
    mine = pl.ds(c * half, half)
    loads = [
        pltpu.make_async_copy(s_ref.at[f, y, c], rq.at[me], wsem.at[0]),
        pltpu.make_async_copy(sg_ref.at[f, y, c], rg.at[me], wsem.at[1]),
        pltpu.make_async_copy(up_ref.at[mine], wu.at[:, own, :], wsem.at[2]),
        pltpu.make_async_copy(upx_ref, wu.at[:, other, :], wsem.at[3]),
        pltpu.make_async_copy(dn_ref.at[mine], wd.at[:, own, :], wsem.at[4]),
        pltpu.make_async_copy(dnx_ref, wd.at[:, other, :], wsem.at[5]),
    ]
    for cp in loads:
        cp.start()
    greet([p[3] for p in group] + z_peers(zs))
    sends, sends_g = [], []
    for out, src, dst, send, recv in ((sends, s_ref, rq, d_s, d_r), (sends_g, sg_ref, rg, g_s, g_r)):
        for k, (fp, yp, cp_, peer) in enumerate(group):
            cp = remote(src.at[fp, yp, cp_], dst.at[me], send.at[k], recv.at[k], peer)
            cp.start()
            out.append(cp)
    one = Pass(False, zs, wu, wd, xg, x_ref, ps, pr, act_ref, gp, res, rin, sems[0])
    two = Pass(True, zs, wd, wu, xg_back, gx_ref, ps, pr_back, gh_ref, gp, res, rin, sems[1])
    order = reorder(sources, half, r // half, False)

    loads[0].wait()
    for cp in sends:
        cp.wait_recv()
    rows = nn(order, rq[...].reshape(sources * r, dh)).astype(BF).reshape(half, m, dh)
    for e in range(half):
        one.spread(e, rows[e])
    for cp in loads[2:]:
        cp.wait()

    @pl.loop(0, half)
    def _(e):
        one.first(e)
        one.cross(e).start()

    loads[1].wait()
    for cp in sends_g:
        cp.wait_recv()
    grads[...] = nn(order, rg[...].reshape(sources * r, dh + 128)).astype(BF).reshape(half, m, dh + 128)

    def turn(e):
        result = one.total(e)
        results[e] = result
        scale = grads[e, :, dh:].astype(F32)[:, :1]
        two.spread(e, (grads[e, :, :dh].astype(F32) + scale * result.astype(F32)).astype(BF))

    lag, lag2 = 2, 4
    start = max(half, lag2 + 1)
    ahead = 3

    def step(t, fixed=True):
        if not fixed or t < half:
            one.second(t)
        if fixed and t - start >= 0 and t - start < half:
            two.second(t - start)
        if not fixed or 0 <= t - lag < half:
            turn(t - lag)
        if not fixed or 0 <= t - lag2 < half:
            one.settle(t - lag2)
            two.first(t - lag2)

    begun = 0
    t = 0
    while t < lag2:
        step(t)
        t += 1
    safe = max(t, start - ahead)
    if safe > t and half > t:
        stop = min(safe, half)

        @pl.loop(t, stop)
        def _(k):
            step(k, False)

        t = stop
    given = None
    pending = []

    def report():
        route = Route(as_ref[...], zs, z)
        returned = route.collect(rb)
        gate = gate_ref[...]
        n, d = returned.shape
        mixed = res_ref[...] + gate * returned
        diff = mixed - route.own(tea_ref[...])
        valid = route.own_col(valid_ref[pl.ds(me, 1), :])
        scale = 1.0 / (jnp.sum(valid_ref[...]) * d)
        weighted = valid * diff
        grad = route.own(cot_ref[...]) + 2.0 * weighted * scale
        sorted_out[span(z, n), :] = mixed.astype(BF)
        pending.extend(gather_z(zs, sorted_out, n, o_s, o_r))
        hot = route.own_hot.astype(F32)
        stat_ref[...] = jnp.zeros_like(stat_ref)
        stat_ref[0:1, 0:EXP] = jnp.sum(hot, axis=0, keepdims=True)
        stat_ref[1:2, 0:EXP] = jnp.sum(hot * gate, axis=0, keepdims=True)
        stat_ref[2:3, :] = jnp.broadcast_to(jnp.sum(weighted * diff * scale), (1, 128))
        for s, peer in enumerate(z_peers(zs)):
            cp = remote(stat_ref, stat_in.at[s], t_s.at[s], t_r.at[s], peer)
            cp.start()
            pending.append(cp)
        gm_ref[...] = grad
        grad_gate = jnp.sum(grad * returned, axis=-1, keepdims=True)
        gl_ref[...] = grad_gate * gate * (1.0 - gate)

    def publish():
        total = stat_ref[...]
        for s, cp in enumerate(pending[zs - 1 :]):
            cp.wait_recv()
            total = total + stat_in[s]
        stat_all[me] = total
        for k, (_, _, _, peer) in enumerate(group):
            cp = remote(stat_all.at[me], stat_all.at[me], u_s.at[k], u_r.at[k], peer)
            cp.start()
            pending.append(cp)

    while t < start + half + 1:
        step(t)
        if given is None and t - lag >= half - 1:
            given = give_back(fs, results, ret, rb, wsem.at[6], b_s, b_r)
        while begun < half and begun <= t - start + ahead and begun <= t - lag2:
            two.cross(begun).start()
            begun += 1
        if 0 <= t - 1 - start < half:
            xg[t - 1 - start] = two.total(t - 1 - start)
        if t == start + half - 2 or (half == 1 and t == start):
            arrived(given)
            report()
        if t == start + half - 1:
            publish()
        t += 1
    given_back = give_back(fs, xg, ret_back, rb_back, wsem.at[7], c_s, c_r)
    route = Route(as_ref[...], zs, z)
    for cp in pending[: zs - 1]:
        cp.wait_recv()
    out_ref[...] = route.unsort(sorted_out[...])
    arrived(given_back)
    gb_ref[...] = route.collect(rb_back)
    for cp in pending[2 * (zs - 1) :]:
        cp.wait_recv()
    for cp in pending + sends + sends_g + given[1] + given_back[1]:
        cp.wait_send()

    @pl.loop(0, half)
    def _(e):
        two.settle(e)

    total = stat_all[0]
    for k in range(1, fs * 4):
        total = total + stat_all[k]
    stat_ref[...] = total


def back_body(fs, zs, rows, gb_ref, res_ref, mi_ref, gm_ref, gl_ref, as_ref, tok_ref, t_ref, w3_ref, wo_ref,
              normed_ref, qt_ref, kv_ref, pt_ref, ctx_ref,
              tg_ref, mix_ref, og_ref, sm_ref,
              sorted_gb, near, away, away_in, far_out, far_in, gn, parts, sorted_tg, dense, dense_in, give, taken, sm_in,
              a_s, a_r, s_s, s_r, t_s, t_r, v_s, v_r, k_s, k_r, g_s, g_r):
    f, i, z, y, c = whereabouts()
    sibling = (f, y * 2 + 1 - c, z)
    across = (f, (1 - y) * 2 + c, z)
    same = []
    for df in range(fs):
        for dy in range(2):
            if df or dy:
                fp = lax.rem(f + df, fs)
                yp = y if dy == 0 else 1 - y
                same.append((fp, yp, (fp, yp * 2 + c, z)))
    greet(z_peers(zs) + [sibling] + [s[2] for s in same])
    route = Route(as_ref[...], zs, z)
    k = qt_ref.shape[0]
    gl = gl_ref[...]
    grad_in = gb_ref[...] + gl * nn(route.own_hot, t_ref[0:EXP, :])
    m, d = grad_in.shape
    xhat, inv = norm_parts(res_ref[...])
    grad = gm_ref[...] + norm_back(grad_in, xhat, inv, t_ref[33:34, :].astype(F32))
    sorted_gb[span(z, m), :] = grad.astype(BF)
    gathers = gather_z(zs, sorted_gb, m, a_s, a_r)
    g2 = jnp.sum(grad_in * xhat, axis=0, keepdims=True)
    cg = _dot(route.own_hot.astype(F32) * gl, mi_ref[...].astype(F32), 0, 0, TOP)
    all_tok = norm_parts(tok_ref[...].astype(F32))[0]
    own_tok, own_inv = norm_parts(route.own(tok_ref[...]))
    for cp in gathers:
        cp.wait_recv()
    gb = route.unsort(sorted_gb[...])
    gct = jnp.transpose(nn(gb, wo_ref[...])).astype(BF)
    dq = attend_back(gct, qt_ref, kv_ref, pt_ref, near, away)
    swap = remote(away, away_in, k_s.at[0], k_r.at[0], sibling)
    swap.start()
    og = tn(gb, ctx_ref[...])
    swap.wait_recv()
    far_out[...] = (near[1] + away_in[1]).astype(BF)
    cross = remote(far_out, far_in, k_s.at[1], k_r.at[1], across)
    cross.start()
    normed = normed_ref[...]
    mg = [tn(normed, dq), None, None]
    gq = nt(dq, w3_ref[0])
    cross.wait_recv()
    kvg = (near[0] + away_in[0] + far_in[...].astype(F32)).astype(BF)
    partial_normed = gq + nt(kvg[:, :k], w3_ref[1]) + nt(kvg[:, k:], w3_ref[2])
    gn[...] = route.sort(partial_normed.astype(BF))
    n = gn.shape[0]
    scat = []
    for s, peer in enumerate(z_peers(zs)):
        cp = remote(gn.at[span(lax.rem(z + s + 1, zs), m)], parts.at[s], s_s.at[s], s_r.at[s], peer)
        cp.start()
        scat.append(cp)
    mg[1] = tn(normed, kvg[:, :k])
    mg[2] = tn(normed, kvg[:, k:])
    g1 = jnp.sum(partial_normed * all_tok, axis=0, keepdims=True)
    last = dense.shape[3] - TAB
    small = jnp.concatenate([cg, g1, g2, jnp.zeros((TAB - EXP - 2, d), F32)], axis=0)
    for s in range(4 * fs):
        at = (s // 4, s % 4 // 2, s % 2)
        lo = s * rows
        for j in range(3):
            dense[at[0], at[1], at[2], 0:rows, j * k : (j + 1) * k] = mg[j][lo : lo + rows, :]
        dense[at[0], at[1], at[2], 0:rows, 3 * k : 4 * k] = og[lo : lo + rows, :]
        dense[at[0], at[1], at[2], last : last + TAB, 0:rows] = small[:, lo : lo + rows]
    pair = remote(dense.at[:, :, 1 - c], dense_in, k_s.at[2], k_r.at[2], sibling)
    pair.start()
    pair.wait_recv()
    shares = []
    for s, (fp, yp, peer) in enumerate(same):
        give[s] = (dense[fp, yp, c] + dense_in[fp, yp]).astype(BF)
        cp = remote(give.at[s], taken.at[s], g_s.at[s], g_r.at[s], peer)
        cp.start()
        shares.append(cp)
    total = gn[span(z, m), :].astype(F32)
    for s, cp in enumerate(scat):
        cp.wait_recv()
        total = total + parts[s].astype(F32)
    tg = grad + norm_back(total, own_tok, own_inv, t_ref[32:33, :].astype(F32))
    sorted_tg[span(z, m), :] = tg.astype(BF)
    ends = gather_z(zs, sorted_tg, m, t_s, t_r)
    kept = dense[f, y, c] + dense_in[f, y]
    for s, cp in enumerate(shares):
        cp.wait_recv()
        kept = kept + taken[s].astype(F32)
    sm_ref[...] = kept[last:, :128]
    smalls = []
    for s, peer in enumerate(z_peers(zs)):
        cp = remote(sm_ref, sm_in.at[s], v_s.at[s], v_r.at[s], peer)
        cp.start()
        smalls.append(cp)
    for j in range(3):
        mix_ref[j] = kept[:rows, j * k : (j + 1) * k]
    og_ref[...] = jnp.transpose(kept[:rows, 3 * k :])
    for cp in ends:
        cp.wait_recv()
    tg_ref[...] = route.unsort(sorted_tg[...])
    for cp in smalls:
        cp.wait()
    total = sm_ref[...]
    for s in range(zs - 1):
        total = total + sm_in[s]
    sm_ref[...] = total
    for cp in gathers + [swap, cross, pair] + scat + shares + ends:
        cp.wait_send()


def per_device(tokens, mixing_weight, output_weight, first_gain, second_gain, centroids, expert_up,
               expert_down, prefix_length, assignment, validity, teacher, cotangent):
    fs, zs = lax.axis_size("fsdp"), lax.axis_size("tp")
    f, i, z = lax.axis_index("fsdp"), lax.axis_index("ctx"), lax.axis_index("tp")
    c = lax.rem(i, 2)
    n, d = tokens.shape[1], tokens.shape[2]
    rows, k = mixing_weight.shape[0], mixing_weight.shape[2]
    local_experts, width, units = expert_up.shape
    half = local_experts // 2
    experts = centroids.shape[0]
    sources = fs * 4
    heads = k // HD
    dma = pltpu.SemaphoreType.DMA
    smem = pl.BlockSpec(memory_space=pltpu.SMEM)
    anyspec = pl.BlockSpec(memory_space=ANY)
    core_pairs = [(0, 1), (1, 0), (2, 3), (3, 2)]

    def core_swap(v):
        return lax.ppermute(v, "ctx", core_pairs)

    down = expert_down.transpose(0, 2, 1)
    mixing = mixing_weight.transpose(1, 0, 2)
    tok = tokens[0]
    chosen = assignment.reshape(1, n)
    small = jnp.concatenate(
        [
            jnp.pad(jnp.concatenate([centroids, first_gain[None], second_gain[None]]), ((0, 0), (0, n - rows))),
            validity.astype(BF),
            jnp.zeros((TAB - experts - 3, n), BF),
        ]
    )
    swapped = (half, width, units)
    per = CAP // zs
    m = n // zs
    r = half * per
    row_shape = (fs, 2, 2, r, d // 2)
    weight_shapes = [sds((3, d, k), BF), sds((d, k), BF), sds((TAB, d), BF), sds((sources, n), F32)]
    swap_shapes = [sds(swapped, BF)] * 2
    token_shapes = [
        sds((n, d), BF), sds((k, n), BF), sds((4, n, 2 * k), BF), sds((heads, 4, n, n), BF), sds((n, k), BF),
        sds((m, d), F32), sds((m, d), BF), sds((m, 1), F32), sds(row_shape, BF), sds(row_shape[:4] + (d // 2 + 128,), BF),
    ]
    scattered = [VMEM((n, d), BF), VMEM((zs - 1, m, d), BF)]
    exchange = scattered + [dma((zs - 1,))] * 2 + [dma((2,))] * 2 + [dma((3,))] * 2
    gather = rows % 16 == 0
    if gather:
        head_in = (prefix_length, tok, mixing, output_weight, small, chosen, teacher[0], cotangent[0], expert_up, down)
        out_shapes = weight_shapes + swap_shapes + token_shapes
        out_specs = [vspec()] * 4 + [anyspec] * 2 + [vspec()] * 10
        scratch = [VMEM((sources, TAB, n), BF)] + exchange + [dma((2 * fs - 1, 3))] * 2 + [dma((2 * fs, 3))] * 2
    else:
        everyone = ("fsdp", "ctx")
        w3 = lax.all_gather(mixing, everyone, axis=1, tiled=True)
        wo = lax.all_gather(output_weight, everyone, axis=1, tiled=True).T
        table = lax.all_gather(small, everyone, axis=0)
        valid_all = table[:, experts + 2, :].astype(F32)
        table = table[:, :, :rows].transpose(1, 0, 2).reshape(TAB, d)
        head_in = (prefix_length, tok, w3, wo, table, valid_all, chosen, teacher[0], cotangent[0], expert_up, down)
        out_shapes = swap_shapes + token_shapes
        out_specs = [anyspec] * 2 + [vspec()] * 10
        scratch = exchange
    results = pl.pallas_call(
        partial(head_body, fs, zs, gather),
        out_shape=out_shapes,
        in_specs=[smem] + [vspec()] * (len(head_in) - 3) + [anyspec] * 2,
        out_specs=out_specs,
        scratch_shapes=scratch,
        compiler_params=params(1),
        name="head",
    )(*head_in)
    if gather:
        w3, wo, table, valid_all = results[:4]
        results = results[4:]
    up_x, dn_x, normed, qt, kv, pt, ctx, residual, mixed_in, gate, slots, slots_g = results

    slots_in = sources * CAP
    dh = d // 2
    hidden = (half, slots_in, units)
    received = (half, slots_in, dh)
    x, act, gx, gh, activations, grad_mixed, grad_logit, grad_back, stats = pl.pallas_call(
        partial(middle_body, fs, zs),
        out_shape=[
            sds(received, BF), sds(hidden, BF), sds(received, BF), sds(hidden, BF), sds((n, d), BF),
            sds((m, d), F32), sds((m, 1), F32), sds((m, d), F32), sds((8, 128), F32),
        ],
        in_specs=[vspec()] * 8 + [anyspec] * 4,
        out_specs=[vspec()] * 9,
        scratch_shapes=[
            VMEM((half, dh, units), BF), VMEM((half, dh, units), BF), VMEM(hidden, BF),
            VMEM((sources, r, dh), BF), VMEM((sources, r, dh + 128), BF), VMEM((half, sources * per, dh + 128), BF),
            VMEM((half, sources * per, dh), BF),
            VMEM((sources, r, dh), BF), VMEM((sources, r, dh), BF), VMEM((sources, r, dh), BF), VMEM((sources, r, dh), BF),
            VMEM((n, d), BF), VMEM((zs - 1, 8, 128), F32), VMEM((sources, 8, 128), F32),
            VMEM((half, sources * per, dh), BF), VMEM((half, sources * per, dh), BF),
            VMEM(hidden, BF), VMEM(hidden, BF), VMEM(hidden, BF),
            VMEM(received, BF), VMEM((half, zs - 1, sources * per, dh), BF),
        ]
        + pass_sems(zs, half) * 2
        + [dma((8,))] + [dma((sources - 1,))] * 8 + [dma((zs - 1,))] * 4 + [dma((sources - 1,))] * 2,
        compiler_params=params(2),
        name="middle",
    )(slots, slots_g, residual, gate, chosen, valid_all, teacher[0], cotangent[0], expert_up, up_x, down, dn_x)
    x_x, act_x, gx_x, gh_x = core_swap(x), core_swap(act), core_swap(gx), core_swap(gh)
    all_tokens = float(n * sources)
    share = stats[0, :experts] / all_tokens - 1.0 / experts
    balance = experts * experts * jnp.sum(share * stats[1, :experts] / all_tokens)
    distill = stats[2, 0]

    piece = (rows + (-rows % 16) + TAB, 4 * k)
    others = 2 * fs - 1
    tokens_gradient, mix_part, out_part, small_part = pl.pallas_call(
        partial(back_body, fs, zs, rows),
        out_shape=[sds((n, d), BF), sds((3, rows, k), F32), sds((k, rows), F32), sds((TAB, 128), F32)],
        in_specs=[vspec()] * 15,
        out_specs=[vspec()] * 4,
        scratch_shapes=[
            VMEM((n, d), BF), VMEM((2, n, 2 * k), F32), VMEM((2, n, 2 * k), F32), VMEM((2, n, 2 * k), F32),
            VMEM((n, 2 * k), BF), VMEM((n, 2 * k), BF), VMEM((n, d), BF), VMEM((zs - 1, m, d), BF), VMEM((n, d), BF),
            VMEM((fs, 2, 2) + piece, F32), VMEM((fs, 2) + piece, F32),
            VMEM((others,) + piece, BF), VMEM((others,) + piece, BF), VMEM((zs - 1, TAB, 128), F32),
        ]
        + [dma((zs - 1,))] * 8 + [dma((3,))] * 2 + [dma((others,))] * 2,
        compiler_params=params(3),
        name="back",
    )(grad_back, residual, mixed_in, grad_mixed, grad_logit, chosen, tok, table, w3, wo, normed, qt, kv, pt, ctx)
    up_gradient, down_gradient = expert_grads(c, x, gh, x_x, gh_x, gx, act, gx_x, act_x)

    return (
        activations[None],
        tokens_gradient[None],
        mix_part.transpose(1, 0, 2),
        out_part,
        small_part[experts, :rows],
        small_part[experts + 1, :rows],
        small_part[:experts, :rows],
        up_gradient,
        down_gradient.transpose(0, 2, 1),
        balance,
        distill,
    )


def solution(mesh):
    in_specs = (
        P("fsdp", "ctx", None),
        P(("fsdp", "ctx"), None, "tp"),
        P("tp", ("fsdp", "ctx")),
        P(("fsdp", "ctx")),
        P(("fsdp", "ctx")),
        P(None, ("fsdp", "ctx")),
        P("fsdp", "ctx", "tp"),
        P("fsdp", "tp", "ctx"),
        P("fsdp"),
        P("fsdp", "ctx", None),
        P("fsdp", "ctx"),
        P("fsdp", "ctx", None),
        P("fsdp", "ctx", None),
    )
    out_specs = (
        P("fsdp", "ctx", None),
        P("fsdp", "ctx", None),
        P(("fsdp", "ctx"), None, "tp"),
        P("tp", ("fsdp", "ctx")),
        P(("fsdp", "ctx")),
        P(("fsdp", "ctx")),
        P(None, ("fsdp", "ctx")),
        P("fsdp", "ctx", "tp"),
        P("fsdp", "tp", "ctx"),
        P(),
        P(),
    )
    return jax.shard_map(
        per_device, mesh=mesh, in_specs=in_specs, out_specs=out_specs, check_vma=False
    )
```

```python
from functools import partial
import math
from types import SimpleNamespace

import jax
import jax.numpy as jnp
from jax import lax
from jax.experimental import pallas as pl
from jax.experimental.pallas import tpu as pltpu
from jax.sharding import PartitionSpec as P

HD = 64
EPSILON = 1e-05
BF = jnp.bfloat16
F32 = jnp.float32
MESH = pl.DeviceIdType.MESH
TOP = lax.Precision.HIGHEST
VMEM = pltpu.VMEM
ANY = pl.ANY
CAP = 16
EXP = 32
TAB = 48


def _dot(a, b, ca, cb, precision=None):
    return lax.dot_general(
        a, b, (((ca,), (cb,)), ((), ())), preferred_element_type=F32, precision=precision
    )


def nn(a, b):
    return _dot(a, b, 1, 0)


def nt(a, b):
    return _dot(a, b, 1, 1)


def tn(a, b):
    return _dot(a, b, 0, 0)


def vspec():
    return pl.BlockSpec(memory_space=VMEM)


def sds(shape, dtype):
    return jax.ShapeDtypeStruct(shape, dtype)


def params(cid=None, mib=56):
    if cid is None:
        return pltpu.CompilerParams(vmem_limit_bytes=mib * 2**20)
    return pltpu.CompilerParams(
        vmem_limit_bytes=mib * 2**20, collective_id=cid, has_side_effects=True
    )


def iota(shape, dim):
    return lax.broadcasted_iota(jnp.int32, shape, dim)


def to_col(row):
    n = row.shape[1]
    return jnp.sum(jnp.where(iota((n, n), 0) == iota((n, n), 1), row, 0.0), axis=1, keepdims=True)


def to_row(col):
    n = col.shape[0]
    return jnp.sum(jnp.where(iota((n, n), 0) == iota((n, n), 1), col, 0.0), axis=0, keepdims=True)


def norm_parts(x):
    c = x - jnp.mean(x, axis=-1, keepdims=True)
    inv = lax.rsqrt(jnp.mean(c * c, axis=-1, keepdims=True) + EPSILON)
    return c * inv, inv


def norm_back(grad, xhat, inv, gain):
    gx = grad * gain
    return inv * (
        gx
        - jnp.mean(gx, axis=-1, keepdims=True)
        - xhat * jnp.mean(gx * xhat, axis=-1, keepdims=True)
    )


def log2(v):
    return v.bit_length() - 1


def shifted(v, by):
    return lax.shift_right_logical(v, by)


class Route:
    def __init__(self, chosen, zs, z, width=0):
        n = chosen.shape[1]
        m = n // zs
        per = CAP // zs
        chosen = to_col(chosen.astype(F32))
        self.hot = (chosen == iota((n, EXP), 1).astype(F32)).astype(BF)
        lower = (iota((n, n), 1) < iota((n, n), 0)).astype(BF)
        rank = jnp.sum(nn(lower, self.hot) * self.hot.astype(F32), axis=1, keepdims=True)
        turn = jnp.floor(rank * (1.0 / zs))
        owner = rank - zs * turn
        owned = (owner == iota((n, zs), 1).astype(F32)).astype(BF)
        place = jnp.sum(nn(lower, owned) * owned.astype(F32), axis=1, keepdims=True)
        self.at = owner * m + place
        self.at_row = to_row(self.at)
        mine = iota((m, n), 0).astype(F32) + lax.convert_element_type(z * m, F32) == self.at_row
        self.mine = mine.astype(BF)
        self.mine_mask = mine
        self.slot = self.own_col(to_row(chosen * per + turn))
        self.own_hot = nn(self.mine, self.hot).astype(BF)
        self.slots = EXP * per
        self.n, self.m, self.width = n, m, width

    def own_col(self, row):
        return jnp.sum(jnp.where(self.mine_mask, row, 0.0), axis=1, keepdims=True)

    def own(self, rows):
        return nn(self.mine, rows)

    def sort(self, rows):
        return nn((iota((self.n, self.n), 0).astype(F32) == self.at_row).astype(BF), rows).astype(BF)

    def unsort(self, rows):
        return nn((iota((self.n, self.n), 1).astype(F32) == self.at).astype(BF), rows).astype(BF)

    def fill(self, rows, s_ref):
        place = (iota((self.slots, self.m), 0).astype(F32) == to_row(self.slot)).astype(BF)
        filled = nn(place, rows).astype(BF)
        fs, _, _, r, _ = s_ref.shape
        h = self.width // 2
        for f in range(fs):
            for c in range(2):
                at = (f * 2 + c) * r
                for y in range(2):
                    s_ref[f, y, c, :, :h] = filled[at : at + r, y * h : (y + 1) * h]
                    if rows.shape[1] > self.width:
                        s_ref[f, y, c, :, h:] = filled[at : at + r, self.width :]

    def collect(self, rb_ref):
        parts = []
        for f in range(rb_ref.shape[0] // 4):
            for c in range(2):
                parts.append(jnp.concatenate([rb_ref[f * 4 + c], rb_ref[f * 4 + 2 + c]], axis=1))
        rows = jnp.concatenate(parts, axis=0)
        place = (iota((self.m, self.slots), 1).astype(F32) == self.slot).astype(BF)
        return nn(place, rows)


def z_peers(zs):
    f, i, z = lax.axis_index("fsdp"), lax.axis_index("ctx"), lax.axis_index("tp")
    return [(f, i, lax.rem(z + s, zs)) for s in range(1, zs)]


def greet(peers):
    barrier = pltpu.get_barrier_semaphore()
    for peer in peers:
        pl.semaphore_signal(barrier, inc=1, device_id=peer, device_id_type=MESH)
    pl.semaphore_wait(barrier, len(peers))


def remote(src, dst, send, recv, peer):
    return pltpu.make_async_remote_copy(
        src_ref=src, dst_ref=dst, send_sem=send, recv_sem=recv, device_id=peer, device_id_type=MESH
    )


def scatter_z(zs, x_ref, parts, send, recv):
    z = lax.axis_index("tp")
    n = x_ref.shape[0] // zs
    copies = []
    for s, peer in enumerate(z_peers(zs)):
        to = lax.rem(z + s + 1, zs)
        cp = remote(x_ref.at[span(to, n)], parts.at[s], send.at[s], recv.at[s], peer)
        cp.start()
        copies.append(cp)
    total = x_ref[span(z, n), :].astype(F32)
    for s, cp in enumerate(copies):
        cp.wait_recv()
        total = total + parts[s].astype(F32)
    return total, copies


def gather_z(zs, x_ref, n, send, recv):
    z = lax.axis_index("tp")
    copies = []
    for s, peer in enumerate(z_peers(zs)):
        cp = remote(x_ref.at[span(z, n)], x_ref.at[span(z, n)], send.at[s], recv.at[s], peer)
        cp.start()
        copies.append(cp)
    return copies


def span(at, n):
    return pl.ds(pl.multiple_of(at * n, n), n)


def group_peers(fs):
    f, i, z = lax.axis_index("fsdp"), lax.axis_index("ctx"), lax.axis_index("tp")
    y, c = lax.div(i, 2), lax.rem(i, 2)
    out = []
    for df in range(fs):
        for dy in range(2):
            for dc in range(2):
                if df or dy or dc:
                    fp = lax.rem(f + df, fs)
                    yp = y if dy == 0 else 1 - y
                    cp = c if dc == 0 else 1 - c
                    out.append((fp, yp, cp, (fp, yp * 2 + cp, z)))
    return out


def attend(mine, prefix, offsets, qt_ref, kv_ref, valid_ref, row0, pt_ref, sc_ref, arrive):
    k, n = qt_ref.shape
    heads = k // HD
    query = iota((n, n), 1) + mine * n
    for j in (0, 2, 1, 3):
        if j == 1:
            arrive()
        key = iota((n, n), 0) + offsets[j] * n
        col = to_col(valid_ref[pl.ds(row0 + offsets[j], 1), :])
        allowed = ((key <= query) | (key < prefix)) & ((col > 0.5) | (key == query))
        for h in range(heads):
            lo = h * HD
            scores = nn(kv_ref[j, :, lo : lo + HD], qt_ref[lo : lo + HD, :]) * (1.0 / math.sqrt(HD))
            sc_ref[h, j] = jnp.where(allowed, scores, -1e30)
    outs = []
    for h in range(heads):
        lo = h * HD
        top = jnp.max(sc_ref[h, 0], axis=0, keepdims=True)
        for j in range(1, 4):
            top = jnp.maximum(top, jnp.max(sc_ref[h, j], axis=0, keepdims=True))
        exps = [jnp.exp(sc_ref[h, j] - top) for j in range(4)]
        share = 1.0 / sum(jnp.sum(e, axis=0, keepdims=True) for e in exps)
        acc = jnp.zeros((HD, n), F32)
        for j in range(4):
            w = (exps[j] * share).astype(BF)
            pt_ref[h, j] = w
            acc = acc + tn(kv_ref[j, :, k + lo : k + lo + HD], w)
        outs.append(acc)
    return jnp.transpose(jnp.concatenate(outs, axis=0)).astype(BF)


def attend_back(gct, qt_ref, kv_ref, pt_ref, near_ref, away_ref):
    k, n = qt_ref.shape
    scale = 1.0 / math.sqrt(HD)
    dqs = []
    for h in range(k // HD):
        lo = h * HD
        dot_ = gct[lo : lo + HD, :]
        qt = qt_ref[lo : lo + HD, :]
        ws = [pt_ref[h, j] for j in range(4)]
        dps = [nn(kv_ref[j, :, k + lo : k + lo + HD], dot_) for j in range(4)]
        mean = sum(jnp.sum(ws[j].astype(F32) * dps[j], axis=0, keepdims=True) for j in range(4))
        dq = jnp.zeros((HD, n), F32)
        for j in range(4):
            ds = (ws[j].astype(F32) * (dps[j] - mean)).astype(BF)
            dq = dq + tn(kv_ref[j, :, lo : lo + HD], ds)
            target = near_ref if j < 2 else away_ref
            target[j % 2, :, lo : lo + HD] = nt(ds, qt) * scale
            target[j % 2, :, k + lo : k + lo + HD] = nt(ws[j], dot_)
        dqs.append(dq * scale)
    return jnp.transpose(jnp.concatenate(dqs, axis=0)).astype(BF)


def finish_body(scalars, c_ref, *refs):
    tg_in, act_in, mix_in, og_in, sm_in, stat_in = refs[8:14]
    up_ref, down_ref, tg_ref, act_ref, mix_ref, og_ref, cen_ref, g1_ref, g2_ref, bal_ref, dis_ref = refs[14:]
    c = c_ref[0]
    for out_ref, at in ((up_ref, 0), (down_ref, 4)):
        for core, (left_ref, right_ref) in ((c, refs[at : at + 2]), (1 - c, refs[at + 2 : at + 4])):
            for e in range(left_ref.shape[0]):
                out_ref[core, e] = nn(left_ref[e], right_ref[e])

    @pl.when(pl.program_id(0) == 0)
    def _():
        tg_ref[...] = tg_in[...]
        act_ref[...] = act_in[...]
        mix_ref[...] = mix_in[...]
        og_ref[...] = og_in[...]
        rows = cen_ref.shape[1]
        cen_ref[...] = sm_in[0:EXP, :rows]
        g1_ref[...] = sm_in[EXP : EXP + 1, :rows]
        g2_ref[...] = sm_in[EXP + 1 : EXP + 2, :rows]
        share = stat_in[0:1, :EXP] / scalars - 1.0 / EXP
        bal_ref[0, 0] = EXP * EXP * jnp.sum(share * stat_in[1:2, :EXP] / scalars)
        dis_ref[0, 0] = jnp.sum(stat_in[2:3, 0:1])


def finish(c, tokens, pairs, small, shapes):
    half, q, n = pairs[0].shape
    units = pairs[1].shape[2]
    step = 2 if half % 2 == 0 else 1
    block = lambda e, c_ref: (e, 0, 0)
    out = sds((2, half, q, units), F32)
    whole = lambda v: pl.BlockSpec(v.shape, lambda e, c_ref: (0,) * len(v.shape))
    smem = pl.BlockSpec(memory_space=pltpu.SMEM)
    scalar = sds((1, 1), F32)
    return pl.pallas_call(
        partial(finish_body, float(tokens)),
        grid_spec=pltpu.PrefetchScalarGridSpec(
            num_scalar_prefetch=1,
            grid=(half // step,),
            in_specs=[pl.BlockSpec((step, q, n), block), pl.BlockSpec((step, n, units), block)] * 4
            + [whole(v) for v in small],
            out_specs=[pl.BlockSpec((2, step, q, units), lambda e, c_ref: (0, e, 0, 0))] * 2
            + [whole(v) for v in shapes] + [smem] * 2,
        ),
        out_shape=[out, out] + shapes + [scalar] * 2,
        compiler_params=params(),
        name="finish",
    )(c.reshape(1), *pairs, *small)


def whereabouts():
    f, i, z = lax.axis_index("fsdp"), lax.axis_index("ctx"), lax.axis_index("tp")
    return f, i, z, lax.div(i, 2), lax.rem(i, 2)


def reorder(sources, half, per, inverse):
    n = sources * half * per
    i, o = iota((n, n), 1), iota((n, n), 0)
    if inverse:
        i, o = o, i
    ls, lh, lp = log2(sources), log2(half), log2(per)
    slot = o & (per - 1)
    source = shifted(o, lp) & (sources - 1)
    expert = shifted(o, lp + ls)
    return (i == source * (half * per) + expert * per + slot).astype(BF)


class Pass:
    def __init__(self, back, zs, w_in, w_out, xg, x_ref, ps, pr, h_ref, gp_ref, res, rin, sems):
        self.back, self.zs, self.w_in, self.w_out = back, zs, w_in, w_out
        self.xg, self.x_ref, self.ps, self.pr = xg, x_ref, ps, pr
        self.h_ref, self.gp_ref, self.res, self.rin = h_ref, gp_ref, res, rin
        self.a_s, self.a_r, self.x_s, self.x_r, self.r_s, self.r_r = sems
        f, i, z, y, c = whereabouts()
        self.z = z
        self.m = xg.shape[1]
        self.across = (f, (1 - y) * 2 + c, z)
        self.peers = z_peers(zs)

    def share(self, e, s):
        to = self.x_ref.at[e, span(self.z, self.m), :]
        return remote(self.xg.at[e], to, self.a_s.at[e, s], self.a_r.at[e, s], self.peers[s])

    def cross(self, e):
        return remote(self.ps.at[e], self.pr.at[e], self.x_s.at[e], self.x_r.at[e], self.across)

    def scatter(self, e, s):
        to = lax.rem(self.z + s + 1, self.zs)
        return remote(
            self.res.at[e, span(to, self.m), :], self.rin.at[e, s], self.r_s.at[e, s], self.r_r.at[e, s], self.peers[s]
        )

    def spread(self, e, rows):
        self.xg[e] = rows
        for s in range(self.zs - 1):
            self.share(e, s).start()
        self.x_ref[e, span(self.z, self.m), :] = rows

    def first(self, e):
        for s in range(self.zs - 1):
            self.share(e, s).wait_recv()
        self.ps[e] = nn(self.x_ref[e], self.w_in[e]).astype(BF)

    def second(self, e):
        self.cross(e).wait_recv()
        total = self.ps[e].astype(F32) + self.pr[e].astype(F32)
        if self.back:
            self.h_ref[e] = (total * self.gp_ref[e].astype(F32)).astype(BF)
        else:
            phi = 0.5 * (1.0 + lax.erf(total * math.sqrt(0.5)))
            self.h_ref[e] = (total * phi).astype(BF)
            bell = jnp.exp(-0.5 * total * total) * (1.0 / math.sqrt(2.0 * math.pi))
            self.gp_ref[e] = (phi + total * bell).astype(BF)
        self.res[e] = nt(self.h_ref[e], self.w_out[e]).astype(BF)
        for s in range(self.zs - 1):
            self.scatter(e, s).start()

    def total(self, e):
        total = self.res[e, span(self.z, self.m), :].astype(F32)
        for s in range(self.zs - 1):
            self.scatter(e, s).wait_recv()
            total = total + self.rin[e, s].astype(F32)
        return total.astype(BF)

    def settle(self, e):
        self.cross(e).wait_send()
        for s in range(self.zs - 1):
            self.share(e, s).wait_send()
            self.scatter(e, s).wait_send()


def give_back(fs, total, ret, rb_ref, own_sem, send, recv):
    f, i, z, y, c = whereabouts()
    me = f * 4 + i
    sources, r, dh = ret.shape
    half = total.shape[0]
    rows = total[...].reshape(sources * r, dh)
    ret[...] = nn(reorder(sources, half, r // half, True), rows).astype(BF).reshape(sources, r, dh)
    keep = pltpu.make_async_copy(ret.at[me], rb_ref.at[me], own_sem)
    keep.start()
    copies = []
    for k, (fp, yp, cp_, peer) in enumerate(group_peers(fs)):
        cp = remote(ret.at[fp * 4 + yp * 2 + cp_], rb_ref.at[me], send.at[k], recv.at[k], peer)
        cp.start()
        copies.append(cp)
    return keep, copies


def arrived(given):
    keep, copies = given
    keep.wait()
    for cp in copies:
        cp.wait_recv()


def head(R, fs, zs, gather):
    f, i, z, y, c = whereabouts()
    me = f * 4 + i
    half, width = R.wu.shape[0], R.up.shape[1]
    k = R.qt.shape[0]
    d = R.tok.shape[1]
    sibling = (f, y * 2 + 1 - c, z)
    across = (f, (1 - y) * 2 + c, z)
    same = same_core(fs)
    waits = []
    mine = pl.ds(c * half, half)
    theirs = pl.ds((1 - c) * half, half)
    own = pl.ds(pl.multiple_of(c * width, 64), width)
    loads = [
        pltpu.make_async_copy(R.up.at[mine], R.wu.at[:, own, :], R.wsem.at[0]),
        pltpu.make_async_copy(R.dn.at[mine], R.wd.at[:, own, :], R.wsem.at[1]),
    ]
    swaps = [
        remote(R.up.at[theirs], R.wu.at[:, own, :], R.wx_s.at[0], R.wx_r.at[0], sibling),
        remote(R.dn.at[theirs], R.wd.at[:, own, :], R.wx_s.at[1], R.wx_r.at[1], sibling),
    ]
    if gather:
        rows = R.mix.shape[1]
        R.small[...] = jnp.zeros(R.small.shape, F32)
        R.small[0:EXP, :rows] = R.cent[...].astype(F32)
        R.small[EXP : EXP + 1, :rows] = R.gain1[...].astype(F32)
        R.small[EXP + 1 : EXP + 2, :rows] = R.gain2[...].astype(F32)
        R.small[EXP + 2 : EXP + 3, :] = R.here[...].astype(F32)
        R.small_all[me] = R.small[...].astype(BF)
        R.w3[:, span(me, rows), :] = R.mix[...]
        R.wo[span(me, rows), :] = jnp.transpose(R.ow[...].astype(F32)).astype(BF)
    greet([p[3] for p in group_peers(fs)] + z_peers(zs))
    for cp in loads:
        cp.start()
    xhat, _ = norm_parts(R.tok[...].astype(F32))
    if gather:

        def places(at):
            rows_ = span(at, rows)
            return [R.w3.at[1:3, rows_, :], R.small_all.at[at], R.w3.at[0:1, rows_, :], R.wo.at[rows_, :]]

        sends = {}
        for m, ref in enumerate(places(me)):
            for n_, (_, _, peer, _) in enumerate(same):
                cp = remote(ref, ref, R.p_s.at[n_, m], R.p_r.at[n_, m], peer)
                cp.start()
                sends[n_, m] = cp
        relays = {}

        def relay(n_, m, at):
            ref = places(at)[m]
            cp = remote(ref, ref, R.q_s.at[n_, m], R.q_r.at[n_, m], sibling)
            cp.start()
            relays[n_, m] = cp

        def pass_on(some):
            for n_, (_, _, _, at) in enumerate(same):
                for m in some:
                    sends[n_, m].wait_recv()
                    relay(n_ + 1, m, at)

        for m in range(4):
            relay(0, m, me)
        pass_on((0, 1))
        for n_ in range(len(same) + 1):
            for m in (0, 1):
                relays[n_, m].wait_recv()
        R.table[...] = jnp.concatenate([R.small_all[s, :, :rows] for s in range(fs * 4)], axis=1)
        for s in range(fs * 4):
            R.valid[s : s + 1, :] = R.small_all[s, EXP + 2 : EXP + 3, :].astype(F32)
    normed = (xhat * R.table[EXP : EXP + 1, :].astype(F32)).astype(BF)
    R.normed[...] = normed
    R.kv[0, :, :k] = nn(normed, R.w3[1]).astype(BF)
    R.kv[0, :, k:] = nn(normed, R.w3[2]).astype(BF)
    far = remote(R.kv.at[0], R.kv.at[1], R.kv_s.at[0], R.kv_r.at[0], across)
    sib = remote(R.kv.at[0], R.kv.at[2], R.kv_s.at[1], R.kv_r.at[1], sibling)
    far.start()
    sib.start()
    if gather:
        pass_on((2, 3))
        for n_ in range(len(same) + 1):
            for m in (2, 3):
                relays[n_, m].wait_recv()
        waits += list(sends.values()) + list(relays.values())
    R.qt[...] = jnp.transpose(nn(normed, R.w3[0])).astype(BF)
    route = Route(R.chosen[...], zs, z, d)
    teacher, cotangent = route.own(R.tea[...]), route.own(R.cot[...])
    own_valid = route.own_col(R.valid[pl.ds(me, 1), :])
    scale = 1.0 / (jnp.sum(R.valid[...]) * d)
    sib.wait_recv()
    last = []

    def arrive():
        far.wait_recv()
        cp = remote(R.kv.at[1], R.kv.at[3], R.kv_s.at[2], R.kv_r.at[2], sibling)
        cp.start()
        for swap in swaps:
            swap.start()
        cp.wait_recv()
        last.append(cp)

    offsets = [i, (1 - y) * 2 + c, y * 2 + 1 - c, (1 - y) * 2 + 1 - c]
    ctx = attend(i, R.prefix[0], offsets, R.qt, R.kv, R.valid, f * 4, R.pt, R.scores, arrive)
    R.ctx[...] = ctx
    R.branch[...] = route.sort(nt(ctx, R.wo[...]).astype(BF))
    total, sums = scatter_z(zs, R.branch, R.parts, R.hz_s, R.hz_r)
    residual = route.own(R.tok[...]) + total
    R.res[...] = residual
    xhat, _ = norm_parts(residual)
    mixed_in = (xhat * R.table[EXP + 1 : EXP + 2, :].astype(F32)).astype(BF)
    R.mi[...] = mixed_in
    logit = jnp.sum(mixed_in.astype(F32) * nn(route.own_hot, R.table[0:EXP, :]), axis=-1, keepdims=True)
    gate = jax.nn.sigmoid(logit)
    route.fill(mixed_in, R.slots)
    weight = 2.0 * own_valid * scale
    known = gate * (cotangent + weight * (residual - teacher))
    slope = jnp.broadcast_to(gate * gate * weight, (known.shape[0], 128))
    route.fill(jnp.concatenate([known, slope], axis=1).astype(BF), R.slots_g)
    waits += swaps + sums + [far, sib] + last
    return SimpleNamespace(route=route, gate=gate, teacher=teacher, cotangent=cotangent, valid=own_valid, scale=scale,
                           loads=loads, swaps=swaps, waits=waits)


def same_core(fs):
    f, i, z, y, c = whereabouts()
    out = []
    for df in range(fs):
        for dy in range(2):
            if df or dy:
                fp, fm = lax.rem(f + df, fs), lax.rem(f - df + fs, fs)
                yp = y if dy == 0 else 1 - y
                out.append((fp, yp, (fp, yp * 2 + c, z), fm * 4 + yp * 2 + c))
    return out


def middle(R, S, fs, zs):
    f, i, z, y, c = whereabouts()
    me = f * 4 + i
    half, width = R.wu.shape[0], R.up.shape[1]
    sources, r, dh = R.rq.shape
    m = sources * r // half
    group = group_peers(fs)
    sibling = (f, y * 2 + 1 - c, z)
    own = pl.ds(pl.multiple_of(c * width, 64), width)
    other = pl.ds(pl.multiple_of((1 - c) * width, 64), width)
    keeps = [
        pltpu.make_async_copy(R.slots.at[f, y, c], R.rq.at[me], R.wsem.at[2]),
        pltpu.make_async_copy(R.slots_g.at[f, y, c], R.rg.at[me], R.wsem.at[3]),
    ]
    for cp in keeps:
        cp.start()
    sends, sends_g = [], []
    for out, src, dst, send, recv in ((sends, R.slots, R.rq, R.d_s, R.d_r), (sends_g, R.slots_g, R.rg, R.g_s, R.g_r)):
        for k, (fp, yp, cp_, peer) in enumerate(group):
            cp = remote(src.at[fp, yp, cp_], dst.at[me], send.at[k], recv.at[k], peer)
            cp.start()
            out.append(cp)
    sems = [[getattr(R, p + n) for n in ("a_s", "a_r", "x_s", "x_r", "r_s", "r_r")] for p in ("one_", "two_")]
    one = Pass(False, zs, R.wu, R.wd, R.xg, R.x, R.ps, R.pr, R.act, R.gp, R.rows, R.rin, sems[0])
    two = Pass(True, zs, R.wd, R.wu, R.xg_back, R.gx, R.ps, R.pr_back, R.gh, R.gp, R.rows, R.rin, sems[1])
    order = reorder(sources, half, r // half, False)
    exports = []

    def export(n, own_src, own_dst, src, dst):
        keep = pltpu.make_async_copy(own_src, own_dst, R.l_s.at[n])
        give = remote(src, dst, R.e_s.at[n], R.e_r.at[n], sibling)
        keep.start()
        give.start()
        exports.append((keep, give))

    for cp in S.loads:
        cp.wait()
    for cp in S.swaps:
        cp.wait_recv()
    keeps[0].wait()
    for cp in sends:
        cp.wait_recv()
    rows = nn(order, R.rq[...].reshape(sources * r, dh)).astype(BF).reshape(half, m, dh)
    for e in range(half):
        one.spread(e, rows[e])

    @pl.loop(0, half)
    def _(e):
        one.first(e)
        one.cross(e).start()

    @pl.loop(0, half)
    def _(e):
        R.xt[e] = jnp.transpose(R.x[e])

    keeps[1].wait()
    for cp in sends_g:
        cp.wait_recv()
    R.grads[...] = nn(order, R.rg[...].reshape(sources * r, dh + 128)).astype(BF).reshape(half, m, dh + 128)
    export(0, R.xt.at[:, own, :], R.xt_own, R.xt.at[:, other, :], R.xt_sib)

    def turn(e):
        result = one.total(e)
        R.results[e] = result
        scale = R.grads[e, :, dh:].astype(F32)[:, :1]
        two.spread(e, (R.grads[e, :, :dh].astype(F32) + scale * result.astype(F32)).astype(BF))

    lag, lag2 = 2, 4
    start = max(half, lag2 + 1)
    ahead = 3

    def step(t, fixed=True):
        if not fixed or t < half:
            one.second(t)
        if fixed and t - start >= 0 and t - start < half:
            two.second(t - start)
        if not fixed or 0 <= t - lag < half:
            turn(t - lag)
        if not fixed or 0 <= t - lag2 < half:
            one.settle(t - lag2)
            two.first(t - lag2)

    begun = 0
    t = 0
    while t < lag2:
        step(t)
        t += 1
    safe = max(t, start - ahead)
    if safe > t and half > t:
        stop = min(safe, half)

        @pl.loop(t, stop)
        def _(k):
            step(k, False)

        t = stop
    given = None
    pending = []

    def report():
        returned = S.route.collect(R.rb)
        n, d = returned.shape
        mixed = R.res[...] + S.gate * returned
        diff = mixed - S.teacher
        weighted = S.valid * diff
        grad = S.cotangent + 2.0 * weighted * S.scale
        R.sorted_out[span(z, n), :] = mixed.astype(BF)
        pending.extend(gather_z(zs, R.sorted_out, n, R.o_s, R.o_r))
        hot = S.route.own_hot.astype(F32)
        R.stat[...] = jnp.zeros_like(R.stat)
        R.stat[0:1, 0:EXP] = jnp.sum(hot, axis=0, keepdims=True)
        R.stat[1:2, 0:EXP] = jnp.sum(hot * S.gate, axis=0, keepdims=True)
        R.stat[2:3, :] = jnp.broadcast_to(jnp.sum(weighted * diff * S.scale), (1, 128))
        for s, peer in enumerate(z_peers(zs)):
            cp = remote(R.stat, R.stat_in.at[s], R.t_s.at[s], R.t_r.at[s], peer)
            cp.start()
            pending.append(cp)
        R.gm[...] = grad
        grad_gate = jnp.sum(grad * returned, axis=-1, keepdims=True)
        R.gl[...] = grad_gate * S.gate * (1.0 - S.gate)

    def publish():
        total = R.stat[...]
        for s, cp in enumerate(pending[zs - 1 :]):
            cp.wait_recv()
            total = total + R.stat_in[s]
        R.stat_all[me] = total
        for k, (_, _, _, peer) in enumerate(group):
            cp = remote(R.stat_all.at[me], R.stat_all.at[me], R.u_s.at[k], R.u_r.at[k], peer)
            cp.start()
            pending.append(cp)

    while t < start + half + 1:
        step(t)
        if given is None and t - lag >= half - 1:
            given = give_back(fs, R.results, R.ret, R.rb, R.wsem.at[4], R.b_s, R.b_r)
            export(1, R.act, R.act_own, R.act, R.act_sib)
        while begun < half and begun <= t - start + ahead and begun <= t - lag2:
            two.cross(begun).start()
            begun += 1
        if 0 <= t - 1 - start < half:
            R.xg[t - 1 - start] = two.total(t - 1 - start)
        if t == max(start + half - 4, start + 1) or (half == 1 and t == start):

            @pl.loop(0, half)
            def _(e):
                R.gxt[e] = jnp.transpose(R.gx[e])

        if t == start + half - 2 or (half == 1 and t == start):
            arrived(given)
            report()
        if t == start + half - 1:
            publish()
        t += 1
    given_back = give_back(fs, R.xg, R.ret_back, R.rb_back, R.wsem.at[5], R.c_s, R.c_r)
    export(2, R.gxt.at[:, own, :], R.gxt_own, R.gxt.at[:, other, :], R.gxt_sib)
    export(3, R.gh, R.gh_own, R.gh, R.gh_sib)
    S.pending, S.exports = pending, exports
    S.waits += pending[: 2 * (zs - 1)] + sends + sends_g + given[1] + given_back[1]
    S.two = two
    arrived(given_back)
    return S.route.collect(R.rb_back)


def back(R, S, grad_back, fs, zs, rows):
    f, i, z, y, c = whereabouts()
    sibling = (f, y * 2 + 1 - c, z)
    across = (f, (1 - y) * 2 + c, z)
    same = same_core(fs)
    route = S.route
    k = R.qt.shape[0]
    gl = R.gl[...]
    grad_in = grad_back + gl * nn(route.own_hot, R.table[0:EXP, :])
    m, d = grad_in.shape
    xhat, inv = norm_parts(R.res[...])
    grad = R.gm[...] + norm_back(grad_in, xhat, inv, R.table[EXP + 1 : EXP + 2, :].astype(F32))
    R.sorted_gb[span(z, m), :] = grad.astype(BF)
    gathers = gather_z(zs, R.sorted_gb, m, R.ba_s, R.ba_r)
    g2 = jnp.sum(grad_in * xhat, axis=0, keepdims=True)
    cg = _dot(route.own_hot.astype(F32) * gl, R.mi[...].astype(F32), 0, 0, TOP)
    all_tok = norm_parts(R.tok[...].astype(F32))[0]
    own_tok, own_inv = norm_parts(route.own(R.tok[...]))
    for cp in S.pending[: zs - 1]:
        cp.wait_recv()
    R.out[...] = route.unsort(R.sorted_out[...])
    for cp in S.pending[2 * (zs - 1) :]:
        cp.wait()
    total = R.stat_all[0]
    for n in range(1, fs * 4):
        total = total + R.stat_all[n]
    R.stat_out[...] = total
    for cp in gathers:
        cp.wait_recv()
    gb = route.unsort(R.sorted_gb[...])
    gct = jnp.transpose(nn(gb, R.wo[...])).astype(BF)
    dq = attend_back(gct, R.qt, R.kv, R.pt, R.near, R.away)
    swap = remote(R.away, R.away_in, R.k_s.at[0], R.k_r.at[0], sibling)
    swap.start()
    og = tn(gb, R.ctx[...])
    swap.wait_recv()
    R.far_out[...] = (R.near[1] + R.away_in[1]).astype(BF)
    cross = remote(R.far_out, R.far_in, R.k_s.at[1], R.k_r.at[1], across)
    cross.start()
    normed = R.normed[...]
    mg = [tn(normed, dq), None, None]
    gq = nt(dq, R.w3[0])
    cross.wait_recv()
    kvg = (R.near[0] + R.away_in[0] + R.far_in[...].astype(F32)).astype(BF)
    partial_normed = gq + nt(kvg[:, :k], R.w3[1]) + nt(kvg[:, k:], R.w3[2])
    R.gn[...] = route.sort(partial_normed.astype(BF))
    scat = []
    for s, peer in enumerate(z_peers(zs)):
        cp = remote(R.gn.at[span(lax.rem(z + s + 1, zs), m)], R.gn_in.at[s], R.bs_s.at[s], R.bs_r.at[s], peer)
        cp.start()
        scat.append(cp)
    mg[1] = tn(normed, kvg[:, :k])
    mg[2] = tn(normed, kvg[:, k:])
    g1 = jnp.sum(partial_normed * all_tok, axis=0, keepdims=True)
    dense = R.dense
    last = dense.shape[3] - TAB
    small = jnp.concatenate([cg, g1, g2, jnp.zeros((TAB - EXP - 2, d), F32)], axis=0)
    for s in range(4 * fs):
        at = (s // 4, s % 4 // 2, s % 2)
        lo = s * rows
        for j in range(3):
            dense[at[0], at[1], at[2], 0:rows, j * k : (j + 1) * k] = mg[j][lo : lo + rows, :]
        dense[at[0], at[1], at[2], 0:rows, 3 * k : 4 * k] = og[lo : lo + rows, :]
        dense[at[0], at[1], at[2], last : last + TAB, 0:rows] = small[:, lo : lo + rows]
    pair = remote(dense.at[:, :, 1 - c], R.dense_in, R.k_s.at[2], R.k_r.at[2], sibling)
    pair.start()
    pair.wait_recv()
    shares = []
    for s, (fp, yp, peer, _) in enumerate(same):
        R.give[s] = (dense[fp, yp, c] + R.dense_in[fp, yp]).astype(BF)
        cp = remote(R.give.at[s], R.taken.at[s], R.bg_s.at[s], R.bg_r.at[s], peer)
        cp.start()
        shares.append(cp)
    total = R.gn[span(z, m), :].astype(F32)
    for s, cp in enumerate(scat):
        cp.wait_recv()
        total = total + R.gn_in[s].astype(F32)
    tg = grad + norm_back(total, own_tok, own_inv, R.table[EXP : EXP + 1, :].astype(F32))
    R.sorted_tg[span(z, m), :] = tg.astype(BF)
    ends = gather_z(zs, R.sorted_tg, m, R.bt_s, R.bt_r)
    kept = dense[f, y, c] + R.dense_in[f, y]
    for s, cp in enumerate(shares):
        cp.wait_recv()
        kept = kept + R.taken[s].astype(F32)
    R.sm[...] = kept[last:, :128]
    smalls = []
    for s, peer in enumerate(z_peers(zs)):
        cp = remote(R.sm, R.sm_in.at[s], R.v_s.at[s], R.v_r.at[s], peer)
        cp.start()
        smalls.append(cp)
    for j in range(3):
        R.mix_out[j] = kept[:rows, j * k : (j + 1) * k]
    R.og_out[...] = jnp.transpose(kept[:rows, 3 * k :])
    for keep, give in S.exports:
        keep.wait()
        give.wait()
    for cp in ends:
        cp.wait_recv()
    R.tg_out[...] = route.unsort(R.sorted_tg[...])
    total = R.sm[...]
    for s, cp in enumerate(smalls):
        cp.wait_recv()
        total = total + R.sm_in[s]
    R.sm_out[...] = total
    for cp in S.waits + gathers + [swap, cross, pair] + scat + shares + ends + smalls:
        cp.wait_send()

    @pl.loop(0, R.wu.shape[0])
    def _(e):
        S.two.settle(e)


def layer_body(names, fs, zs, gather, rows, *refs):
    R = SimpleNamespace(**dict(zip(names, refs)))
    S = head(R, fs, zs, gather)
    grad_back = middle(R, S, fs, zs)
    back(R, S, grad_back, fs, zs, rows)


def per_device(tokens, mixing_weight, output_weight, first_gain, second_gain, centroids, expert_up,
               expert_down, prefix_length, assignment, validity, teacher, cotangent):
    fs, zs = lax.axis_size("fsdp"), lax.axis_size("tp")
    c = lax.rem(lax.axis_index("ctx"), 2)
    n, d = tokens.shape[1], tokens.shape[2]
    rows, k = mixing_weight.shape[0], mixing_weight.shape[2]
    local_experts, width, units = expert_up.shape
    half = local_experts // 2
    experts = centroids.shape[0]
    sources = fs * 4
    heads = k // HD
    dma = pltpu.SemaphoreType.DMA
    per = CAP // zs
    m = n // zs
    r = half * per
    dh = d // 2
    own_rows = sources * per
    slots_in = sources * CAP
    others = 2 * fs - 1
    smem = pl.BlockSpec(memory_space=pltpu.SMEM)
    anyspec = pl.BlockSpec(memory_space=ANY)

    mixing = mixing_weight.transpose(1, 0, 2)
    ins = [("prefix", prefix_length, smem), ("tok", tokens[0], vspec()), ("chosen", assignment.reshape(1, n), vspec()),
           ("tea", teacher[0], vspec()), ("cot", cotangent[0], vspec()),
           ("up", expert_up, anyspec), ("dn", expert_down.transpose(0, 2, 1), anyspec)]
    scratch = []
    weights = [("w3", (3, d, k), BF), ("wo", (d, k), BF), ("table", (TAB, d), BF), ("valid", (sources, n), F32)]
    gather = rows % 16 == 0
    if gather:
        ins += [("mix", mixing, vspec()), ("ow", output_weight, vspec()), ("cent", centroids, vspec()),
                ("gain1", first_gain.reshape(1, rows), vspec()), ("gain2", second_gain.reshape(1, rows), vspec()),
                ("here", validity, vspec())]
        scratch += weights
        scratch += [("small", (TAB, n), F32), ("small_all", (sources, TAB, n), BF)]
        scratch += [(v, (others + w, 4), dma) for v, w in (("p_s", 0), ("p_r", 0), ("q_s", 1), ("q_r", 1))]
    else:
        small = jnp.concatenate(
            [
                jnp.pad(jnp.concatenate([centroids, first_gain[None], second_gain[None]]), ((0, 0), (0, n - rows))),
                validity.astype(BF),
                jnp.zeros((TAB - experts - 3, n), BF),
            ]
        )
        everyone = ("fsdp", "ctx")
        table = lax.all_gather(small, everyone, axis=0)
        full = (
            lax.all_gather(mixing, everyone, axis=1, tiled=True),
            lax.all_gather(output_weight, everyone, axis=1, tiled=True).T,
            table[:, :, :rows].transpose(1, 0, 2).reshape(TAB, d),
            table[:, experts + 2, :].astype(F32),
        )
        ins += [(w[0], v, vspec()) for w, v in zip(weights, full)]
    hidden, received, left = (half, slots_in, units), (half, slots_in, dh), (half, width, slots_in)
    outs = [(name, shape, BF, anyspec) for name, shape in (
        ("xt_own", left), ("xt_sib", left), ("act_own", hidden), ("act_sib", hidden),
        ("gxt_own", left), ("gxt_sib", left), ("gh_own", hidden), ("gh_sib", hidden))]
    outs += [("tg_out", (n, d), BF, vspec()), ("out", (n, d), BF, vspec()), ("mix_out", (3, rows, k), F32, vspec()),
             ("og_out", (k, rows), F32, vspec()), ("sm_out", (TAB, 128), F32, vspec()), ("stat_out", (8, 128), F32, vspec())]
    piece = (rows + (-rows % 16) + TAB, 4 * k)
    slots = (fs, 2, 2, r)
    scratch += [
        ("normed", (n, d), BF), ("qt", (k, n), BF), ("kv", (4, n, 2 * k), BF), ("pt", (heads, 4, n, n), BF),
        ("scores", (heads, 4, n, n), F32), ("ctx", (n, k), BF), ("branch", (n, d), BF), ("parts", (zs - 1, m, d), BF),
        ("res", (m, d), F32), ("mi", (m, d), BF), ("slots", slots + (dh,), BF), ("slots_g", slots + (dh + 128,), BF),
        ("wu", (half, dh, units), BF), ("wd", (half, dh, units), BF), ("gp", hidden, BF),
        ("act", hidden, BF), ("gh", hidden, BF), ("x", received, BF), ("gx", received, BF),
        ("xt", (half, dh, slots_in), BF), ("gxt", (half, dh, slots_in), BF),
        ("rq", (sources, r, dh), BF), ("rg", (sources, r, dh + 128), BF), ("grads", (half, own_rows, dh + 128), BF),
        ("results", (half, own_rows, dh), BF), ("xg", (half, own_rows, dh), BF), ("xg_back", (half, own_rows, dh), BF),
        ("ret", (sources, r, dh), BF), ("ret_back", (sources, r, dh), BF),
        ("rb", (sources, r, dh), BF), ("rb_back", (sources, r, dh), BF),
        ("sorted_out", (n, d), BF), ("stat", (8, 128), F32), ("stat_in", (zs - 1, 8, 128), F32),
        ("stat_all", (sources, 8, 128), F32),
        ("ps", hidden, BF), ("pr", hidden, BF), ("pr_back", hidden, BF), ("rows", received, BF),
        ("rin", (half, zs - 1, own_rows, dh), BF), ("gm", (m, d), F32), ("gl", (m, 1), F32),
        ("sorted_gb", (n, d), BF), ("near", (2, n, 2 * k), F32), ("away", (2, n, 2 * k), F32),
        ("away_in", (2, n, 2 * k), F32), ("far_out", (n, 2 * k), BF), ("far_in", (n, 2 * k), BF), ("gn", (n, d), BF),
        ("gn_in", (zs - 1, m, d), BF), ("sorted_tg", (n, d), BF), ("dense", (fs, 2, 2) + piece, F32),
        ("dense_in", (fs, 2) + piece, F32), ("give", (others,) + piece, BF), ("taken", (others,) + piece, BF),
        ("sm", (TAB, 128), F32), ("sm_in", (zs - 1, TAB, 128), F32),
    ]
    for name, shape in (("hz", (zs - 1,)), ("wx", (2,)), ("kv", (3,)), ("d", (sources - 1,)), ("g", (sources - 1,)),
                        ("b", (sources - 1,)), ("c", (sources - 1,)), ("u", (sources - 1,)), ("o", (zs - 1,)),
                        ("t", (zs - 1,)), ("e", (4,)), ("ba", (zs - 1,)), ("bs", (zs - 1,)), ("bt", (zs - 1,)),
                        ("v", (zs - 1,)), ("k", (3,)), ("bg", (others,)),
                        ("one_a", (half, zs - 1)), ("one_x", (half,)), ("one_r", (half, zs - 1)),
                        ("two_a", (half, zs - 1)), ("two_x", (half,)), ("two_r", (half, zs - 1))):
        scratch += [(name + "_s", shape, dma), (name + "_r", shape, dma)]
    scratch += [("wsem", (6,), dma), ("l_s", (4,), dma)]
    names = [v[0] for v in ins] + [v[0] for v in outs] + [v[0] for v in scratch]
    results = pl.pallas_call(
        partial(layer_body, names, fs, zs, gather, rows),
        out_shape=[sds(v[1], v[2]) for v in outs],
        in_specs=[v[2] for v in ins],
        out_specs=[v[3] for v in outs],
        scratch_shapes=[dma(v[1]) if v[2] is dma else VMEM(v[1], v[2]) for v in scratch],
        compiler_params=params(1, 60),
        name="layer",
    )(*[v[1] for v in ins])
    xt, xt_x, act, act_x, gxt, gxt_x, gh, gh_x = results[:8]
    shapes = [sds((n, d), BF), sds((n, d), BF), sds((3, rows, k), F32), sds((k, rows), F32),
              sds((experts, rows), F32), sds((1, rows), F32), sds((1, rows), F32)]
    up, down, tokens_gradient, activations, mix_part, out_part, cen_part, g1, g2, balance, distill = finish(
        c, n * sources, (xt, gh, xt_x, gh_x, gxt, act, gxt_x, act_x), results[8:], shapes
    )
    return (
        activations[None],
        tokens_gradient[None],
        mix_part.transpose(1, 0, 2),
        out_part,
        g1.reshape(rows),
        g2.reshape(rows),
        cen_part,
        up.reshape(local_experts, width, units),
        down.reshape(local_experts, width, units).transpose(0, 2, 1),
        balance.reshape(()),
        distill.reshape(()),
    )


def solution(mesh):
    in_specs = (
        P("fsdp", "ctx", None),
        P(("fsdp", "ctx"), None, "tp"),
        P("tp", ("fsdp", "ctx")),
        P(("fsdp", "ctx")),
        P(("fsdp", "ctx")),
        P(None, ("fsdp", "ctx")),
        P("fsdp", "ctx", "tp"),
        P("fsdp", "tp", "ctx"),
        P("fsdp"),
        P("fsdp", "ctx", None),
        P("fsdp", "ctx"),
        P("fsdp", "ctx", None),
        P("fsdp", "ctx", None),
    )
    out_specs = (
        P("fsdp", "ctx", None),
        P("fsdp", "ctx", None),
        P(("fsdp", "ctx"), None, "tp"),
        P("tp", ("fsdp", "ctx")),
        P(("fsdp", "ctx")),
        P(("fsdp", "ctx")),
        P(None, ("fsdp", "ctx")),
        P("fsdp", "ctx", "tp"),
        P("fsdp", "tp", "ctx"),
        P(),
        P(),
    )
    return jax.shard_map(
        per_device, mesh=mesh, in_specs=in_specs, out_specs=out_specs, check_vma=False
    )
```

```python
from functools import partial
import math
from types import SimpleNamespace

import jax
import jax.numpy as jnp
from jax import lax
from jax.experimental import pallas as pl
from jax.experimental.pallas import tpu as pltpu
from jax.sharding import PartitionSpec as P

HD = 64
EPSILON = 1e-05
BF = jnp.bfloat16
F32 = jnp.float32
MESH = pl.DeviceIdType.MESH
TOP = lax.Precision.HIGHEST
VMEM = pltpu.VMEM
ANY = pl.ANY
CAP = 16
EXP = 32
TAB = 48


def _dot(a, b, ca, cb, precision=None):
    return lax.dot_general(
        a, b, (((ca,), (cb,)), ((), ())), preferred_element_type=F32, precision=precision
    )


def nn(a, b):
    return _dot(a, b, 1, 0)


def nt(a, b):
    return _dot(a, b, 1, 1)


def tn(a, b):
    return _dot(a, b, 0, 0)


def vspec():
    return pl.BlockSpec(memory_space=VMEM)


def sds(shape, dtype):
    return jax.ShapeDtypeStruct(shape, dtype)


def params(cid=None, mib=56):
    if cid is None:
        return pltpu.CompilerParams(vmem_limit_bytes=mib * 2**20)
    return pltpu.CompilerParams(
        vmem_limit_bytes=mib * 2**20, collective_id=cid, has_side_effects=True
    )


def iota(shape, dim):
    return lax.broadcasted_iota(jnp.int32, shape, dim)


def to_col(row):
    n = row.shape[1]
    return jnp.sum(jnp.where(iota((n, n), 0) == iota((n, n), 1), row, 0.0), axis=1, keepdims=True)


def to_row(col):
    n = col.shape[0]
    return jnp.sum(jnp.where(iota((n, n), 0) == iota((n, n), 1), col, 0.0), axis=0, keepdims=True)


def norm_parts(x):
    c = x - jnp.mean(x, axis=-1, keepdims=True)
    inv = lax.rsqrt(jnp.mean(c * c, axis=-1, keepdims=True) + EPSILON)
    return c * inv, inv


def norm_back(grad, xhat, inv, gain):
    gx = grad * gain
    return inv * (
        gx
        - jnp.mean(gx, axis=-1, keepdims=True)
        - xhat * jnp.mean(gx * xhat, axis=-1, keepdims=True)
    )


def log2(v):
    return v.bit_length() - 1


def shifted(v, by):
    return lax.shift_right_logical(v, by)


def owners(zs):
    return sorted(range(1, zs), key=lambda s: (-min(s, zs - s), s)) + [0]


class Route:
    def __init__(self, chosen, zs, z, width=0):
        n = chosen.shape[1]
        m = n // zs
        per = CAP // zs
        chosen = to_col(chosen.astype(F32))
        self.hot = (chosen == iota((n, EXP), 1).astype(F32)).astype(BF)
        lower = (iota((n, n), 1) < iota((n, n), 0)).astype(BF)
        rank = jnp.sum(nn(lower, self.hot) * self.hot.astype(F32), axis=1, keepdims=True)
        turn = jnp.floor(rank * (1.0 / zs))
        owner = rank - zs * turn
        owned = (owner == iota((n, zs), 1).astype(F32)).astype(BF)
        place = jnp.sum(nn(lower, owned) * owned.astype(F32), axis=1, keepdims=True)
        ahead = owner - lax.convert_element_type(z, F32)
        ahead = jnp.where(ahead < 0, ahead + zs, ahead)
        order = sum(jnp.where(ahead == step, float(k), 0.0) for k, step in enumerate(owners(zs)))
        self.at = order * m + place
        self.at_row = to_row(self.at)
        mine = iota((m, n), 0).astype(F32) + float((zs - 1) * m) == self.at_row
        self.mine = mine.astype(BF)
        self.mine_mask = mine
        self.slot = self.own_col(to_row(chosen * per + turn))
        self.own_hot = nn(self.mine, self.hot).astype(BF)
        self.slots = EXP * per
        self.n, self.m, self.width = n, m, width

    def positions(self):
        n = self.n
        return jnp.sum(jnp.where(self.at == iota((n, n), 1).astype(F32), iota((n, n), 0).astype(F32), 0.0), axis=0, keepdims=True)

    def own_col(self, row):
        return jnp.sum(jnp.where(self.mine_mask, row, 0.0), axis=1, keepdims=True)

    def own(self, rows):
        return nn(self.mine, rows)

    def sort(self, rows):
        return nn((iota((self.n, self.n), 0).astype(F32) == self.at_row).astype(BF), rows).astype(BF)

    def unsort(self, rows):
        return nn((iota((self.n, self.n), 1).astype(F32) == self.at).astype(BF), rows).astype(BF)

    def fill(self, rows, s_ref):
        place = (iota((self.slots, self.m), 0).astype(F32) == to_row(self.slot)).astype(BF)
        filled = nn(place, rows).astype(BF)
        fs, _, _, r, _ = s_ref.shape
        h = self.width // 2
        for f in range(fs):
            for c in range(2):
                at = (f * 2 + c) * r
                for y in range(2):
                    s_ref[f, y, c, :, :h] = filled[at : at + r, y * h : (y + 1) * h]
                    if rows.shape[1] > self.width:
                        s_ref[f, y, c, :, h:] = filled[at : at + r, self.width :]

    def collect(self, rb_ref):
        parts = []
        for f in range(rb_ref.shape[0] // 4):
            for c in range(2):
                parts.append(jnp.concatenate([rb_ref[f * 4 + c], rb_ref[f * 4 + 2 + c]], axis=1))
        rows = jnp.concatenate(parts, axis=0)
        place = (iota((self.m, self.slots), 1).astype(F32) == self.slot).astype(BF)
        return nn(place, rows)


def z_peers(zs):
    f, i, z = lax.axis_index("fsdp"), lax.axis_index("ctx"), lax.axis_index("tp")
    return [(f, i, lax.rem(z + s, zs)) for s in range(1, zs)]


def greet(peers):
    barrier = pltpu.get_barrier_semaphore()
    for peer in peers:
        pl.semaphore_signal(barrier, inc=1, device_id=peer, device_id_type=MESH)
    pl.semaphore_wait(barrier, len(peers))


def remote(src, dst, send, recv, peer):
    return pltpu.make_async_remote_copy(
        src_ref=src, dst_ref=dst, send_sem=send, recv_sem=recv, device_id=peer, device_id_type=MESH
    )


class Scatter:
    def __init__(self, zs, x_ref, parts, send, recv):
        self.zs, self.x_ref, self.parts, self.send, self.recv = zs, x_ref, parts, send, recv
        self.m = x_ref.shape[0] // zs
        self.copies = []

    def start(self, lo, hi):
        peers = z_peers(self.zs)
        for k, step in list(enumerate(owners(self.zs)))[lo:hi]:
            if step:
                cp = remote(
                    self.x_ref.at[pl.ds(k * self.m, self.m)], self.parts.at[step - 1],
                    self.send.at[step - 1], self.recv.at[step - 1], peers[step - 1],
                )
                cp.start()
                self.copies.append((step, cp))

    def finish(self):
        total = self.x_ref[pl.ds((self.zs - 1) * self.m, self.m), :].astype(F32)
        for step, cp in sorted(self.copies, key=lambda v: v[0]):
            cp.wait_recv()
            total = total + self.parts[step - 1].astype(F32)
        return total


def gather_z(zs, x_ref, m, send, recv):
    copies = []
    order = owners(zs)
    for s, peer in enumerate(z_peers(zs)):
        to = order.index(zs - s - 1)
        cp = remote(
            x_ref.at[pl.ds((zs - 1) * m, m)], x_ref.at[pl.ds(to * m, m)], send.at[s], recv.at[s], peer
        )
        cp.start()
        copies.append(cp)
    return copies


def span(at, n):
    return pl.ds(pl.multiple_of(at * n, n), n)


def group_peers(fs):
    f, i, z = lax.axis_index("fsdp"), lax.axis_index("ctx"), lax.axis_index("tp")
    y, c = lax.div(i, 2), lax.rem(i, 2)
    out = []
    for df in range(fs):
        for dy in range(2):
            for dc in range(2):
                if df or dy or dc:
                    fp = lax.rem(f + df, fs)
                    yp = y if dy == 0 else 1 - y
                    cp = c if dc == 0 else 1 - c
                    out.append((fp, yp, cp, (fp, yp * 2 + cp, z)))
    return out


class Attention:
    def __init__(self, R, mine, offsets, row0, positions):
        self.R = R
        self.k, self.n = R.qt.shape
        self.heads = self.k // HD
        self.offsets, self.row0 = offsets, row0
        self.query = positions + lax.convert_element_type(mine * self.n, F32)

    def lanes(self, half):
        return slice(half * (self.n // 2), (half + 1) * (self.n // 2))

    def scores(self, half, j):
        R, at, w = self.R, self.lanes(half), self.n // 2
        key = (iota((self.n, w), 0) + self.offsets[j] * self.n).astype(F32)
        col = to_col(R.valid[pl.ds(self.row0 + self.offsets[j], 1), :])
        query = self.query[:, at]
        prefix = lax.convert_element_type(R.prefix[0], F32)
        allowed = ((key <= query) | (key < prefix)) & ((col > 0.5) | (key == query))
        for h in range(self.heads):
            lo = h * HD
            scores = nn(R.kv[j, :, lo : lo + HD], R.qt[lo : lo + HD, at]) * (1.0 / math.sqrt(HD))
            R.scores[h, j, :, at] = jnp.where(allowed, scores, -1e30)

    def context(self, half):
        R, at, w, k = self.R, self.lanes(half), self.n // 2, self.k
        outs = []
        for h in range(self.heads):
            lo = h * HD
            top = jnp.max(R.scores[h, 0, :, at], axis=0, keepdims=True)
            for j in range(1, 4):
                top = jnp.maximum(top, jnp.max(R.scores[h, j, :, at], axis=0, keepdims=True))
            exps = [jnp.exp(R.scores[h, j, :, at] - top) for j in range(4)]
            share = 1.0 / sum(jnp.sum(e, axis=0, keepdims=True) for e in exps)
            acc = jnp.zeros((HD, w), F32)
            for j in range(4):
                weights = (exps[j] * share).astype(BF)
                R.pt[h, j, :, at] = weights
                acc = acc + tn(R.kv[j, :, k + lo : k + lo + HD], weights)
            outs.append(acc)
        return jnp.transpose(jnp.concatenate(outs, axis=0)).astype(BF)

    def back(self, half, gct, fresh, made):
        R, at, k = self.R, self.lanes(half), self.k
        scale = 1.0 / math.sqrt(HD)
        means, dqs = [], []
        for h in range(self.heads):
            lo = h * HD
            mean = 0.0
            for j in range(4):
                dp = nn(R.kv[j, :, k + lo : k + lo + HD], gct[lo : lo + HD, :])
                R.scores[h, j, :, at] = dp
                mean = mean + jnp.sum(R.pt[h, j, :, at].astype(F32) * dp, axis=0, keepdims=True)
            means.append(mean)
            dqs.append(jnp.zeros((HD, self.n // 2), F32))
        for j in (3, 1, 2, 0):
            target = R.near if j < 2 else R.away
            for h in range(self.heads):
                lo = h * HD
                w = R.pt[h, j, :, at]
                ds = (w.astype(F32) * (R.scores[h, j, :, at] - means[h])).astype(BF)
                dqs[h] = dqs[h] + tn(R.kv[j, :, lo : lo + HD], ds)
                dk = nt(ds, R.qt[lo : lo + HD, at]) * scale
                dv = nt(w, gct[lo : lo + HD, :])
                if not fresh:
                    dk = dk + target[j % 2, :, lo : lo + HD]
                    dv = dv + target[j % 2, :, k + lo : k + lo + HD]
                target[j % 2, :, lo : lo + HD] = dk
                target[j % 2, :, k + lo : k + lo + HD] = dv
            made(j)
        return jnp.concatenate(dqs, axis=0) * scale


def finish_body(scalars, c_ref, *refs):
    tg_in, act_in, mix_in, og_in, sm_in, stat_in = refs[8:14]
    up_ref, down_ref, tg_ref, act_ref, mix_ref, og_ref, cen_ref, g1_ref, g2_ref, bal_ref, dis_ref = refs[14:]
    c = c_ref[0]
    for out_ref, at in ((up_ref, 0), (down_ref, 4)):
        for core, (left_ref, right_ref) in ((c, refs[at : at + 2]), (1 - c, refs[at + 2 : at + 4])):
            for e in range(left_ref.shape[0]):
                out_ref[core, e] = nn(left_ref[e], right_ref[e])

    @pl.when(pl.program_id(0) == 0)
    def _():
        tg_ref[...] = tg_in[...]
        act_ref[...] = act_in[...]
        mix_ref[...] = mix_in[...]
        og_ref[...] = og_in[...]
        rows = cen_ref.shape[1]
        cen_ref[...] = sm_in[0:EXP, :rows]
        g1_ref[...] = sm_in[EXP : EXP + 1, :rows]
        g2_ref[...] = sm_in[EXP + 1 : EXP + 2, :rows]
        share = stat_in[0:1, :EXP] / scalars - 1.0 / EXP
        bal_ref[0, 0] = EXP * EXP * jnp.sum(share * stat_in[1:2, :EXP] / scalars)
        dis_ref[0, 0] = jnp.sum(stat_in[2:3, 0:1])


def finish(c, tokens, pairs, small, shapes):
    half, q, n = pairs[0].shape
    units = pairs[1].shape[2]
    step = 2 if half % 2 == 0 else 1
    block = lambda e, c_ref: (e, 0, 0)
    out = sds((2, half, q, units), F32)
    whole = lambda v: pl.BlockSpec(v.shape, lambda e, c_ref: (0,) * len(v.shape))
    smem = pl.BlockSpec(memory_space=pltpu.SMEM)
    scalar = sds((1, 1), F32)
    return pl.pallas_call(
        partial(finish_body, float(tokens)),
        grid_spec=pltpu.PrefetchScalarGridSpec(
            num_scalar_prefetch=1,
            grid=(half // step,),
            in_specs=[pl.BlockSpec((step, q, n), block), pl.BlockSpec((step, n, units), block)] * 4
            + [whole(v) for v in small],
            out_specs=[pl.BlockSpec((2, step, q, units), lambda e, c_ref: (0, e, 0, 0))] * 2
            + [whole(v) for v in shapes] + [smem] * 2,
        ),
        out_shape=[out, out] + shapes + [scalar] * 2,
        compiler_params=params(),
        name="finish",
    )(c.reshape(1), *pairs, *small)


def whereabouts():
    f, i, z = lax.axis_index("fsdp"), lax.axis_index("ctx"), lax.axis_index("tp")
    return f, i, z, lax.div(i, 2), lax.rem(i, 2)


def reorder(sources, half, per, inverse):
    n = sources * half * per
    i, o = iota((n, n), 1), iota((n, n), 0)
    if inverse:
        i, o = o, i
    ls, lh, lp = log2(sources), log2(half), log2(per)
    slot = o & (per - 1)
    source = shifted(o, lp) & (sources - 1)
    expert = shifted(o, lp + ls)
    return (i == source * (half * per) + expert * per + slot).astype(BF)


class Pass:
    def __init__(self, back, zs, w_in, w_out, xg, x_ref, ps, pr, h_ref, gp_ref, res, rin, sems):
        self.back, self.zs, self.w_in, self.w_out = back, zs, w_in, w_out
        self.xg, self.x_ref, self.ps, self.pr = xg, x_ref, ps, pr
        self.h_ref, self.gp_ref, self.res, self.rin = h_ref, gp_ref, res, rin
        self.a_s, self.a_r, self.x_s, self.x_r, self.r_s, self.r_r = sems
        f, i, z, y, c = whereabouts()
        self.z = z
        self.m = xg.shape[1]
        self.across = (f, (1 - y) * 2 + c, z)
        self.peers = z_peers(zs)

    def share(self, e, s):
        to = self.x_ref.at[e, span(self.z, self.m), :]
        return remote(self.xg.at[e], to, self.a_s.at[e, s], self.a_r.at[e, s], self.peers[s])

    def cross(self, e):
        return remote(self.ps.at[e], self.pr.at[e], self.x_s.at[e], self.x_r.at[e], self.across)

    def scatter(self, e, s):
        to = lax.rem(self.z + s + 1, self.zs)
        return remote(
            self.res.at[e, span(to, self.m), :], self.rin.at[e, s], self.r_s.at[e, s], self.r_r.at[e, s], self.peers[s]
        )

    def spread(self, e, rows):
        self.xg[e] = rows
        for s in range(self.zs - 1):
            self.share(e, s).start()
        self.x_ref[e, span(self.z, self.m), :] = rows

    def first(self, e):
        for s in range(self.zs - 1):
            self.share(e, s).wait_recv()
        self.ps[e] = nn(self.x_ref[e], self.w_in[e]).astype(BF)

    def second(self, e):
        self.cross(e).wait_recv()
        total = self.ps[e].astype(F32) + self.pr[e].astype(F32)
        if self.back:
            self.h_ref[e] = (total * self.gp_ref[e].astype(F32)).astype(BF)
        else:
            phi = 0.5 * (1.0 + lax.erf(total * math.sqrt(0.5)))
            self.h_ref[e] = (total * phi).astype(BF)
            bell = jnp.exp(-0.5 * total * total) * (1.0 / math.sqrt(2.0 * math.pi))
            self.gp_ref[e] = (phi + total * bell).astype(BF)
        self.res[e] = nt(self.h_ref[e], self.w_out[e]).astype(BF)
        for s in range(self.zs - 1):
            self.scatter(e, s).start()

    def total(self, e):
        total = self.res[e, span(self.z, self.m), :].astype(F32)
        for s in range(self.zs - 1):
            self.scatter(e, s).wait_recv()
            total = total + self.rin[e, s].astype(F32)
        return total.astype(BF)

    def settle(self, e):
        self.cross(e).wait_send()
        for s in range(self.zs - 1):
            self.share(e, s).wait_send()
            self.scatter(e, s).wait_send()


def give_back(fs, total, ret, rb_ref, own_sem, send, recv):
    f, i, z, y, c = whereabouts()
    me = f * 4 + i
    sources, r, dh = ret.shape
    half = total.shape[0]
    rows = total[...].reshape(sources * r, dh)
    ret[...] = nn(reorder(sources, half, r // half, True), rows).astype(BF).reshape(sources, r, dh)
    keep = pltpu.make_async_copy(ret.at[me], rb_ref.at[me], own_sem)
    keep.start()
    copies = []
    for k, (fp, yp, cp_, peer) in enumerate(group_peers(fs)):
        cp = remote(ret.at[fp * 4 + yp * 2 + cp_], rb_ref.at[me], send.at[k], recv.at[k], peer)
        cp.start()
        copies.append(cp)
    return keep, copies


def arrived(given):
    keep, copies = given
    keep.wait()
    for cp in copies:
        cp.wait_recv()


def head(R, fs, zs, gather):
    f, i, z, y, c = whereabouts()
    me = f * 4 + i
    half, width = R.wu.shape[0], R.up.shape[1]
    k = R.qt.shape[0]
    d = R.tok.shape[1]
    sibling = (f, y * 2 + 1 - c, z)
    across = (f, (1 - y) * 2 + c, z)
    same = same_core(fs)
    waits = []
    mine = pl.ds(c * half, half)
    theirs = pl.ds((1 - c) * half, half)
    own = pl.ds(pl.multiple_of(c * width, 64), width)
    loads = [
        pltpu.make_async_copy(R.up.at[mine], R.wu.at[:, own, :], R.wsem.at[0]),
        pltpu.make_async_copy(R.dn.at[mine], R.wd.at[:, own, :], R.wsem.at[1]),
    ]
    swaps = [
        remote(R.up.at[theirs], R.wu.at[:, own, :], R.wx_s.at[0], R.wx_r.at[0], sibling),
        remote(R.dn.at[theirs], R.wd.at[:, own, :], R.wx_s.at[1], R.wx_r.at[1], sibling),
    ]
    if gather:
        rows = R.mix.shape[1]
        R.small[...] = jnp.zeros(R.small.shape, F32)
        R.small[0:EXP, :rows] = R.cent[...].astype(F32)
        R.small[EXP : EXP + 1, :rows] = R.gain1[...].astype(F32)
        R.small[EXP + 1 : EXP + 2, :rows] = R.gain2[...].astype(F32)
        R.small[EXP + 2 : EXP + 3, :] = R.here[...].astype(F32)
        R.small_all[me] = R.small[...].astype(BF)
        R.w3[:, span(me, rows), :] = R.mix[...]
        R.wo[span(me, rows), :] = jnp.transpose(R.ow[...].astype(F32)).astype(BF)
    greet([p[3] for p in group_peers(fs)] + z_peers(zs))
    for cp in loads:
        cp.start()
    xhat, _ = norm_parts(R.tok[...].astype(F32))
    if gather:

        def places(at):
            rows_ = span(at, rows)
            return [R.w3.at[1:3, rows_, :], R.small_all.at[at], R.w3.at[0:1, rows_, :], R.wo.at[rows_, :]]

        sends = {}
        for m, ref in enumerate(places(me)):
            for n_, (_, _, peer, _) in enumerate(same):
                cp = remote(ref, ref, R.p_s.at[n_, m], R.p_r.at[n_, m], peer)
                cp.start()
                sends[n_, m] = cp
        relays = {}

        def relay(n_, m, at):
            ref = places(at)[m]
            cp = remote(ref, ref, R.q_s.at[n_, m], R.q_r.at[n_, m], sibling)
            cp.start()
            relays[n_, m] = cp

        def pass_on(some):
            for n_, (_, _, _, at) in enumerate(same):
                for m in some:
                    sends[n_, m].wait_recv()
                    relay(n_ + 1, m, at)

        for m in range(4):
            relay(0, m, me)
        pass_on((0, 1))
        for n_ in range(len(same) + 1):
            for m in (0, 1):
                relays[n_, m].wait_recv()
        R.table[...] = jnp.concatenate([R.small_all[s, :, :rows] for s in range(fs * 4)], axis=1)
        for s in range(fs * 4):
            R.valid[s : s + 1, :] = R.small_all[s, EXP + 2 : EXP + 3, :].astype(F32)
    normed = (xhat * R.table[EXP : EXP + 1, :].astype(F32)).astype(BF)
    R.normed[...] = normed
    R.kv[0, :, :k] = nn(normed, R.w3[1]).astype(BF)
    R.kv[0, :, k:] = nn(normed, R.w3[2]).astype(BF)
    far = remote(R.kv.at[0], R.kv.at[1], R.kv_s.at[0], R.kv_r.at[0], across)
    sib = remote(R.kv.at[0], R.kv.at[2], R.kv_s.at[1], R.kv_r.at[1], sibling)
    far.start()
    sib.start()
    if gather:
        pass_on((2, 3))
        for n_ in range(len(same) + 1):
            for m in (2, 3):
                relays[n_, m].wait_recv()
        waits += list(sends.values()) + list(relays.values())
    route = Route(R.chosen[...], zs, z, d)
    R.qt[...] = jnp.transpose(route.sort(nn(normed, R.w3[0]).astype(BF)).astype(F32)).astype(BF)
    teacher, cotangent = route.own(R.tea[...]), route.own(R.cot[...])
    own_tokens = route.own(R.tok[...])
    own_valid = route.own_col(R.valid[pl.ds(me, 1), :])
    scale = 1.0 / (jnp.sum(R.valid[...]) * d)
    sib.wait_recv()
    offsets = [i, (1 - y) * 2 + c, y * 2 + 1 - c, (1 - y) * 2 + 1 - c]
    attention = Attention(R, i, offsets, f * 4, route.positions())
    for j in (0, 2):
        for half_ in range(2):
            attention.scores(half_, j)
    far.wait_recv()
    last = remote(R.kv.at[1], R.kv.at[3], R.kv_s.at[2], R.kv_r.at[2], sibling)
    last.start()
    for swap in swaps:
        swap.start()
    attention.scores(0, 1)
    attention.scores(1, 1)
    last.wait_recv()
    sums = Scatter(zs, R.branch, R.parts, R.hz_s, R.hz_r)
    n = R.tok.shape[0]
    for half_ in range(2):
        attention.scores(half_, 3)
        rows_ = pl.ds(half_ * (n // 2), n // 2)
        ctx = attention.context(half_)
        R.ctx[rows_, :] = ctx
        R.branch[rows_, :] = nt(ctx, R.wo[...]).astype(BF)
        sums.start(half_ * (zs // 2), (half_ + 1) * (zs // 2))
    residual = own_tokens + sums.finish()
    R.res[...] = residual
    xhat, _ = norm_parts(residual)
    mixed_in = (xhat * R.table[EXP + 1 : EXP + 2, :].astype(F32)).astype(BF)
    R.mi[...] = mixed_in
    logit = jnp.sum(mixed_in.astype(F32) * nn(route.own_hot, R.table[0:EXP, :]), axis=-1, keepdims=True)
    gate = jax.nn.sigmoid(logit)
    route.fill(mixed_in, R.slots)
    sends = dispatch(fs, R.slots, R.rq, R.d_s, R.d_r, R.wsem.at[2])
    weight = 2.0 * own_valid * scale
    known = gate * (cotangent + weight * (residual - teacher))
    slope = jnp.broadcast_to(gate * gate * weight, (known.shape[0], 128))
    route.fill(jnp.concatenate([known, slope], axis=1).astype(BF), R.slots_g)
    sends_g = dispatch(fs, R.slots_g, R.rg, R.g_s, R.g_r, R.wsem.at[3])
    waits += swaps + [v[1] for v in sums.copies] + [far, sib, last]
    return SimpleNamespace(route=route, attention=attention, own_tokens=own_tokens, sends=sends, sends_g=sends_g, gate=gate, teacher=teacher, cotangent=cotangent, valid=own_valid, scale=scale,
                           loads=loads, swaps=swaps, waits=waits)


def dispatch(fs, src, dst, send, recv, own_sem):
    f, i, z, y, c = whereabouts()
    me = f * 4 + i
    copies = [pltpu.make_async_copy(src.at[f, y, c], dst.at[me], own_sem)]
    for k, (fp, yp, cp_, peer) in enumerate(group_peers(fs)):
        copies.append(remote(src.at[fp, yp, cp_], dst.at[me], send.at[k], recv.at[k], peer))
    for cp in copies:
        cp.start()
    return copies


def same_core(fs):
    f, i, z, y, c = whereabouts()
    out = []
    for df in range(fs):
        for dy in range(2):
            if df or dy:
                fp, fm = lax.rem(f + df, fs), lax.rem(f - df + fs, fs)
                yp = y if dy == 0 else 1 - y
                out.append((fp, yp, (fp, yp * 2 + c, z), fm * 4 + yp * 2 + c))
    return out


def middle(R, S, fs, zs):
    f, i, z, y, c = whereabouts()
    me = f * 4 + i
    half, width = R.wu.shape[0], R.up.shape[1]
    sources, r, dh = R.rq.shape
    m = sources * r // half
    group = group_peers(fs)
    sibling = (f, y * 2 + 1 - c, z)
    own = pl.ds(pl.multiple_of(c * width, 64), width)
    other = pl.ds(pl.multiple_of((1 - c) * width, 64), width)
    sems = [[getattr(R, p + n) for n in ("a_s", "a_r", "x_s", "x_r", "r_s", "r_r")] for p in ("one_", "two_")]
    one = Pass(False, zs, R.wu, R.wd, R.xg, R.x, R.ps, R.pr, R.act, R.gp, R.rows, R.rin, sems[0])
    two = Pass(True, zs, R.wd, R.wu, R.xg_back, R.gx, R.ps, R.pr_back, R.gh, R.gp, R.rows, R.rin, sems[1])
    order = reorder(sources, half, r // half, False)
    exports = []

    def export(n, own_src, own_dst, src, dst):
        keep = pltpu.make_async_copy(own_src, own_dst, R.l_s.at[n])
        give = remote(src, dst, R.e_s.at[n], R.e_r.at[n], sibling)
        keep.start()
        give.start()
        exports.append((keep, give))

    for cp in S.loads:
        cp.wait()
    for cp in S.swaps:
        cp.wait_recv()
    arrived((S.sends[0], S.sends[1:]))
    rows = nn(order, R.rq[...].reshape(sources * r, dh)).astype(BF).reshape(half, m, dh)
    for e in range(half):
        one.spread(e, rows[e])

    @pl.loop(0, half)
    def _(e):
        one.first(e)
        one.cross(e).start()

    @pl.loop(0, half)
    def _(e):
        R.xt[e] = jnp.transpose(R.x[e])

    arrived((S.sends_g[0], S.sends_g[1:]))
    R.grads[...] = nn(order, R.rg[...].reshape(sources * r, dh + 128)).astype(BF).reshape(half, m, dh + 128)
    export(0, R.xt.at[:, own, :], R.xt_own, R.xt.at[:, other, :], R.xt_sib)

    def turn(e):
        result = one.total(e)
        R.results[e] = result
        scale = R.grads[e, :, dh:].astype(F32)[:, :1]
        two.spread(e, (R.grads[e, :, :dh].astype(F32) + scale * result.astype(F32)).astype(BF))

    lag, lag2 = 2, 4
    start = max(half, lag2 + 1)
    ahead = 3

    def step(t, fixed=True):
        if not fixed or t < half:
            one.second(t)
        if fixed and t - start >= 0 and t - start < half:
            two.second(t - start)
        if not fixed or 0 <= t - lag < half:
            turn(t - lag)
        if not fixed or 0 <= t - lag2 < half:
            one.settle(t - lag2)
            two.first(t - lag2)

    begun = 0
    t = 0
    while t < lag2:
        step(t)
        t += 1
    safe = max(t, start - ahead)
    if safe > t and half > t:
        stop = min(safe, half)

        @pl.loop(t, stop)
        def _(k):
            step(k, False)

        t = stop
    given = None
    pending = []

    def report():
        returned = S.route.collect(R.rb)
        n, d = returned.shape
        mixed = R.res[...] + S.gate * returned
        diff = mixed - S.teacher
        weighted = S.valid * diff
        grad = S.cotangent + 2.0 * weighted * S.scale
        R.sorted_out[pl.ds((zs - 1) * n, n), :] = mixed.astype(BF)
        pending.extend(gather_z(zs, R.sorted_out, n, R.o_s, R.o_r))
        hot = S.route.own_hot.astype(F32)
        R.stat[...] = jnp.zeros_like(R.stat)
        R.stat[0:1, 0:EXP] = jnp.sum(hot, axis=0, keepdims=True)
        R.stat[1:2, 0:EXP] = jnp.sum(hot * S.gate, axis=0, keepdims=True)
        R.stat[2:3, :] = jnp.broadcast_to(jnp.sum(weighted * diff * S.scale), (1, 128))
        for s, peer in enumerate(z_peers(zs)):
            cp = remote(R.stat, R.stat_in.at[s], R.t_s.at[s], R.t_r.at[s], peer)
            cp.start()
            pending.append(cp)
        R.gm[...] = grad
        grad_gate = jnp.sum(grad * returned, axis=-1, keepdims=True)
        R.gl[...] = grad_gate * S.gate * (1.0 - S.gate)

    def publish():
        total = R.stat[...]
        for s, cp in enumerate(pending[zs - 1 :]):
            cp.wait_recv()
            total = total + R.stat_in[s]
        R.stat_all[me] = total
        for k, (_, _, _, peer) in enumerate(group):
            cp = remote(R.stat_all.at[me], R.stat_all.at[me], R.u_s.at[k], R.u_r.at[k], peer)
            cp.start()
            pending.append(cp)

    while t < start + half + 1:
        step(t)
        if given is None and t - lag >= half - 1:
            given = give_back(fs, R.results, R.ret, R.rb, R.wsem.at[4], R.b_s, R.b_r)
            export(1, R.act, R.act_own, R.act, R.act_sib)
        while begun < half and begun <= t - start + ahead and begun <= t - lag2:
            two.cross(begun).start()
            begun += 1
        if 0 <= t - 1 - start < half:
            R.xg[t - 1 - start] = two.total(t - 1 - start)
        if t == max(start + half - 4, start + 1) or (half == 1 and t == start):

            @pl.loop(0, half)
            def _(e):
                R.gxt[e] = jnp.transpose(R.gx[e])

        if t == start + half - 2 or (half == 1 and t == start):
            arrived(given)
            report()
        if t == start + half - 1:
            publish()
        t += 1
    given_back = give_back(fs, R.xg, R.ret_back, R.rb_back, R.wsem.at[5], R.c_s, R.c_r)
    export(2, R.gxt.at[:, own, :], R.gxt_own, R.gxt.at[:, other, :], R.gxt_sib)
    export(3, R.gh, R.gh_own, R.gh, R.gh_sib)
    S.pending, S.exports = pending, exports
    S.waits += pending[: 2 * (zs - 1)] + S.sends[1:] + S.sends_g[1:] + given[1] + given_back[1]
    S.two = two
    arrived(given_back)
    return S.route.collect(R.rb_back)


def back(R, S, grad_back, fs, zs, rows):
    f, i, z, y, c = whereabouts()
    sibling = (f, y * 2 + 1 - c, z)
    across = (f, (1 - y) * 2 + c, z)
    same = same_core(fs)
    route = S.route
    k = R.qt.shape[0]
    gl = R.gl[...]
    grad_in = grad_back + gl * nn(route.own_hot, R.table[0:EXP, :])
    m, d = grad_in.shape
    xhat, inv = norm_parts(R.res[...])
    grad = R.gm[...] + norm_back(grad_in, xhat, inv, R.table[EXP + 1 : EXP + 2, :].astype(F32))
    R.sorted_gb[pl.ds((zs - 1) * m, m), :] = grad.astype(BF)
    gathers = gather_z(zs, R.sorted_gb, m, R.ba_s, R.ba_r)
    g2 = jnp.sum(grad_in * xhat, axis=0, keepdims=True)
    cg = _dot(route.own_hot.astype(F32) * gl, R.mi[...].astype(F32), 0, 0, TOP)
    all_tok = norm_parts(route.sort(R.tok[...]).astype(F32))[0]
    own_tok, own_inv = norm_parts(S.own_tokens)
    for cp in S.pending[: zs - 1]:
        cp.wait_recv()
    R.out[...] = route.unsort(R.sorted_out[...])
    for cp in S.pending[2 * (zs - 1) :]:
        cp.wait()
    total = R.stat_all[0]
    for n in range(1, fs * 4):
        total = total + R.stat_all[n]
    R.stat_out[...] = total
    n = R.tok.shape[0]
    swaps = [remote(R.away.at[j], R.away_in.at[j], R.k_s.at[j], R.k_r.at[j], sibling) for j in range(2)]
    cross = remote(R.far_out, R.far_in, R.k_s.at[2], R.k_r.at[2], across)

    def nothing(j):
        pass

    def made(j):
        if j == 3:
            swaps[1].start()
        if j == 1:
            swaps[1].wait_recv()
            R.far_out[...] = (R.near[1] + R.away_in[1]).astype(BF)
            cross.start()
        if j == 2:
            swaps[0].start()

    dqs = {}
    for half, steps in ((1, (0,)), (0, range(1, zs - 1))):
        for s in steps:
            gathers[s].wait_recv()
        gct = jnp.transpose(nn(R.sorted_gb[pl.ds(half * (n // 2), n // 2), :], R.wo[...])).astype(BF)
        dqs[half] = S.attention.back(half, gct, half == 1, nothing if half == 1 else made)
    dq = jnp.transpose(jnp.concatenate([dqs[0], dqs[1]], axis=1)).astype(BF)
    normed = R.normed[...]
    gq = nt(dq, R.w3[0])
    mg = [tn(normed, route.unsort(dq)), None, None]
    og = tn(R.sorted_gb[...], R.ctx[...])
    swaps[0].wait_recv()
    near = R.near[0] + R.away_in[0]
    cross.wait_recv()
    kvg = (near + R.far_in[...].astype(F32)).astype(BF)
    kvs = route.sort(kvg)
    partial_normed = gq + nt(kvs[:, :k], R.w3[1]) + nt(kvs[:, k:], R.w3[2])
    R.gn[...] = partial_normed.astype(BF)
    scat = Scatter(zs, R.gn, R.gn_in, R.bs_s, R.bs_r)
    scat.start(0, zs)
    mg[1] = tn(normed, kvg[:, :k])
    mg[2] = tn(normed, kvg[:, k:])
    g1 = jnp.sum(partial_normed * all_tok, axis=0, keepdims=True)
    dense = R.dense
    last = dense.shape[3] - TAB
    small = jnp.concatenate([cg, g1, g2, jnp.zeros((TAB - EXP - 2, d), F32)], axis=0)
    for s in range(4 * fs):
        at = (s // 4, s % 4 // 2, s % 2)
        lo = s * rows
        for j in range(3):
            dense[at[0], at[1], at[2], 0:rows, j * k : (j + 1) * k] = mg[j][lo : lo + rows, :]
        dense[at[0], at[1], at[2], 0:rows, 3 * k : 4 * k] = og[lo : lo + rows, :]
        dense[at[0], at[1], at[2], last : last + TAB, 0:rows] = small[:, lo : lo + rows]
    pair = remote(dense.at[:, :, 1 - c], R.dense_in, R.k_s.at[3], R.k_r.at[3], sibling)
    pair.start()
    pair.wait_recv()
    shares = []
    for s, (fp, yp, peer, _) in enumerate(same):
        R.give[s] = (dense[fp, yp, c] + R.dense_in[fp, yp]).astype(BF)
        cp = remote(R.give.at[s], R.taken.at[s], R.bg_s.at[s], R.bg_r.at[s], peer)
        cp.start()
        shares.append(cp)
    total = scat.finish()
    tg = grad + norm_back(total, own_tok, own_inv, R.table[EXP : EXP + 1, :].astype(F32))
    R.sorted_tg[pl.ds((zs - 1) * m, m), :] = tg.astype(BF)
    ends = gather_z(zs, R.sorted_tg, m, R.bt_s, R.bt_r)
    kept = dense[f, y, c] + R.dense_in[f, y]
    for s, cp in enumerate(shares):
        cp.wait_recv()
        kept = kept + R.taken[s].astype(F32)
    R.sm[...] = kept[last:, :128]
    smalls = []
    for s, peer in enumerate(z_peers(zs)):
        cp = remote(R.sm, R.sm_in.at[s], R.v_s.at[s], R.v_r.at[s], peer)
        cp.start()
        smalls.append(cp)
    for j in range(3):
        R.mix_out[j] = kept[:rows, j * k : (j + 1) * k]
    R.og_out[...] = jnp.transpose(kept[:rows, 3 * k :])
    for keep, give in S.exports:
        keep.wait()
        give.wait()
    for cp in ends:
        cp.wait_recv()
    R.tg_out[...] = route.unsort(R.sorted_tg[...])
    total = R.sm[...]
    for s, cp in enumerate(smalls):
        cp.wait_recv()
        total = total + R.sm_in[s]
    R.sm_out[...] = total
    for cp in S.waits + gathers + swaps + [cross, pair] + [v[1] for v in scat.copies] + shares + ends + smalls:
        cp.wait_send()

    @pl.loop(0, R.wu.shape[0])
    def _(e):
        S.two.settle(e)


def layer_body(names, fs, zs, gather, rows, *refs):
    R = SimpleNamespace(**dict(zip(names, refs)))
    S = head(R, fs, zs, gather)
    grad_back = middle(R, S, fs, zs)
    back(R, S, grad_back, fs, zs, rows)


def per_device(tokens, mixing_weight, output_weight, first_gain, second_gain, centroids, expert_up,
               expert_down, prefix_length, assignment, validity, teacher, cotangent):
    fs, zs = lax.axis_size("fsdp"), lax.axis_size("tp")
    c = lax.rem(lax.axis_index("ctx"), 2)
    n, d = tokens.shape[1], tokens.shape[2]
    rows, k = mixing_weight.shape[0], mixing_weight.shape[2]
    local_experts, width, units = expert_up.shape
    half = local_experts // 2
    experts = centroids.shape[0]
    sources = fs * 4
    heads = k // HD
    dma = pltpu.SemaphoreType.DMA
    per = CAP // zs
    m = n // zs
    r = half * per
    dh = d // 2
    own_rows = sources * per
    slots_in = sources * CAP
    others = 2 * fs - 1
    smem = pl.BlockSpec(memory_space=pltpu.SMEM)
    anyspec = pl.BlockSpec(memory_space=ANY)

    mixing = mixing_weight.transpose(1, 0, 2)
    ins = [("prefix", prefix_length, smem), ("tok", tokens[0], vspec()), ("chosen", assignment.reshape(1, n), vspec()),
           ("tea", teacher[0], vspec()), ("cot", cotangent[0], vspec()),
           ("up", expert_up, anyspec), ("dn", expert_down.transpose(0, 2, 1), anyspec)]
    scratch = []
    weights = [("w3", (3, d, k), BF), ("wo", (d, k), BF), ("table", (TAB, d), BF), ("valid", (sources, n), F32)]
    gather = rows % 16 == 0
    if gather:
        ins += [("mix", mixing, vspec()), ("ow", output_weight, vspec()), ("cent", centroids, vspec()),
                ("gain1", first_gain.reshape(1, rows), vspec()), ("gain2", second_gain.reshape(1, rows), vspec()),
                ("here", validity, vspec())]
        scratch += weights
        scratch += [("small", (TAB, n), F32), ("small_all", (sources, TAB, n), BF)]
        scratch += [(v, (others + w, 4), dma) for v, w in (("p_s", 0), ("p_r", 0), ("q_s", 1), ("q_r", 1))]
    else:
        small = jnp.concatenate(
            [
                jnp.pad(jnp.concatenate([centroids, first_gain[None], second_gain[None]]), ((0, 0), (0, n - rows))),
                validity.astype(BF),
                jnp.zeros((TAB - experts - 3, n), BF),
            ]
        )
        everyone = ("fsdp", "ctx")
        table = lax.all_gather(small, everyone, axis=0)
        full = (
            lax.all_gather(mixing, everyone, axis=1, tiled=True),
            lax.all_gather(output_weight, everyone, axis=1, tiled=True).T,
            table[:, :, :rows].transpose(1, 0, 2).reshape(TAB, d),
            table[:, experts + 2, :].astype(F32),
        )
        ins += [(w[0], v, vspec()) for w, v in zip(weights, full)]
    hidden, received, left = (half, slots_in, units), (half, slots_in, dh), (half, width, slots_in)
    outs = [(name, shape, BF, anyspec) for name, shape in (
        ("xt_own", left), ("xt_sib", left), ("act_own", hidden), ("act_sib", hidden),
        ("gxt_own", left), ("gxt_sib", left), ("gh_own", hidden), ("gh_sib", hidden))]
    outs += [("tg_out", (n, d), BF, vspec()), ("out", (n, d), BF, vspec()), ("mix_out", (3, rows, k), F32, vspec()),
             ("og_out", (k, rows), F32, vspec()), ("sm_out", (TAB, 128), F32, vspec()), ("stat_out", (8, 128), F32, vspec())]
    piece = (rows + (-rows % 16) + TAB, 4 * k)
    slots = (fs, 2, 2, r)
    scratch += [
        ("normed", (n, d), BF), ("qt", (k, n), BF), ("kv", (4, n, 2 * k), BF), ("pt", (heads, 4, n, n), BF),
        ("scores", (heads, 4, n, n), F32), ("ctx", (n, k), BF), ("branch", (n, d), BF), ("parts", (zs - 1, m, d), BF),
        ("res", (m, d), F32), ("mi", (m, d), BF), ("slots", slots + (dh,), BF), ("slots_g", slots + (dh + 128,), BF),
        ("wu", (half, dh, units), BF), ("wd", (half, dh, units), BF), ("gp", hidden, BF),
        ("act", hidden, BF), ("gh", hidden, BF), ("x", received, BF), ("gx", received, BF),
        ("xt", (half, dh, slots_in), BF), ("gxt", (half, dh, slots_in), BF),
        ("rq", (sources, r, dh), BF), ("rg", (sources, r, dh + 128), BF), ("grads", (half, own_rows, dh + 128), BF),
        ("results", (half, own_rows, dh), BF), ("xg", (half, own_rows, dh), BF), ("xg_back", (half, own_rows, dh), BF),
        ("ret", (sources, r, dh), BF), ("ret_back", (sources, r, dh), BF),
        ("rb", (sources, r, dh), BF), ("rb_back", (sources, r, dh), BF),
        ("sorted_out", (n, d), BF), ("stat", (8, 128), F32), ("stat_in", (zs - 1, 8, 128), F32),
        ("stat_all", (sources, 8, 128), F32),
        ("ps", hidden, BF), ("pr", hidden, BF), ("pr_back", hidden, BF), ("rows", received, BF),
        ("rin", (half, zs - 1, own_rows, dh), BF), ("gm", (m, d), F32), ("gl", (m, 1), F32),
        ("sorted_gb", (n, d), BF), ("near", (2, n, 2 * k), F32), ("away", (2, n, 2 * k), F32),
        ("away_in", (2, n, 2 * k), F32), ("far_out", (n, 2 * k), BF), ("far_in", (n, 2 * k), BF), ("gn", (n, d), BF),
        ("gn_in", (zs - 1, m, d), BF), ("sorted_tg", (n, d), BF), ("dense", (fs, 2, 2) + piece, F32),
        ("dense_in", (fs, 2) + piece, F32), ("give", (others,) + piece, BF), ("taken", (others,) + piece, BF),
        ("sm", (TAB, 128), F32), ("sm_in", (zs - 1, TAB, 128), F32),
    ]
    for name, shape in (("hz", (zs - 1,)), ("wx", (2,)), ("kv", (3,)), ("d", (sources - 1,)), ("g", (sources - 1,)),
                        ("b", (sources - 1,)), ("c", (sources - 1,)), ("u", (sources - 1,)), ("o", (zs - 1,)),
                        ("t", (zs - 1,)), ("e", (4,)), ("ba", (zs - 1,)), ("bs", (zs - 1,)), ("bt", (zs - 1,)),
                        ("v", (zs - 1,)), ("k", (4,)), ("bg", (others,)),
                        ("one_a", (half, zs - 1)), ("one_x", (half,)), ("one_r", (half, zs - 1)),
                        ("two_a", (half, zs - 1)), ("two_x", (half,)), ("two_r", (half, zs - 1))):
        scratch += [(name + "_s", shape, dma), (name + "_r", shape, dma)]
    scratch += [("wsem", (6,), dma), ("l_s", (4,), dma)]
    names = [v[0] for v in ins] + [v[0] for v in outs] + [v[0] for v in scratch]
    results = pl.pallas_call(
        partial(layer_body, names, fs, zs, gather, rows),
        out_shape=[sds(v[1], v[2]) for v in outs],
        in_specs=[v[2] for v in ins],
        out_specs=[v[3] for v in outs],
        scratch_shapes=[dma(v[1]) if v[2] is dma else VMEM(v[1], v[2]) for v in scratch],
        compiler_params=params(1, 60),
        name="layer",
    )(*[v[1] for v in ins])
    xt, xt_x, act, act_x, gxt, gxt_x, gh, gh_x = results[:8]
    shapes = [sds((n, d), BF), sds((n, d), BF), sds((3, rows, k), F32), sds((k, rows), F32),
              sds((experts, rows), F32), sds((1, rows), F32), sds((1, rows), F32)]
    up, down, tokens_gradient, activations, mix_part, out_part, cen_part, g1, g2, balance, distill = finish(
        c, n * sources, (xt, gh, xt_x, gh_x, gxt, act, gxt_x, act_x), results[8:], shapes
    )
    return (
        activations[None],
        tokens_gradient[None],
        mix_part.transpose(1, 0, 2),
        out_part,
        g1.reshape(rows),
        g2.reshape(rows),
        cen_part,
        up.reshape(local_experts, width, units),
        down.reshape(local_experts, width, units).transpose(0, 2, 1),
        balance.reshape(()),
        distill.reshape(()),
    )


def solution(mesh):
    in_specs = (
        P("fsdp", "ctx", None),
        P(("fsdp", "ctx"), None, "tp"),
        P("tp", ("fsdp", "ctx")),
        P(("fsdp", "ctx")),
        P(("fsdp", "ctx")),
        P(None, ("fsdp", "ctx")),
        P("fsdp", "ctx", "tp"),
        P("fsdp", "tp", "ctx"),
        P("fsdp"),
        P("fsdp", "ctx", None),
        P("fsdp", "ctx"),
        P("fsdp", "ctx", None),
        P("fsdp", "ctx", None),
    )
    out_specs = (
        P("fsdp", "ctx", None),
        P("fsdp", "ctx", None),
        P(("fsdp", "ctx"), None, "tp"),
        P("tp", ("fsdp", "ctx")),
        P(("fsdp", "ctx")),
        P(("fsdp", "ctx")),
        P(None, ("fsdp", "ctx")),
        P("fsdp", "ctx", "tp"),
        P("fsdp", "tp", "ctx"),
        P(),
        P(),
    )
    return jax.shard_map(
        per_device, mesh=mesh, in_specs=in_specs, out_specs=out_specs, check_vma=False
    )
```

```python
from functools import partial
import math
from types import SimpleNamespace

import jax
import jax.numpy as jnp
from jax import lax
from jax.experimental import pallas as pl
from jax.experimental.pallas import tpu as pltpu
from jax.sharding import PartitionSpec as P

HD = 64
EPSILON = 1e-05
BF = jnp.bfloat16
F32 = jnp.float32
MESH = pl.DeviceIdType.MESH
TOP = lax.Precision.HIGHEST
VMEM = pltpu.VMEM
ANY = pl.ANY
CAP = 16
EXP = 32
TAB = 48


def _dot(a, b, ca, cb, precision=None):
    return lax.dot_general(
        a, b, (((ca,), (cb,)), ((), ())), preferred_element_type=F32, precision=precision
    )


def nn(a, b):
    return _dot(a, b, 1, 0)


def nt(a, b):
    return _dot(a, b, 1, 1)


def tn(a, b):
    return _dot(a, b, 0, 0)


def vspec():
    return pl.BlockSpec(memory_space=VMEM)


def sds(shape, dtype):
    return jax.ShapeDtypeStruct(shape, dtype)


def params(cid=None, mib=56):
    if cid is None:
        return pltpu.CompilerParams(vmem_limit_bytes=mib * 2**20)
    return pltpu.CompilerParams(
        vmem_limit_bytes=mib * 2**20, collective_id=cid, has_side_effects=True
    )


def iota(shape, dim):
    return lax.broadcasted_iota(jnp.int32, shape, dim)


def to_col(row):
    n = row.shape[1]
    return jnp.sum(jnp.where(iota((n, n), 0) == iota((n, n), 1), row, 0.0), axis=1, keepdims=True)


def to_row(col):
    n = col.shape[0]
    return jnp.sum(jnp.where(iota((n, n), 0) == iota((n, n), 1), col, 0.0), axis=0, keepdims=True)


def norm_parts(x):
    c = x - jnp.mean(x, axis=-1, keepdims=True)
    inv = lax.rsqrt(jnp.mean(c * c, axis=-1, keepdims=True) + EPSILON)
    return c * inv, inv


def norm_back(grad, xhat, inv, gain):
    gx = grad * gain
    return inv * (
        gx
        - jnp.mean(gx, axis=-1, keepdims=True)
        - xhat * jnp.mean(gx * xhat, axis=-1, keepdims=True)
    )


def log2(v):
    return v.bit_length() - 1


def shifted(v, by):
    return lax.shift_right_logical(v, by)


def owners(zs):
    return sorted(range(1, zs), key=lambda s: (-min(s, zs - s), s)) + [0]


class Route:
    def __init__(self, chosen, zs, z, width=0):
        n = chosen.shape[1]
        m = n // zs
        per = CAP // zs
        chosen = to_col(chosen.astype(F32))
        self.hot = (chosen == iota((n, EXP), 1).astype(F32)).astype(BF)
        lower = (iota((n, n), 1) < iota((n, n), 0)).astype(BF)
        rank = jnp.sum(nn(lower, self.hot) * self.hot.astype(F32), axis=1, keepdims=True)
        turn = jnp.floor(rank * (1.0 / zs))
        owner = rank - zs * turn
        owned = (owner == iota((n, zs), 1).astype(F32)).astype(BF)
        place = jnp.sum(nn(lower, owned) * owned.astype(F32), axis=1, keepdims=True)
        ahead = owner - lax.convert_element_type(z, F32)
        ahead = jnp.where(ahead < 0, ahead + zs, ahead)
        order = sum(jnp.where(ahead == step, float(k), 0.0) for k, step in enumerate(owners(zs)))
        self.at = order * m + place
        self.at_row = to_row(self.at)
        mine = iota((m, n), 0).astype(F32) + float((zs - 1) * m) == self.at_row
        self.mine = mine.astype(BF)
        self.mine_mask = mine
        self.slot = self.own_col(to_row(chosen * per + turn))
        self.own_hot = nn(self.mine, self.hot).astype(BF)
        self.slots = EXP * per
        self.n, self.m, self.width = n, m, width

    def positions(self):
        n = self.n
        return jnp.sum(jnp.where(self.at == iota((n, n), 1).astype(F32), iota((n, n), 0).astype(F32), 0.0), axis=0, keepdims=True)

    def own_col(self, row):
        return jnp.sum(jnp.where(self.mine_mask, row, 0.0), axis=1, keepdims=True)

    def own(self, rows):
        return nn(self.mine, rows)

    def sort(self, rows):
        return nn((iota((self.n, self.n), 0).astype(F32) == self.at_row).astype(BF), rows).astype(BF)

    def unsort(self, rows):
        return nn((iota((self.n, self.n), 1).astype(F32) == self.at).astype(BF), rows).astype(BF)

    def fill(self, rows, s_ref):
        place = (iota((self.slots, self.m), 0).astype(F32) == to_row(self.slot)).astype(BF)
        filled = nn(place, rows).astype(BF)
        fs, _, _, r, _ = s_ref.shape
        h = self.width // 2
        for f in range(fs):
            for c in range(2):
                at = (f * 2 + c) * r
                for y in range(2):
                    s_ref[f, y, c, :, :h] = filled[at : at + r, y * h : (y + 1) * h]
                    if rows.shape[1] > self.width:
                        s_ref[f, y, c, :, h:] = filled[at : at + r, self.width :]

    def collect(self, rb_ref):
        parts = []
        for f in range(rb_ref.shape[0] // 4):
            for c in range(2):
                parts.append(jnp.concatenate([rb_ref[f * 4 + c], rb_ref[f * 4 + 2 + c]], axis=1))
        rows = jnp.concatenate(parts, axis=0)
        place = (iota((self.m, self.slots), 1).astype(F32) == self.slot).astype(BF)
        return nn(place, rows)


def z_peers(zs):
    f, i, z = lax.axis_index("fsdp"), lax.axis_index("ctx"), lax.axis_index("tp")
    return [(f, i, lax.rem(z + s, zs)) for s in range(1, zs)]


def greet(peers):
    barrier = pltpu.get_barrier_semaphore()
    for peer in peers:
        pl.semaphore_signal(barrier, inc=1, device_id=peer, device_id_type=MESH)
    pl.semaphore_wait(barrier, len(peers))


def remote(src, dst, send, recv, peer):
    return pltpu.make_async_remote_copy(
        src_ref=src, dst_ref=dst, send_sem=send, recv_sem=recv, device_id=peer, device_id_type=MESH
    )


class Scatter:
    def __init__(self, zs, x_ref, parts, send, recv):
        self.zs, self.x_ref, self.parts, self.send, self.recv = zs, x_ref, parts, send, recv
        self.m = x_ref.shape[0] // zs
        self.copies = []

    def start(self, lo, hi):
        peers = z_peers(self.zs)
        for k, step in list(enumerate(owners(self.zs)))[lo:hi]:
            if step:
                cp = remote(
                    self.x_ref.at[pl.ds(k * self.m, self.m)], self.parts.at[step - 1],
                    self.send.at[step - 1], self.recv.at[step - 1], peers[step - 1],
                )
                cp.start()
                self.copies.append((step, cp))

    def finish(self):
        total = self.x_ref[pl.ds((self.zs - 1) * self.m, self.m), :].astype(F32)
        for step, cp in sorted(self.copies, key=lambda v: v[0]):
            cp.wait_recv()
            total = total + self.parts[step - 1].astype(F32)
        return total


def gather_z(zs, x_ref, m, send, recv):
    copies = []
    order = owners(zs)
    for s, peer in enumerate(z_peers(zs)):
        to = order.index(zs - s - 1)
        cp = remote(
            x_ref.at[pl.ds((zs - 1) * m, m)], x_ref.at[pl.ds(to * m, m)], send.at[s], recv.at[s], peer
        )
        cp.start()
        copies.append(cp)
    return copies


def span(at, n):
    return pl.ds(pl.multiple_of(at * n, n), n)


def group_peers(fs):
    f, i, z = lax.axis_index("fsdp"), lax.axis_index("ctx"), lax.axis_index("tp")
    y, c = lax.div(i, 2), lax.rem(i, 2)
    out = []
    for df in range(fs):
        for dy in range(2):
            for dc in range(2):
                if df or dy or dc:
                    fp = lax.rem(f + df, fs)
                    yp = y if dy == 0 else 1 - y
                    cp = c if dc == 0 else 1 - c
                    out.append((fp, yp, cp, (fp, yp * 2 + cp, z)))
    return out


class Attention:
    def __init__(self, R, mine, offsets, row0, positions):
        self.R = R
        self.k, self.n = R.qt.shape
        self.heads = self.k // HD
        self.offsets, self.row0 = offsets, row0
        self.query = positions + lax.convert_element_type(mine * self.n, F32)

    def lanes(self, half):
        return slice(half * (self.n // 2), (half + 1) * (self.n // 2))

    def scores(self, half, j):
        R, at, w = self.R, self.lanes(half), self.n // 2
        key = (iota((self.n, w), 0) + self.offsets[j] * self.n).astype(F32)
        col = to_col(R.valid[pl.ds(self.row0 + self.offsets[j], 1), :])
        query = self.query[:, at]
        prefix = lax.convert_element_type(R.prefix[0], F32)
        allowed = ((key <= query) | (key < prefix)) & ((col > 0.5) | (key == query))
        for h in range(self.heads):
            lo = h * HD
            scores = nn(R.kv[j, :, lo : lo + HD], R.qt[lo : lo + HD, at]) * (1.0 / math.sqrt(HD))
            R.scores[h, j, :, at] = jnp.where(allowed, scores, -1e30)

    def context(self, half):
        R, at, w, k = self.R, self.lanes(half), self.n // 2, self.k
        outs = []
        for h in range(self.heads):
            lo = h * HD
            top = jnp.max(R.scores[h, 0, :, at], axis=0, keepdims=True)
            for j in range(1, 4):
                top = jnp.maximum(top, jnp.max(R.scores[h, j, :, at], axis=0, keepdims=True))
            exps = [jnp.exp(R.scores[h, j, :, at] - top) for j in range(4)]
            share = 1.0 / sum(jnp.sum(e, axis=0, keepdims=True) for e in exps)
            acc = jnp.zeros((HD, w), F32)
            for j in range(4):
                weights = (exps[j] * share).astype(BF)
                R.pt[h, j, :, at] = weights
                acc = acc + tn(R.kv[j, :, k + lo : k + lo + HD], weights)
            outs.append(acc)
        return jnp.transpose(jnp.concatenate(outs, axis=0)).astype(BF)

    def back(self, half, gct, fresh, made):
        R, at, k = self.R, self.lanes(half), self.k
        scale = 1.0 / math.sqrt(HD)
        means, dqs = [], []
        for h in range(self.heads):
            lo = h * HD
            mean = 0.0
            for j in range(4):
                dp = nn(R.kv[j, :, k + lo : k + lo + HD], gct[lo : lo + HD, :])
                R.scores[h, j, :, at] = dp
                mean = mean + jnp.sum(R.pt[h, j, :, at].astype(F32) * dp, axis=0, keepdims=True)
            means.append(mean)
            dqs.append(jnp.zeros((HD, self.n // 2), F32))
        for j in (3, 1, 2, 0):
            target = R.near if j < 2 else R.away
            for h in range(self.heads):
                lo = h * HD
                w = R.pt[h, j, :, at]
                ds = (w.astype(F32) * (R.scores[h, j, :, at] - means[h])).astype(BF)
                dqs[h] = dqs[h] + tn(R.kv[j, :, lo : lo + HD], ds)
                dk = nt(ds, R.qt[lo : lo + HD, at]) * scale
                dv = nt(w, gct[lo : lo + HD, :])
                if not fresh:
                    dk = dk + target[j % 2, :, lo : lo + HD]
                    dv = dv + target[j % 2, :, k + lo : k + lo + HD]
                target[j % 2, :, lo : lo + HD] = dk
                target[j % 2, :, k + lo : k + lo + HD] = dv
            made(j)
        return jnp.concatenate(dqs, axis=0) * scale


def finish_body(scalars, c_ref, *refs):
    tg_in, act_in, mix_in, og_in, sm_in, stat_in = refs[8:14]
    up_ref, down_ref, tg_ref, act_ref, mix_ref, og_ref, cen_ref, g1_ref, g2_ref, bal_ref, dis_ref = refs[14:]
    c = c_ref[0]
    for out_ref, at in ((up_ref, 0), (down_ref, 4)):
        for core, (left_ref, right_ref) in ((c, refs[at : at + 2]), (1 - c, refs[at + 2 : at + 4])):
            for e in range(left_ref.shape[0]):
                out_ref[core, e] = nn(left_ref[e], right_ref[e])

    @pl.when(pl.program_id(0) == 0)
    def _():
        tg_ref[...] = tg_in[...]
        act_ref[...] = act_in[...]
        mix_ref[...] = mix_in[...]
        og_ref[...] = og_in[...]
        rows = cen_ref.shape[1]
        cen_ref[...] = sm_in[0:EXP, :rows]
        g1_ref[...] = sm_in[EXP : EXP + 1, :rows]
        g2_ref[...] = sm_in[EXP + 1 : EXP + 2, :rows]
        share = stat_in[0:1, :EXP] / scalars - 1.0 / EXP
        bal_ref[0, 0] = EXP * EXP * jnp.sum(share * stat_in[1:2, :EXP] / scalars)
        dis_ref[0, 0] = jnp.sum(stat_in[2:3, 0:1])


def finish(c, tokens, pairs, small, shapes):
    half, q, n = pairs[0].shape
    units = pairs[1].shape[2]
    step = 2 if half % 2 == 0 else 1
    block = lambda e, c_ref: (e, 0, 0)
    out = sds((2, half, q, units), F32)
    whole = lambda v: pl.BlockSpec(v.shape, lambda e, c_ref: (0,) * len(v.shape))
    smem = pl.BlockSpec(memory_space=pltpu.SMEM)
    scalar = sds((1, 1), F32)
    return pl.pallas_call(
        partial(finish_body, float(tokens)),
        grid_spec=pltpu.PrefetchScalarGridSpec(
            num_scalar_prefetch=1,
            grid=(half // step,),
            in_specs=[pl.BlockSpec((step, q, n), block), pl.BlockSpec((step, n, units), block)] * 4
            + [whole(v) for v in small],
            out_specs=[pl.BlockSpec((2, step, q, units), lambda e, c_ref: (0, e, 0, 0))] * 2
            + [whole(v) for v in shapes] + [smem] * 2,
        ),
        out_shape=[out, out] + shapes + [scalar] * 2,
        compiler_params=params(),
        name="finish",
    )(c.reshape(1), *pairs, *small)


def whereabouts():
    f, i, z = lax.axis_index("fsdp"), lax.axis_index("ctx"), lax.axis_index("tp")
    return f, i, z, lax.div(i, 2), lax.rem(i, 2)


def reorder(sources, half, per, inverse):
    n = sources * half * per
    i, o = iota((n, n), 1), iota((n, n), 0)
    if inverse:
        i, o = o, i
    ls, lh, lp = log2(sources), log2(half), log2(per)
    slot = o & (per - 1)
    source = shifted(o, lp) & (sources - 1)
    expert = shifted(o, lp + ls)
    return (i == source * (half * per) + expert * per + slot).astype(BF)


class Pass:
    def __init__(self, back, zs, w_in, w_out, xg, x_ref, ps, pr, h_ref, gp_ref, res, rin, sems):
        self.back, self.zs, self.w_in, self.w_out = back, zs, w_in, w_out
        self.xg, self.x_ref, self.ps, self.pr = xg, x_ref, ps, pr
        self.h_ref, self.gp_ref, self.res, self.rin = h_ref, gp_ref, res, rin
        self.a_s, self.a_r, self.x_s, self.x_r, self.r_s, self.r_r = sems
        f, i, z, y, c = whereabouts()
        self.z = z
        self.m = xg.shape[1]
        self.across = (f, (1 - y) * 2 + c, z)
        self.peers = z_peers(zs)

    def share(self, e, s):
        to = self.x_ref.at[e, span(self.z, self.m), :]
        return remote(self.xg.at[e], to, self.a_s.at[e, s], self.a_r.at[e, s], self.peers[s])

    def cross(self, e):
        return remote(self.ps.at[e], self.pr.at[e], self.x_s.at[e], self.x_r.at[e], self.across)

    def scatter(self, e, s):
        to = lax.rem(self.z + s + 1, self.zs)
        return remote(
            self.res.at[e, span(to, self.m), :], self.rin.at[e, s], self.r_s.at[e, s], self.r_r.at[e, s], self.peers[s]
        )

    def spread(self, e, rows):
        self.xg[e] = rows
        for s in range(self.zs - 1):
            self.share(e, s).start()
        self.x_ref[e, span(self.z, self.m), :] = rows

    def first(self, e):
        for s in range(self.zs - 1):
            self.share(e, s).wait_recv()
        self.ps[e] = nn(self.x_ref[e], self.w_in[e]).astype(BF)

    def second(self, e):
        self.cross(e).wait_recv()
        total = self.ps[e].astype(F32) + self.pr[e].astype(F32)
        if self.back:
            self.h_ref[e] = (total * self.gp_ref[e].astype(F32)).astype(BF)
        else:
            phi = 0.5 * (1.0 + lax.erf(total * math.sqrt(0.5)))
            self.h_ref[e] = (total * phi).astype(BF)
            bell = jnp.exp(-0.5 * total * total) * (1.0 / math.sqrt(2.0 * math.pi))
            self.gp_ref[e] = (phi + total * bell).astype(BF)
        self.res[e] = nt(self.h_ref[e], self.w_out[e]).astype(BF)
        for s in range(self.zs - 1):
            self.scatter(e, s).start()

    def total(self, e):
        total = self.res[e, span(self.z, self.m), :].astype(F32)
        for s in range(self.zs - 1):
            self.scatter(e, s).wait_recv()
            total = total + self.rin[e, s].astype(F32)
        return total.astype(BF)

    def settle(self, e):
        self.cross(e).wait_send()
        for s in range(self.zs - 1):
            self.share(e, s).wait_send()
            self.scatter(e, s).wait_send()


def give_back(fs, total, ret, rb_ref, own_sem, send, recv):
    f, i, z, y, c = whereabouts()
    me = f * 4 + i
    sources, r, dh = ret.shape
    half = total.shape[0]
    rows = total[...].reshape(sources * r, dh)
    ret[...] = nn(reorder(sources, half, r // half, True), rows).astype(BF).reshape(sources, r, dh)
    keep = pltpu.make_async_copy(ret.at[me], rb_ref.at[me], own_sem)
    keep.start()
    copies = []
    for k, (fp, yp, cp_, peer) in enumerate(group_peers(fs)):
        cp = remote(ret.at[fp * 4 + yp * 2 + cp_], rb_ref.at[me], send.at[k], recv.at[k], peer)
        cp.start()
        copies.append(cp)
    return keep, copies


def arrived(given):
    keep, copies = given
    keep.wait()
    for cp in copies:
        cp.wait_recv()


def head(R, fs, zs, gather):
    f, i, z, y, c = whereabouts()
    me = f * 4 + i
    half, width = R.wu.shape[0], R.up.shape[1]
    k = R.qt.shape[0]
    d = R.tok.shape[1]
    sibling = (f, y * 2 + 1 - c, z)
    across = (f, (1 - y) * 2 + c, z)
    same = same_core(fs)
    waits = []
    mine = pl.ds(c * half, half)
    theirs = pl.ds((1 - c) * half, half)
    own = pl.ds(pl.multiple_of(c * width, 64), width)
    loads = [
        pltpu.make_async_copy(R.up.at[mine], R.wu.at[:, own, :], R.wsem.at[0]),
        pltpu.make_async_copy(R.dn.at[mine], R.wd.at[:, own, :], R.wsem.at[1]),
    ]
    swaps = [
        remote(R.up.at[theirs], R.wu.at[:, own, :], R.wx_s.at[0], R.wx_r.at[0], sibling),
        remote(R.dn.at[theirs], R.wd.at[:, own, :], R.wx_s.at[1], R.wx_r.at[1], sibling),
    ]
    if gather:
        rows = R.mix.shape[1]
        R.small[...] = jnp.zeros(R.small.shape, F32)
        R.small[0:EXP, :rows] = R.cent[...].astype(F32)
        R.small[EXP : EXP + 1, :rows] = R.gain1[...].astype(F32)
        R.small[EXP + 1 : EXP + 2, :rows] = R.gain2[...].astype(F32)
        R.small[EXP + 2 : EXP + 3, :] = R.here[...].astype(F32)
        R.small_all[me] = R.small[...].astype(BF)
        R.w3[:, span(me, rows), :] = R.mix[...]
        R.wo[span(me, rows), :] = jnp.transpose(R.ow[...].astype(F32)).astype(BF)
    greet([p[3] for p in group_peers(fs)] + z_peers(zs))
    for cp in loads:
        cp.start()
    xhat, _ = norm_parts(R.tok[...].astype(F32))
    others = []

    def over_z(rows_, pair):
        n_ = len(others) // (zs - 1)
        for s, peer in enumerate(z_peers(zs)):
            cp = remote(R.wo.at[rows_, :], R.wo_all.at[z, pair, c], R.wz_s.at[s, n_], R.wz_r.at[s, n_], peer)
            cp.start()
            others.append(cp)

    if gather:

        def places(at):
            rows_ = span(at, rows)
            return [R.w3.at[1:3, rows_, :], R.small_all.at[at], R.w3.at[0:1, rows_, :], R.wo.at[rows_, :]]

        sends = {}
        for m, ref in sorted(enumerate(places(me)), key=lambda v: (0, 1, 3, 2)[v[0]]):
            for n_, (_, _, peer, _) in enumerate(same):
                cp = remote(ref, ref, R.p_s.at[n_, m], R.p_r.at[n_, m], peer)
                cp.start()
                sends[n_, m] = cp
        over_z(span(me, rows), f * 2 + y)
        relays = {}

        def relay(n_, m, at):
            ref = places(at)[m]
            cp = remote(ref, ref, R.q_s.at[n_, m], R.q_r.at[n_, m], sibling)
            cp.start()
            relays[n_, m] = cp

        def pass_on(some):
            for n_, (_, _, _, at) in enumerate(same):
                for m in some:
                    sends[n_, m].wait_recv()
                    relay(n_ + 1, m, at)

        for m in range(4):
            relay(0, m, me)
        pass_on((0, 1))
        pass_on((3,))
        for _, _, _, at in same:
            over_z(span(at, rows), lax.div(at, 2))
        for n_ in range(len(same) + 1):
            for m in (0, 1):
                relays[n_, m].wait_recv()
        R.table[...] = jnp.concatenate([R.small_all[s, :, :rows] for s in range(fs * 4)], axis=1)
        for s in range(fs * 4):
            R.valid[s : s + 1, :] = R.small_all[s, EXP + 2 : EXP + 3, :].astype(F32)
    normed = (xhat * R.table[EXP : EXP + 1, :].astype(F32)).astype(BF)
    R.normed[...] = normed
    R.kv[0, :, :k] = nn(normed, R.w3[1]).astype(BF)
    R.kv[0, :, k:] = nn(normed, R.w3[2]).astype(BF)
    far = remote(R.kv.at[0], R.kv.at[1], R.kv_s.at[0], R.kv_r.at[0], across)
    sib = remote(R.kv.at[0], R.kv.at[2], R.kv_s.at[1], R.kv_r.at[1], sibling)
    far.start()
    sib.start()
    if gather:
        pass_on((2,))
        for n_ in range(len(same) + 1):
            for m in (2, 3):
                relays[n_, m].wait_recv()
        waits += list(sends.values()) + list(relays.values())
    else:
        over_z(span(c, d // 2), 0)
    route = Route(R.chosen[...], zs, z, d)
    R.qt[...] = jnp.transpose(route.sort(nn(normed, R.w3[0]).astype(BF)).astype(F32)).astype(BF)
    teacher, cotangent = route.own(R.tea[...]), route.own(R.cot[...])
    own_tokens = route.own(R.tok[...])
    own_valid = route.own_col(R.valid[pl.ds(me, 1), :])
    scale = 1.0 / (jnp.sum(R.valid[...]) * d)
    sib.wait_recv()
    offsets = [i, (1 - y) * 2 + c, y * 2 + 1 - c, (1 - y) * 2 + 1 - c]
    attention = Attention(R, i, offsets, f * 4, route.positions())
    for j in (0, 2):
        for half_ in range(2):
            attention.scores(half_, j)
    far.wait_recv()
    last = remote(R.kv.at[1], R.kv.at[3], R.kv_s.at[2], R.kv_r.at[2], sibling)
    last.start()
    for swap in swaps:
        swap.start()
    attention.scores(0, 1)
    attention.scores(1, 1)
    last.wait_recv()
    n = R.tok.shape[0]
    m = n // zs
    peers = z_peers(zs)
    sums, passed = [], []
    for half_ in range(2):
        attention.scores(half_, 3)
        R.ctx[pl.ds(half_ * (n // 2), n // 2), :] = attention.context(half_)
        for k_, step in list(enumerate(owners(zs)))[half_ * (zs // 2) : (half_ + 1) * (zs // 2)]:
            if step:
                cp = remote(
                    R.ctx.at[pl.ds(k_ * m, m)], R.ctx_in.at[step - 1],
                    R.hz_s.at[step - 1], R.hz_r.at[step - 1], peers[step - 1],
                )
                cp.start()
                sums.append(cp)
        if half_ == 1:
            for cp in others:
                cp.wait_recv()
            for s in range(zs - 1):
                ref = R.wo_all.at[lax.rem(z - s - 1 + zs, zs), :, c]
                cp = remote(ref, ref, R.wy_s.at[s], R.wy_r.at[s], sibling)
                cp.start()
                passed.append(cp)
    residual = own_tokens + nt(R.ctx[pl.ds((zs - 1) * m, m), :], R.wo[...])
    for cp in sums + passed:
        cp.wait_recv()
    for step in range(1, zs):
        residual = residual + nt(R.ctx_in[step - 1], R.wo_all[lax.rem(z - step + zs, zs)].reshape(R.wo.shape))
    R.res[...] = residual
    xhat, _ = norm_parts(residual)
    mixed_in = (xhat * R.table[EXP + 1 : EXP + 2, :].astype(F32)).astype(BF)
    R.mi[...] = mixed_in
    logit = jnp.sum(mixed_in.astype(F32) * nn(route.own_hot, R.table[0:EXP, :]), axis=-1, keepdims=True)
    gate = jax.nn.sigmoid(logit)
    route.fill(mixed_in, R.slots)
    sends = dispatch(fs, R.slots, R.rq, R.d_s, R.d_r, R.wsem.at[2])
    weight = 2.0 * own_valid * scale
    known = gate * (cotangent + weight * (residual - teacher))
    slope = jnp.broadcast_to(gate * gate * weight, (known.shape[0], 128))
    route.fill(jnp.concatenate([known, slope], axis=1).astype(BF), R.slots_g)
    sends_g = dispatch(fs, R.slots_g, R.rg, R.g_s, R.g_r, R.wsem.at[3])
    waits += swaps + sums + others + passed + [far, sib, last]
    return SimpleNamespace(route=route, attention=attention, own_tokens=own_tokens, sends=sends, sends_g=sends_g, gate=gate, teacher=teacher, cotangent=cotangent, valid=own_valid, scale=scale,
                           loads=loads, swaps=swaps, waits=waits)


def dispatch(fs, src, dst, send, recv, own_sem):
    f, i, z, y, c = whereabouts()
    me = f * 4 + i
    copies = [pltpu.make_async_copy(src.at[f, y, c], dst.at[me], own_sem)]
    for k, (fp, yp, cp_, peer) in enumerate(group_peers(fs)):
        copies.append(remote(src.at[fp, yp, cp_], dst.at[me], send.at[k], recv.at[k], peer))
    for cp in copies:
        cp.start()
    return copies


def same_core(fs):
    f, i, z, y, c = whereabouts()
    out = []
    for df in range(fs):
        for dy in range(2):
            if df or dy:
                fp, fm = lax.rem(f + df, fs), lax.rem(f - df + fs, fs)
                yp = y if dy == 0 else 1 - y
                out.append((fp, yp, (fp, yp * 2 + c, z), fm * 4 + yp * 2 + c))
    return out


def middle(R, S, fs, zs):
    f, i, z, y, c = whereabouts()
    me = f * 4 + i
    half, width = R.wu.shape[0], R.up.shape[1]
    sources, r, dh = R.rq.shape
    m = sources * r // half
    group = group_peers(fs)
    sibling = (f, y * 2 + 1 - c, z)
    own = pl.ds(pl.multiple_of(c * width, 64), width)
    other = pl.ds(pl.multiple_of((1 - c) * width, 64), width)
    sems = [[getattr(R, p + n) for n in ("a_s", "a_r", "x_s", "x_r", "r_s", "r_r")] for p in ("one_", "two_")]
    one = Pass(False, zs, R.wu, R.wd, R.xg, R.x, R.ps, R.pr, R.act, R.gp, R.rows, R.rin, sems[0])
    two = Pass(True, zs, R.wd, R.wu, R.xg_back, R.gx, R.ps, R.pr_back, R.gh, R.gp, R.rows, R.rin, sems[1])
    order = reorder(sources, half, r // half, False)
    exports = []

    def export(n, own_src, own_dst, src, dst):
        keep = pltpu.make_async_copy(own_src, own_dst, R.l_s.at[n])
        give = remote(src, dst, R.e_s.at[n], R.e_r.at[n], sibling)
        keep.start()
        give.start()
        exports.append((keep, give))

    for cp in S.loads:
        cp.wait()
    for cp in S.swaps:
        cp.wait_recv()
    arrived((S.sends[0], S.sends[1:]))
    rows = nn(order, R.rq[...].reshape(sources * r, dh)).astype(BF).reshape(half, m, dh)
    for e in range(half):
        one.spread(e, rows[e])

    @pl.loop(0, half)
    def _(e):
        one.first(e)
        one.cross(e).start()

    @pl.loop(0, half)
    def _(e):
        R.xt[e] = jnp.transpose(R.x[e])

    arrived((S.sends_g[0], S.sends_g[1:]))
    R.grads[...] = nn(order, R.rg[...].reshape(sources * r, dh + 128)).astype(BF).reshape(half, m, dh + 128)
    export(0, R.xt.at[:, own, :], R.xt_own, R.xt.at[:, other, :], R.xt_sib)

    def turn(e):
        result = one.total(e)
        R.results[e] = result
        scale = R.grads[e, :, dh:].astype(F32)[:, :1]
        two.spread(e, (R.grads[e, :, :dh].astype(F32) + scale * result.astype(F32)).astype(BF))

    lag, lag2 = 2, 4
    start = max(half, lag2 + 1)
    ahead = 3

    def step(t, fixed=True):
        if not fixed or t < half:
            one.second(t)
        if fixed and t - start >= 0 and t - start < half:
            two.second(t - start)
        if not fixed or 0 <= t - lag < half:
            turn(t - lag)
        if not fixed or 0 <= t - lag2 < half:
            one.settle(t - lag2)
            two.first(t - lag2)

    begun = 0
    t = 0
    while t < lag2:
        step(t)
        t += 1
    safe = max(t, start - ahead)
    if safe > t and half > t:
        stop = min(safe, half)

        @pl.loop(t, stop)
        def _(k):
            step(k, False)

        t = stop
    given = None
    pending = []

    def report():
        returned = S.route.collect(R.rb)
        n, d = returned.shape
        mixed = R.res[...] + S.gate * returned
        diff = mixed - S.teacher
        weighted = S.valid * diff
        grad = S.cotangent + 2.0 * weighted * S.scale
        R.sorted_out[pl.ds((zs - 1) * n, n), :] = mixed.astype(BF)
        pending.extend(gather_z(zs, R.sorted_out, n, R.o_s, R.o_r))
        hot = S.route.own_hot.astype(F32)
        R.stat[...] = jnp.zeros_like(R.stat)
        R.stat[0:1, 0:EXP] = jnp.sum(hot, axis=0, keepdims=True)
        R.stat[1:2, 0:EXP] = jnp.sum(hot * S.gate, axis=0, keepdims=True)
        R.stat[2:3, :] = jnp.broadcast_to(jnp.sum(weighted * diff * S.scale), (1, 128))
        for s, peer in enumerate(z_peers(zs)):
            cp = remote(R.stat, R.stat_in.at[s], R.t_s.at[s], R.t_r.at[s], peer)
            cp.start()
            pending.append(cp)
        R.gm[...] = grad
        grad_gate = jnp.sum(grad * returned, axis=-1, keepdims=True)
        R.gl[...] = grad_gate * S.gate * (1.0 - S.gate)

    def publish():
        total = R.stat[...]
        for s, cp in enumerate(pending[zs - 1 :]):
            cp.wait_recv()
            total = total + R.stat_in[s]
        R.stat_all[me] = total
        for k, (_, _, _, peer) in enumerate(group):
            cp = remote(R.stat_all.at[me], R.stat_all.at[me], R.u_s.at[k], R.u_r.at[k], peer)
            cp.start()
            pending.append(cp)

    while t < start + half + 1:
        step(t)
        if given is None and t - lag >= half - 1:
            given = give_back(fs, R.results, R.ret, R.rb, R.wsem.at[4], R.b_s, R.b_r)
            export(1, R.act, R.act_own, R.act, R.act_sib)
        while begun < half and begun <= t - start + ahead and begun <= t - lag2:
            two.cross(begun).start()
            begun += 1
        if 0 <= t - 1 - start < half:
            R.xg[t - 1 - start] = two.total(t - 1 - start)
        if t == max(start + half - 4, start + 1) or (half == 1 and t == start):

            @pl.loop(0, half)
            def _(e):
                R.gxt[e] = jnp.transpose(R.gx[e])

        if t == start + half - 2 or (half == 1 and t == start):
            arrived(given)
            report()
        if t == start + half - 1:
            publish()
        t += 1
    given_back = give_back(fs, R.xg, R.ret_back, R.rb_back, R.wsem.at[5], R.c_s, R.c_r)
    export(2, R.gxt.at[:, own, :], R.gxt_own, R.gxt.at[:, other, :], R.gxt_sib)
    export(3, R.gh, R.gh_own, R.gh, R.gh_sib)
    S.pending, S.exports = pending, exports
    S.waits += pending[: 2 * (zs - 1)] + S.sends[1:] + S.sends_g[1:] + given[1] + given_back[1]
    S.two = two
    arrived(given_back)
    return S.route.collect(R.rb_back)


def back(R, S, grad_back, fs, zs, rows):
    f, i, z, y, c = whereabouts()
    sibling = (f, y * 2 + 1 - c, z)
    across = (f, (1 - y) * 2 + c, z)
    same = same_core(fs)
    route = S.route
    k = R.qt.shape[0]
    gl = R.gl[...]
    grad_in = grad_back + gl * nn(route.own_hot, R.table[0:EXP, :])
    m, d = grad_in.shape
    xhat, inv = norm_parts(R.res[...])
    grad = R.gm[...] + norm_back(grad_in, xhat, inv, R.table[EXP + 1 : EXP + 2, :].astype(F32))
    R.sorted_gb[pl.ds((zs - 1) * m, m), :] = grad.astype(BF)
    gb = grad.astype(BF)
    order = owners(zs)
    pieces = []
    for s, peer in enumerate(z_peers(zs)):
        R.gct_out[s] = nn(gb, R.wo_all[lax.rem(z + s + 1, zs)].reshape(R.wo.shape)).astype(BF)
        to = R.gct.at[pl.ds(order.index(zs - s - 1) * m, m)]
        cp = remote(R.gct_out.at[s], to, R.gc_s.at[s], R.gc_r.at[s], peer)
        cp.start()
        pieces.append(cp)
    R.gct[pl.ds((zs - 1) * m, m), :] = nn(gb, R.wo[...]).astype(BF)
    gathers = gather_z(zs, R.sorted_gb, m, R.ba_s, R.ba_r)
    g2 = jnp.sum(grad_in * xhat, axis=0, keepdims=True)
    cg = _dot(route.own_hot.astype(F32) * gl, R.mi[...].astype(F32), 0, 0, TOP)
    all_tok = norm_parts(route.sort(R.tok[...]).astype(F32))[0]
    own_tok, own_inv = norm_parts(S.own_tokens)
    for cp in S.pending[: zs - 1]:
        cp.wait_recv()
    R.out[...] = route.unsort(R.sorted_out[...])
    for cp in S.pending[2 * (zs - 1) :]:
        cp.wait()
    total = R.stat_all[0]
    for n in range(1, fs * 4):
        total = total + R.stat_all[n]
    R.stat_out[...] = total
    n = R.tok.shape[0]
    swaps = [remote(R.away.at[j], R.away_in.at[j], R.k_s.at[j], R.k_r.at[j], sibling) for j in range(2)]
    cross = remote(R.far_out, R.far_in, R.k_s.at[2], R.k_r.at[2], across)

    def nothing(j):
        pass

    def made(j):
        if j == 3:
            swaps[1].start()
        if j == 1:
            swaps[1].wait_recv()
            R.far_out[...] = (R.near[1] + R.away_in[1]).astype(BF)
            cross.start()
        if j == 2:
            swaps[0].start()

    dqs = {}
    for half, steps in ((1, (0,)), (0, range(1, zs - 1))):
        for s in steps:
            pieces[s].wait_recv()
        gct = jnp.transpose(R.gct[pl.ds(half * (n // 2), n // 2), :])
        dqs[half] = S.attention.back(half, gct, half == 1, nothing if half == 1 else made)
    dq = jnp.transpose(jnp.concatenate([dqs[0], dqs[1]], axis=1)).astype(BF)
    normed = R.normed[...]
    gq = nt(dq, R.w3[0])
    mg = [tn(normed, route.unsort(dq)), None, None]
    swaps[0].wait_recv()
    near = R.near[0] + R.away_in[0]
    cross.wait_recv()
    kvg = (near + R.far_in[...].astype(F32)).astype(BF)
    kvs = route.sort(kvg)
    partial_normed = gq + nt(kvs[:, :k], R.w3[1]) + nt(kvs[:, k:], R.w3[2])
    R.gn[...] = partial_normed.astype(BF)
    scat = Scatter(zs, R.gn, R.gn_in, R.bs_s, R.bs_r)
    scat.start(0, zs)
    mg[1] = tn(normed, kvg[:, :k])
    mg[2] = tn(normed, kvg[:, k:])
    g1 = jnp.sum(partial_normed * all_tok, axis=0, keepdims=True)
    for cp in gathers:
        cp.wait_recv()
    og = tn(R.sorted_gb[...], R.ctx[...])
    dense = R.dense
    last = dense.shape[3] - TAB
    small = jnp.concatenate([cg, g1, g2, jnp.zeros((TAB - EXP - 2, d), F32)], axis=0)
    for s in range(4 * fs):
        at = (s // 4, s % 4 // 2, s % 2)
        lo = s * rows
        for j in range(3):
            dense[at[0], at[1], at[2], 0:rows, j * k : (j + 1) * k] = mg[j][lo : lo + rows, :]
        dense[at[0], at[1], at[2], 0:rows, 3 * k : 4 * k] = og[lo : lo + rows, :]
        dense[at[0], at[1], at[2], last : last + TAB, 0:rows] = small[:, lo : lo + rows]
    pair = remote(dense.at[:, :, 1 - c], R.dense_in, R.k_s.at[3], R.k_r.at[3], sibling)
    pair.start()
    pair.wait_recv()
    shares = []
    for s, (fp, yp, peer, _) in enumerate(same):
        R.give[s] = (dense[fp, yp, c] + R.dense_in[fp, yp]).astype(BF)
        cp = remote(R.give.at[s], R.taken.at[s], R.bg_s.at[s], R.bg_r.at[s], peer)
        cp.start()
        shares.append(cp)
    total = scat.finish()
    tg = grad + norm_back(total, own_tok, own_inv, R.table[EXP : EXP + 1, :].astype(F32))
    R.sorted_tg[pl.ds((zs - 1) * m, m), :] = tg.astype(BF)
    ends = gather_z(zs, R.sorted_tg, m, R.bt_s, R.bt_r)
    kept = dense[f, y, c] + R.dense_in[f, y]
    for s, cp in enumerate(shares):
        cp.wait_recv()
        kept = kept + R.taken[s].astype(F32)
    R.sm[...] = kept[last:, :128]
    smalls = []
    for s, peer in enumerate(z_peers(zs)):
        cp = remote(R.sm, R.sm_in.at[s], R.v_s.at[s], R.v_r.at[s], peer)
        cp.start()
        smalls.append(cp)
    for j in range(3):
        R.mix_out[j] = kept[:rows, j * k : (j + 1) * k]
    R.og_out[...] = jnp.transpose(kept[:rows, 3 * k :])
    for keep, give in S.exports:
        keep.wait()
        give.wait()
    for cp in ends:
        cp.wait_recv()
    R.tg_out[...] = route.unsort(R.sorted_tg[...])
    total = R.sm[...]
    for s, cp in enumerate(smalls):
        cp.wait_recv()
        total = total + R.sm_in[s]
    R.sm_out[...] = total
    for cp in S.waits + pieces + gathers + swaps + [cross, pair] + [v[1] for v in scat.copies] + shares + ends + smalls:
        cp.wait_send()

    @pl.loop(0, R.wu.shape[0])
    def _(e):
        S.two.settle(e)


def layer_body(names, fs, zs, gather, rows, *refs):
    R = SimpleNamespace(**dict(zip(names, refs)))
    S = head(R, fs, zs, gather)
    grad_back = middle(R, S, fs, zs)
    back(R, S, grad_back, fs, zs, rows)


def per_device(tokens, mixing_weight, output_weight, first_gain, second_gain, centroids, expert_up,
               expert_down, prefix_length, assignment, validity, teacher, cotangent):
    fs, zs = lax.axis_size("fsdp"), lax.axis_size("tp")
    c = lax.rem(lax.axis_index("ctx"), 2)
    n, d = tokens.shape[1], tokens.shape[2]
    rows, k = mixing_weight.shape[0], mixing_weight.shape[2]
    local_experts, width, units = expert_up.shape
    half = local_experts // 2
    experts = centroids.shape[0]
    sources = fs * 4
    heads = k // HD
    dma = pltpu.SemaphoreType.DMA
    per = CAP // zs
    m = n // zs
    r = half * per
    dh = d // 2
    own_rows = sources * per
    slots_in = sources * CAP
    others = 2 * fs - 1
    smem = pl.BlockSpec(memory_space=pltpu.SMEM)
    anyspec = pl.BlockSpec(memory_space=ANY)

    mixing = mixing_weight.transpose(1, 0, 2)
    ins = [("prefix", prefix_length, smem), ("tok", tokens[0], vspec()), ("chosen", assignment.reshape(1, n), vspec()),
           ("tea", teacher[0], vspec()), ("cot", cotangent[0], vspec()),
           ("up", expert_up, anyspec), ("dn", expert_down.transpose(0, 2, 1), anyspec)]
    scratch = []
    weights = [("w3", (3, d, k), BF), ("wo", (d, k), BF), ("table", (TAB, d), BF), ("valid", (sources, n), F32)]
    gather = rows % 16 == 0
    pairs = 2 * fs if gather else 1
    if gather:
        ins += [("mix", mixing, vspec()), ("ow", output_weight, vspec()), ("cent", centroids, vspec()),
                ("gain1", first_gain.reshape(1, rows), vspec()), ("gain2", second_gain.reshape(1, rows), vspec()),
                ("here", validity, vspec())]
        scratch += weights
        scratch += [("small", (TAB, n), F32), ("small_all", (sources, TAB, n), BF)]
        scratch += [(v, (others + w, 4), dma) for v, w in (("p_s", 0), ("p_r", 0), ("q_s", 1), ("q_r", 1))]
    else:
        small = jnp.concatenate(
            [
                jnp.pad(jnp.concatenate([centroids, first_gain[None], second_gain[None]]), ((0, 0), (0, n - rows))),
                validity.astype(BF),
                jnp.zeros((TAB - experts - 3, n), BF),
            ]
        )
        everyone = ("fsdp", "ctx")
        table = lax.all_gather(small, everyone, axis=0)
        full = (
            lax.all_gather(mixing, everyone, axis=1, tiled=True),
            lax.all_gather(output_weight, everyone, axis=1, tiled=True).T,
            table[:, :, :rows].transpose(1, 0, 2).reshape(TAB, d),
            table[:, experts + 2, :].astype(F32),
        )
        ins += [(w[0], v, vspec()) for w, v in zip(weights, full)]
    hidden, received, left = (half, slots_in, units), (half, slots_in, dh), (half, width, slots_in)
    outs = [(name, shape, BF, anyspec) for name, shape in (
        ("xt_own", left), ("xt_sib", left), ("act_own", hidden), ("act_sib", hidden),
        ("gxt_own", left), ("gxt_sib", left), ("gh_own", hidden), ("gh_sib", hidden))]
    outs += [("tg_out", (n, d), BF, vspec()), ("out", (n, d), BF, vspec()), ("mix_out", (3, rows, k), F32, vspec()),
             ("og_out", (k, rows), F32, vspec()), ("sm_out", (TAB, 128), F32, vspec()), ("stat_out", (8, 128), F32, vspec())]
    piece = (rows + (-rows % 16) + TAB, 4 * k)
    slots = (fs, 2, 2, r)
    scratch += [
        ("normed", (n, d), BF), ("qt", (k, n), BF), ("kv", (4, n, 2 * k), BF), ("pt", (heads, 4, n, n), BF),
        ("scores", (heads, 4, n, n), F32), ("ctx", (n, k), BF), ("ctx_in", (zs - 1, m, k), BF), ("wo_all", (zs, pairs, 2, d // (2 * pairs), k), BF),
        ("gct", (n, k), BF), ("gct_out", (zs - 1, m, k), BF),
        ("res", (m, d), F32), ("mi", (m, d), BF), ("slots", slots + (dh,), BF), ("slots_g", slots + (dh + 128,), BF),
        ("wu", (half, dh, units), BF), ("wd", (half, dh, units), BF), ("gp", hidden, BF),
        ("act", hidden, BF), ("gh", hidden, BF), ("x", received, BF), ("gx", received, BF),
        ("xt", (half, dh, slots_in), BF), ("gxt", (half, dh, slots_in), BF),
        ("rq", (sources, r, dh), BF), ("rg", (sources, r, dh + 128), BF), ("grads", (half, own_rows, dh + 128), BF),
        ("results", (half, own_rows, dh), BF), ("xg", (half, own_rows, dh), BF), ("xg_back", (half, own_rows, dh), BF),
        ("ret", (sources, r, dh), BF), ("ret_back", (sources, r, dh), BF),
        ("rb", (sources, r, dh), BF), ("rb_back", (sources, r, dh), BF),
        ("sorted_out", (n, d), BF), ("stat", (8, 128), F32), ("stat_in", (zs - 1, 8, 128), F32),
        ("stat_all", (sources, 8, 128), F32),
        ("ps", hidden, BF), ("pr", hidden, BF), ("pr_back", hidden, BF), ("rows", received, BF),
        ("rin", (half, zs - 1, own_rows, dh), BF), ("gm", (m, d), F32), ("gl", (m, 1), F32),
        ("sorted_gb", (n, d), BF), ("near", (2, n, 2 * k), F32), ("away", (2, n, 2 * k), F32),
        ("away_in", (2, n, 2 * k), F32), ("far_out", (n, 2 * k), BF), ("far_in", (n, 2 * k), BF), ("gn", (n, d), BF),
        ("gn_in", (zs - 1, m, d), BF), ("sorted_tg", (n, d), BF), ("dense", (fs, 2, 2) + piece, F32),
        ("dense_in", (fs, 2) + piece, F32), ("give", (others,) + piece, BF), ("taken", (others,) + piece, BF),
        ("sm", (TAB, 128), F32), ("sm_in", (zs - 1, TAB, 128), F32),
    ]
    for name, shape in (("hz", (zs - 1,)), ("wx", (2,)), ("kv", (3,)), ("d", (sources - 1,)), ("g", (sources - 1,)),
                        ("b", (sources - 1,)), ("c", (sources - 1,)), ("u", (sources - 1,)), ("o", (zs - 1,)),
                        ("t", (zs - 1,)), ("e", (4,)), ("ba", (zs - 1,)), ("bs", (zs - 1,)), ("bt", (zs - 1,)),
                        ("v", (zs - 1,)), ("k", (4,)), ("wz", (zs - 1, pairs)), ("wy", (zs - 1,)), ("gc", (zs - 1,)), ("bg", (others,)),
                        ("one_a", (half, zs - 1)), ("one_x", (half,)), ("one_r", (half, zs - 1)),
                        ("two_a", (half, zs - 1)), ("two_x", (half,)), ("two_r", (half, zs - 1))):
        scratch += [(name + "_s", shape, dma), (name + "_r", shape, dma)]
    scratch += [("wsem", (6,), dma), ("l_s", (4,), dma)]
    names = [v[0] for v in ins] + [v[0] for v in outs] + [v[0] for v in scratch]
    results = pl.pallas_call(
        partial(layer_body, names, fs, zs, gather, rows),
        out_shape=[sds(v[1], v[2]) for v in outs],
        in_specs=[v[2] for v in ins],
        out_specs=[v[3] for v in outs],
        scratch_shapes=[dma(v[1]) if v[2] is dma else VMEM(v[1], v[2]) for v in scratch],
        compiler_params=params(1, 60),
        name="layer",
    )(*[v[1] for v in ins])
    xt, xt_x, act, act_x, gxt, gxt_x, gh, gh_x = results[:8]
    shapes = [sds((n, d), BF), sds((n, d), BF), sds((3, rows, k), F32), sds((k, rows), F32),
              sds((experts, rows), F32), sds((1, rows), F32), sds((1, rows), F32)]
    up, down, tokens_gradient, activations, mix_part, out_part, cen_part, g1, g2, balance, distill = finish(
        c, n * sources, (xt, gh, xt_x, gh_x, gxt, act, gxt_x, act_x), results[8:], shapes
    )
    return (
        activations[None],
        tokens_gradient[None],
        mix_part.transpose(1, 0, 2),
        out_part,
        g1.reshape(rows),
        g2.reshape(rows),
        cen_part,
        up.reshape(local_experts, width, units),
        down.reshape(local_experts, width, units).transpose(0, 2, 1),
        balance.reshape(()),
        distill.reshape(()),
    )


def solution(mesh):
    in_specs = (
        P("fsdp", "ctx", None),
        P(("fsdp", "ctx"), None, "tp"),
        P("tp", ("fsdp", "ctx")),
        P(("fsdp", "ctx")),
        P(("fsdp", "ctx")),
        P(None, ("fsdp", "ctx")),
        P("fsdp", "ctx", "tp"),
        P("fsdp", "tp", "ctx"),
        P("fsdp"),
        P("fsdp", "ctx", None),
        P("fsdp", "ctx"),
        P("fsdp", "ctx", None),
        P("fsdp", "ctx", None),
    )
    out_specs = (
        P("fsdp", "ctx", None),
        P("fsdp", "ctx", None),
        P(("fsdp", "ctx"), None, "tp"),
        P("tp", ("fsdp", "ctx")),
        P(("fsdp", "ctx")),
        P(("fsdp", "ctx")),
        P(None, ("fsdp", "ctx")),
        P("fsdp", "ctx", "tp"),
        P("fsdp", "tp", "ctx"),
        P(),
        P(),
    )
    return jax.shard_map(
        per_device, mesh=mesh, in_specs=in_specs, out_specs=out_specs, check_vma=False
    )
```

```python
from functools import partial
import math
from types import SimpleNamespace

import jax
import jax.numpy as jnp
from jax import lax
from jax.experimental import pallas as pl
from jax.experimental.pallas import tpu as pltpu
from jax.sharding import PartitionSpec as P

HD = 64
EPSILON = 1e-05
BF = jnp.bfloat16
F32 = jnp.float32
MESH = pl.DeviceIdType.MESH
TOP = lax.Precision.HIGHEST
VMEM = pltpu.VMEM
ANY = pl.ANY
CAP = 16
EXP = 32
STEP = 4
TAB = 48


def _dot(a, b, ca, cb, precision=None):
    return lax.dot_general(
        a, b, (((ca,), (cb,)), ((), ())), preferred_element_type=F32, precision=precision
    )


def nn(a, b):
    return _dot(a, b, 1, 0)


def nt(a, b):
    return _dot(a, b, 1, 1)


def tn(a, b):
    return _dot(a, b, 0, 0)


def vspec():
    return pl.BlockSpec(memory_space=VMEM)


def sds(shape, dtype):
    return jax.ShapeDtypeStruct(shape, dtype)


def params(cid=None, mib=56):
    if cid is None:
        return pltpu.CompilerParams(vmem_limit_bytes=mib * 2**20)
    return pltpu.CompilerParams(
        vmem_limit_bytes=mib * 2**20, collective_id=cid, has_side_effects=True
    )


def iota(shape, dim):
    return lax.broadcasted_iota(jnp.int32, shape, dim)


def to_col(row):
    n = row.shape[1]
    return jnp.sum(jnp.where(iota((n, n), 0) == iota((n, n), 1), row, 0.0), axis=1, keepdims=True)


def to_row(col):
    n = col.shape[0]
    return jnp.sum(jnp.where(iota((n, n), 0) == iota((n, n), 1), col, 0.0), axis=0, keepdims=True)


def norm_parts(x):
    c = x - jnp.mean(x, axis=-1, keepdims=True)
    inv = lax.rsqrt(jnp.mean(c * c, axis=-1, keepdims=True) + EPSILON)
    return c * inv, inv


def norm_back(grad, xhat, inv, gain):
    gx = grad * gain
    return inv * (
        gx
        - jnp.mean(gx, axis=-1, keepdims=True)
        - xhat * jnp.mean(gx * xhat, axis=-1, keepdims=True)
    )


def log2(v):
    return v.bit_length() - 1


def shifted(v, by):
    return lax.shift_right_logical(v, by)


def owners(zs):
    return sorted(range(1, zs), key=lambda s: (-min(s, zs - s), s)) + [0]


class Route:
    def __init__(self, chosen, zs, z, width=0):
        n = chosen.shape[1]
        m = n // zs
        per = CAP // zs
        chosen = to_col(chosen.astype(F32))
        self.hot = (chosen == iota((n, EXP), 1).astype(F32)).astype(BF)
        lower = (iota((n, n), 1) < iota((n, n), 0)).astype(BF)
        rank = jnp.sum(nn(lower, self.hot) * self.hot.astype(F32), axis=1, keepdims=True)
        turn = jnp.floor(rank * (1.0 / zs))
        owner = rank - zs * turn
        owned = (owner == iota((n, zs), 1).astype(F32)).astype(BF)
        place = jnp.sum(nn(lower, owned) * owned.astype(F32), axis=1, keepdims=True)
        ahead = owner - lax.convert_element_type(z, F32)
        ahead = jnp.where(ahead < 0, ahead + zs, ahead)
        order = sum(jnp.where(ahead == step, float(k), 0.0) for k, step in enumerate(owners(zs)))
        self.at = order * m + place
        self.at_row = to_row(self.at)
        mine = iota((m, n), 0).astype(F32) + float((zs - 1) * m) == self.at_row
        self.mine = mine.astype(BF)
        self.mine_mask = mine
        self.slot = self.own_col(to_row(chosen * per + turn))
        self.own_hot = nn(self.mine, self.hot).astype(BF)
        self.slots = EXP * per
        self.n, self.m, self.width = n, m, width

    def positions(self):
        n = self.n
        return jnp.sum(jnp.where(self.at == iota((n, n), 1).astype(F32), iota((n, n), 0).astype(F32), 0.0), axis=0, keepdims=True)

    def own_col(self, row):
        return jnp.sum(jnp.where(self.mine_mask, row, 0.0), axis=1, keepdims=True)

    def own(self, rows):
        return nn(self.mine, rows)

    def sort(self, rows):
        return nn((iota((self.n, self.n), 0).astype(F32) == self.at_row).astype(BF), rows).astype(BF)

    def unsort(self, rows):
        return nn((iota((self.n, self.n), 1).astype(F32) == self.at).astype(BF), rows).astype(BF)

    def fill(self, rows, s_ref):
        place = (iota((self.slots, self.m), 0).astype(F32) == to_row(self.slot)).astype(BF)
        filled = nn(place, rows).astype(BF)
        fs, _, _, r, _ = s_ref.shape
        h = self.width // 2
        for f in range(fs):
            for c in range(2):
                at = (f * 2 + c) * r
                for y in range(2):
                    s_ref[f, y, c, :, :h] = filled[at : at + r, y * h : (y + 1) * h]
                    if rows.shape[1] > self.width:
                        s_ref[f, y, c, :, h:] = filled[at : at + r, self.width :]

    def collect(self, rb_ref):
        parts = []
        for f in range(rb_ref.shape[0] // 4):
            for c in range(2):
                parts.append(jnp.concatenate([rb_ref[f * 4 + c], rb_ref[f * 4 + 2 + c]], axis=1))
        rows = jnp.concatenate(parts, axis=0)
        place = (iota((self.m, self.slots), 1).astype(F32) == self.slot).astype(BF)
        return nn(place, rows)


def z_peers(zs):
    f, i, z = lax.axis_index("fsdp"), lax.axis_index("ctx"), lax.axis_index("tp")
    return [(f, i, lax.rem(z + s, zs)) for s in range(1, zs)]


def greet(peers):
    barrier = pltpu.get_barrier_semaphore()
    for peer in peers:
        pl.semaphore_signal(barrier, inc=1, device_id=peer, device_id_type=MESH)
    pl.semaphore_wait(barrier, len(peers))


def remote(src, dst, send, recv, peer):
    return pltpu.make_async_remote_copy(
        src_ref=src, dst_ref=dst, send_sem=send, recv_sem=recv, device_id=peer, device_id_type=MESH
    )


class Scatter:
    def __init__(self, zs, x_ref, parts, send, recv):
        self.zs, self.x_ref, self.parts, self.send, self.recv = zs, x_ref, parts, send, recv
        self.m = x_ref.shape[0] // zs
        self.copies = []

    def start(self, lo, hi):
        peers = z_peers(self.zs)
        for k, step in list(enumerate(owners(self.zs)))[lo:hi]:
            if step:
                cp = remote(
                    self.x_ref.at[pl.ds(k * self.m, self.m)], self.parts.at[step - 1],
                    self.send.at[step - 1], self.recv.at[step - 1], peers[step - 1],
                )
                cp.start()
                self.copies.append((step, cp))

    def finish(self):
        total = self.x_ref[pl.ds((self.zs - 1) * self.m, self.m), :].astype(F32)
        for step, cp in sorted(self.copies, key=lambda v: v[0]):
            cp.wait_recv()
            total = total + self.parts[step - 1].astype(F32)
        return total


def gather_z(zs, x_ref, m, send, recv):
    copies = []
    order = owners(zs)
    for s, peer in enumerate(z_peers(zs)):
        to = order.index(zs - s - 1)
        cp = remote(
            x_ref.at[pl.ds((zs - 1) * m, m)], x_ref.at[pl.ds(to * m, m)], send.at[s], recv.at[s], peer
        )
        cp.start()
        copies.append(cp)
    return copies


def span(at, n):
    return pl.ds(pl.multiple_of(at * n, n), n)


def group_peers(fs):
    f, i, z = lax.axis_index("fsdp"), lax.axis_index("ctx"), lax.axis_index("tp")
    y, c = lax.div(i, 2), lax.rem(i, 2)
    out = []
    for df in range(fs):
        for dy in range(2):
            for dc in range(2):
                if df or dy or dc:
                    fp = lax.rem(f + df, fs)
                    yp = y if dy == 0 else 1 - y
                    cp = c if dc == 0 else 1 - c
                    out.append((fp, yp, cp, (fp, yp * 2 + cp, z)))
    return out


class Attention:
    def __init__(self, R, mine, offsets, row0, positions):
        self.R = R
        self.k, self.n = R.qt.shape
        self.heads = self.k // HD
        self.offsets, self.row0 = offsets, row0
        self.query = positions + lax.convert_element_type(mine * self.n, F32)

    def lanes(self, half):
        return slice(half * (self.n // 2), (half + 1) * (self.n // 2))

    def scores(self, half, j):
        R, at, w = self.R, self.lanes(half), self.n // 2
        key = (iota((self.n, w), 0) + self.offsets[j] * self.n).astype(F32)
        col = to_col(R.valid[pl.ds(self.row0 + self.offsets[j], 1), :])
        query = self.query[:, at]
        prefix = lax.convert_element_type(R.prefix[0], F32)
        allowed = ((key <= query) | (key < prefix)) & ((col > 0.5) | (key == query))
        for h in range(self.heads):
            lo = h * HD
            scores = nn(R.kv[j, :, lo : lo + HD], R.qt[lo : lo + HD, at]) * (1.0 / math.sqrt(HD))
            R.scores[h, j, :, at] = jnp.where(allowed, scores, -1e30)

    def context(self, half):
        R, at, w, k = self.R, self.lanes(half), self.n // 2, self.k
        outs = []
        for h in range(self.heads):
            lo = h * HD
            top = jnp.max(R.scores[h, 0, :, at], axis=0, keepdims=True)
            for j in range(1, 4):
                top = jnp.maximum(top, jnp.max(R.scores[h, j, :, at], axis=0, keepdims=True))
            exps = [jnp.exp(R.scores[h, j, :, at] - top) for j in range(4)]
            share = 1.0 / sum(jnp.sum(e, axis=0, keepdims=True) for e in exps)
            acc = jnp.zeros((HD, w), F32)
            for j in range(4):
                weights = (exps[j] * share).astype(BF)
                R.pt[h, j, :, at] = weights
                acc = acc + tn(R.kv[j, :, k + lo : k + lo + HD], weights)
            outs.append(acc)
        return jnp.transpose(jnp.concatenate(outs, axis=0)).astype(BF)

    def back(self, half, gct, fresh, made):
        R, at, k = self.R, self.lanes(half), self.k
        scale = 1.0 / math.sqrt(HD)
        means, dqs = [], []
        for h in range(self.heads):
            lo = h * HD
            mean = 0.0
            for j in range(4):
                dp = nn(R.kv[j, :, k + lo : k + lo + HD], gct[lo : lo + HD, :])
                R.scores[h, j, :, at] = dp
                mean = mean + jnp.sum(R.pt[h, j, :, at].astype(F32) * dp, axis=0, keepdims=True)
            means.append(mean)
            dqs.append(jnp.zeros((HD, self.n // 2), F32))
        for j in (3, 1, 2, 0):
            target = R.near if j < 2 else R.away
            for h in range(self.heads):
                lo = h * HD
                w = R.pt[h, j, :, at]
                ds = (w.astype(F32) * (R.scores[h, j, :, at] - means[h])).astype(BF)
                dqs[h] = dqs[h] + tn(R.kv[j, :, lo : lo + HD], ds)
                dk = nt(ds, R.qt[lo : lo + HD, at]) * scale
                dv = nt(w, gct[lo : lo + HD, :])
                if not fresh:
                    dk = dk + target[j % 2, :, lo : lo + HD]
                    dv = dv + target[j % 2, :, k + lo : k + lo + HD]
                target[j % 2, :, lo : lo + HD] = dk
                target[j % 2, :, k + lo : k + lo + HD] = dv
            made(j)
        return jnp.concatenate(dqs, axis=0) * scale


def finish_body(tokens, step, *refs):
    ins = refs[:8]
    tg_in, act_in, mix_in, og_in, sm_in, stat_in = refs[8:14]
    up_out, down_out, tg_ref, act_ref, mix_ref, og_ref, cen_ref, g1_ref, g2_ref, bal_ref, dis_ref = refs[14:25]
    held, (up, down, in_sem, out_sem) = refs[25:33], refs[33:]
    c = lax.rem(lax.axis_index("ctx"), 2)
    half = up.shape[1]
    loads = {}
    for n in range(half // step):
        at = pl.ds(n * step, step)
        for k in range(8):
            cp = pltpu.make_async_copy(ins[k].at[at], held[k].at[at], in_sem.at[k, n])
            cp.start()
            loads[k, n] = cp
    tg_ref[...] = tg_in[...]
    act_ref[...] = act_in[...]
    mix_ref[...] = mix_in[...]
    og_ref[...] = og_in[...]
    rows = cen_ref.shape[1]
    cen_ref[...] = sm_in[0:EXP, :rows]
    g1_ref[...] = sm_in[EXP : EXP + 1, :rows]
    g2_ref[...] = sm_in[EXP + 1 : EXP + 2, :rows]
    share = stat_in[0:1, :EXP] / tokens - 1.0 / EXP
    bal_ref[0, 0] = EXP * EXP * jnp.sum(share * stat_in[1:2, :EXP] / tokens)
    dis_ref[0, 0] = jnp.sum(stat_in[2:3, 0:1])
    stores = []
    for n in range(half // step):
        for m, (made, out) in enumerate(((up, up_out), (down, down_out))):
            for k, core in enumerate((c, 1 - c)):
                left, right = 4 * m + 2 * k, 4 * m + 2 * k + 1
                loads[left, n].wait()
                loads[right, n].wait()
                for e in range(n * step, (n + 1) * step):
                    made[k, e] = nn(held[left][e], held[right][e])
                at = pl.ds(n * step, step)
                cp = pltpu.make_async_copy(made.at[k, at], out.at[core, at], out_sem.at[m, k, n])
                cp.start()
                stores.append(cp)
    for cp in stores:
        cp.wait()


def finish(tokens, pairs, small, shapes):
    half, q, n = pairs[0].shape
    units = pairs[1].shape[2]
    step = STEP if half % STEP == 0 else 1
    out = sds((2, half, q, units), F32)
    smem = pl.BlockSpec(memory_space=pltpu.SMEM)
    anyspec = pl.BlockSpec(memory_space=ANY)
    dma = pltpu.SemaphoreType.DMA
    return pl.pallas_call(
        partial(finish_body, float(tokens), step),
        in_specs=[anyspec] * 8 + [vspec()] * len(small),
        out_specs=[anyspec] * 2 + [vspec()] * len(shapes) + [smem] * 2,
        out_shape=[out, out] + shapes + [sds((1, 1), F32)] * 2,
        scratch_shapes=[VMEM(v.shape, BF) for v in pairs]
        + [VMEM(out.shape, F32)] * 2
        + [dma((8, half // step)), dma((2, 2, half // step))],
        compiler_params=params(),
        name="finish",
    )(*pairs, *small)


def whereabouts():
    f, i, z = lax.axis_index("fsdp"), lax.axis_index("ctx"), lax.axis_index("tp")
    return f, i, z, lax.div(i, 2), lax.rem(i, 2)


def reorder(sources, half, per, inverse):
    n = sources * half * per
    i, o = iota((n, n), 1), iota((n, n), 0)
    if inverse:
        i, o = o, i
    ls, lh, lp = log2(sources), log2(half), log2(per)
    slot = o & (per - 1)
    source = shifted(o, lp) & (sources - 1)
    expert = shifted(o, lp + ls)
    return (i == source * (half * per) + expert * per + slot).astype(BF)


class Pass:
    def __init__(self, back, zs, w_in, w_out, xg, x_ref, ps, pr, h_ref, gp_ref, res, rin, sems):
        self.back, self.zs, self.w_in, self.w_out = back, zs, w_in, w_out
        self.xg, self.x_ref, self.ps, self.pr = xg, x_ref, ps, pr
        self.h_ref, self.gp_ref, self.res, self.rin = h_ref, gp_ref, res, rin
        self.a_s, self.a_r, self.x_s, self.x_r, self.r_s, self.r_r = sems
        f, i, z, y, c = whereabouts()
        self.z = z
        self.m = xg.shape[1]
        self.across = (f, (1 - y) * 2 + c, z)
        self.peers = z_peers(zs)

    def share(self, e, s):
        to = self.x_ref.at[e, span(self.z, self.m), :]
        return remote(self.xg.at[e], to, self.a_s.at[e, s], self.a_r.at[e, s], self.peers[s])

    def cross(self, e):
        return remote(self.ps.at[e], self.pr.at[e], self.x_s.at[e], self.x_r.at[e], self.across)

    def scatter(self, e, s):
        to = lax.rem(self.z + s + 1, self.zs)
        return remote(
            self.res.at[e, span(to, self.m), :], self.rin.at[e, s], self.r_s.at[e, s], self.r_r.at[e, s], self.peers[s]
        )

    def spread(self, e, rows):
        self.xg[e] = rows
        for s in range(self.zs - 1):
            self.share(e, s).start()
        self.x_ref[e, span(self.z, self.m), :] = rows

    def first(self, e):
        for s in range(self.zs - 1):
            self.share(e, s).wait_recv()
        self.ps[e] = nn(self.x_ref[e], self.w_in[e]).astype(BF)

    def second(self, e):
        self.cross(e).wait_recv()
        total = self.ps[e].astype(F32) + self.pr[e].astype(F32)
        if self.back:
            self.h_ref[e] = (total * self.gp_ref[e].astype(F32)).astype(BF)
        else:
            phi = 0.5 * (1.0 + lax.erf(total * math.sqrt(0.5)))
            self.h_ref[e] = (total * phi).astype(BF)
            bell = jnp.exp(-0.5 * total * total) * (1.0 / math.sqrt(2.0 * math.pi))
            self.gp_ref[e] = (phi + total * bell).astype(BF)
        self.res[e] = nt(self.h_ref[e], self.w_out[e]).astype(BF)
        for s in range(self.zs - 1):
            self.scatter(e, s).start()

    def total(self, e):
        total = self.res[e, span(self.z, self.m), :].astype(F32)
        for s in range(self.zs - 1):
            self.scatter(e, s).wait_recv()
            total = total + self.rin[e, s].astype(F32)
        return total.astype(BF)

    def settle(self, e):
        self.cross(e).wait_send()
        for s in range(self.zs - 1):
            self.share(e, s).wait_send()
            self.scatter(e, s).wait_send()


def give_back(fs, total, ret, rb_ref, own_sem, send, recv):
    f, i, z, y, c = whereabouts()
    me = f * 4 + i
    sources, r, dh = ret.shape
    half = total.shape[0]
    rows = total[...].reshape(sources * r, dh)
    ret[...] = nn(reorder(sources, half, r // half, True), rows).astype(BF).reshape(sources, r, dh)
    keep = pltpu.make_async_copy(ret.at[me], rb_ref.at[me], own_sem)
    keep.start()
    copies = []
    for k, (fp, yp, cp_, peer) in enumerate(group_peers(fs)):
        cp = remote(ret.at[fp * 4 + yp * 2 + cp_], rb_ref.at[me], send.at[k], recv.at[k], peer)
        cp.start()
        copies.append(cp)
    return keep, copies


def arrived(given):
    keep, copies = given
    keep.wait()
    for cp in copies:
        cp.wait_recv()


def head(R, fs, zs, gather):
    f, i, z, y, c = whereabouts()
    me = f * 4 + i
    half, width = R.wu.shape[0], R.up.shape[1]
    k = R.qt.shape[0]
    d = R.tok.shape[1]
    sibling = (f, y * 2 + 1 - c, z)
    across = (f, (1 - y) * 2 + c, z)
    same = same_core(fs)
    waits = []
    mine = pl.ds(c * half, half)
    theirs = pl.ds((1 - c) * half, half)
    own = pl.ds(pl.multiple_of(c * width, 64), width)
    loads = [
        pltpu.make_async_copy(R.up.at[mine], R.wu.at[:, own, :], R.wsem.at[0]),
        pltpu.make_async_copy(R.dn.at[mine], R.wd.at[:, own, :], R.wsem.at[1]),
    ]
    swaps = [
        remote(R.up.at[theirs], R.wu.at[:, own, :], R.wx_s.at[0], R.wx_r.at[0], sibling),
        remote(R.dn.at[theirs], R.wd.at[:, own, :], R.wx_s.at[1], R.wx_r.at[1], sibling),
    ]
    if gather:
        rows = R.mix.shape[1]
        R.small[...] = jnp.zeros(R.small.shape, F32)
        R.small[0:EXP, :rows] = R.cent[...].astype(F32)
        R.small[EXP : EXP + 1, :rows] = R.gain1[...].astype(F32)
        R.small[EXP + 1 : EXP + 2, :rows] = R.gain2[...].astype(F32)
        R.small[EXP + 2 : EXP + 3, :] = R.here[...].astype(F32)
        R.small_all[me] = R.small[...].astype(BF)
        R.w3[:, span(me, rows), :] = R.mix[...]
        R.wo[span(me, rows), :] = jnp.transpose(R.ow[...].astype(F32)).astype(BF)
    greet([p[3] for p in group_peers(fs)] + z_peers(zs))
    for cp in loads:
        cp.start()
    xhat, _ = norm_parts(R.tok[...].astype(F32))
    others = []

    def over_z(rows_, pair):
        n_ = len(others) // (zs - 1)
        for s, peer in enumerate(z_peers(zs)):
            cp = remote(R.wo.at[rows_, :], R.wo_all.at[z, pair, c], R.wz_s.at[s, n_], R.wz_r.at[s, n_], peer)
            cp.start()
            others.append(cp)

    if gather:

        def places(at):
            rows_ = span(at, rows)
            return [R.w3.at[1:3, rows_, :], R.small_all.at[at], R.w3.at[0:1, rows_, :], R.wo.at[rows_, :]]

        sends = {}
        for m, ref in sorted(enumerate(places(me)), key=lambda v: (0, 1, 3, 2)[v[0]]):
            for n_, (_, _, peer, _) in enumerate(same):
                cp = remote(ref, ref, R.p_s.at[n_, m], R.p_r.at[n_, m], peer)
                cp.start()
                sends[n_, m] = cp
        over_z(span(me, rows), f * 2 + y)
        relays = {}

        def relay(n_, m, at):
            ref = places(at)[m]
            cp = remote(ref, ref, R.q_s.at[n_, m], R.q_r.at[n_, m], sibling)
            cp.start()
            relays[n_, m] = cp

        def pass_on(some):
            for n_, (_, _, _, at) in enumerate(same):
                for m in some:
                    sends[n_, m].wait_recv()
                    relay(n_ + 1, m, at)

        for m in range(4):
            relay(0, m, me)
        pass_on((0, 1))
        pass_on((3,))
        for _, _, _, at in same:
            over_z(span(at, rows), lax.div(at, 2))
        for n_ in range(len(same) + 1):
            for m in (0, 1):
                relays[n_, m].wait_recv()
        R.table[...] = jnp.concatenate([R.small_all[s, :, :rows] for s in range(fs * 4)], axis=1)
        for s in range(fs * 4):
            R.valid[s : s + 1, :] = R.small_all[s, EXP + 2 : EXP + 3, :].astype(F32)
    normed = (xhat * R.table[EXP : EXP + 1, :].astype(F32)).astype(BF)
    R.normed[...] = normed
    R.kv[0, :, :k] = nn(normed, R.w3[1]).astype(BF)
    R.kv[0, :, k:] = nn(normed, R.w3[2]).astype(BF)
    far = remote(R.kv.at[0], R.kv.at[1], R.kv_s.at[0], R.kv_r.at[0], across)
    sib = remote(R.kv.at[0], R.kv.at[2], R.kv_s.at[1], R.kv_r.at[1], sibling)
    far.start()
    sib.start()
    if gather:
        pass_on((2,))
        for n_ in range(len(same) + 1):
            for m in (2, 3):
                relays[n_, m].wait_recv()
        waits += list(sends.values()) + list(relays.values())
    else:
        over_z(span(c, d // 2), 0)
    route = Route(R.chosen[...], zs, z, d)
    R.qt[...] = jnp.transpose(route.sort(nn(normed, R.w3[0]).astype(BF)).astype(F32)).astype(BF)
    teacher, cotangent = route.own(R.tea[...]), route.own(R.cot[...])
    own_tokens = route.own(R.tok[...])
    own_valid = route.own_col(R.valid[pl.ds(me, 1), :])
    scale = 1.0 / (jnp.sum(R.valid[...]) * d)
    sib.wait_recv()
    offsets = [i, (1 - y) * 2 + c, y * 2 + 1 - c, (1 - y) * 2 + 1 - c]
    attention = Attention(R, i, offsets, f * 4, route.positions())
    for j in (0, 2):
        for half_ in range(2):
            attention.scores(half_, j)
    far.wait_recv()
    last = remote(R.kv.at[1], R.kv.at[3], R.kv_s.at[2], R.kv_r.at[2], sibling)
    last.start()
    for swap in swaps:
        swap.start()
    attention.scores(0, 1)
    attention.scores(1, 1)
    last.wait_recv()
    n = R.tok.shape[0]
    m = n // zs
    peers = z_peers(zs)
    sums, passed = [], []
    for half_ in range(2):
        attention.scores(half_, 3)
        R.ctx[pl.ds(half_ * (n // 2), n // 2), :] = attention.context(half_)
        for k_, step in list(enumerate(owners(zs)))[half_ * (zs // 2) : (half_ + 1) * (zs // 2)]:
            if step:
                cp = remote(
                    R.ctx.at[pl.ds(k_ * m, m)], R.ctx_in.at[step - 1],
                    R.hz_s.at[step - 1], R.hz_r.at[step - 1], peers[step - 1],
                )
                cp.start()
                sums.append(cp)
        if half_ == 1:
            for cp in others:
                cp.wait_recv()
            for s in range(zs - 1):
                ref = R.wo_all.at[lax.rem(z - s - 1 + zs, zs), :, c]
                cp = remote(ref, ref, R.wy_s.at[s], R.wy_r.at[s], sibling)
                cp.start()
                passed.append(cp)
    residual = own_tokens + nt(R.ctx[pl.ds((zs - 1) * m, m), :], R.wo[...])
    for cp in sums + passed:
        cp.wait_recv()
    for step in range(1, zs):
        residual = residual + nt(R.ctx_in[step - 1], R.wo_all[lax.rem(z - step + zs, zs)].reshape(R.wo.shape))
    R.res[...] = residual
    xhat, _ = norm_parts(residual)
    mixed_in = (xhat * R.table[EXP + 1 : EXP + 2, :].astype(F32)).astype(BF)
    R.mi[...] = mixed_in
    logit = jnp.sum(mixed_in.astype(F32) * nn(route.own_hot, R.table[0:EXP, :]), axis=-1, keepdims=True)
    gate = jax.nn.sigmoid(logit)
    route.fill(mixed_in, R.slots)
    sends = dispatch(fs, R.slots, R.rq, R.d_s, R.d_r, R.wsem.at[2])
    weight = 2.0 * own_valid * scale
    known = gate * (cotangent + weight * (residual - teacher))
    slope = jnp.broadcast_to(gate * gate * weight, (known.shape[0], 128))
    route.fill(jnp.concatenate([known, slope], axis=1).astype(BF), R.slots_g)
    sends_g = dispatch(fs, R.slots_g, R.rg, R.g_s, R.g_r, R.wsem.at[3])
    waits += swaps + sums + others + passed + [far, sib, last]
    return SimpleNamespace(route=route, attention=attention, own_tokens=own_tokens, sends=sends, sends_g=sends_g, gate=gate, teacher=teacher, cotangent=cotangent, valid=own_valid, scale=scale,
                           loads=loads, swaps=swaps, waits=waits)


def dispatch(fs, src, dst, send, recv, own_sem):
    f, i, z, y, c = whereabouts()
    me = f * 4 + i
    copies = [pltpu.make_async_copy(src.at[f, y, c], dst.at[me], own_sem)]
    for k, (fp, yp, cp_, peer) in enumerate(group_peers(fs)):
        copies.append(remote(src.at[fp, yp, cp_], dst.at[me], send.at[k], recv.at[k], peer))
    for cp in copies:
        cp.start()
    return copies


def same_core(fs):
    f, i, z, y, c = whereabouts()
    out = []
    for df in range(fs):
        for dy in range(2):
            if df or dy:
                fp, fm = lax.rem(f + df, fs), lax.rem(f - df + fs, fs)
                yp = y if dy == 0 else 1 - y
                out.append((fp, yp, (fp, yp * 2 + c, z), fm * 4 + yp * 2 + c))
    return out


def middle(R, S, fs, zs):
    f, i, z, y, c = whereabouts()
    me = f * 4 + i
    half, width = R.wu.shape[0], R.up.shape[1]
    sources, r, dh = R.rq.shape
    m = sources * r // half
    group = group_peers(fs)
    sibling = (f, y * 2 + 1 - c, z)
    own = pl.ds(pl.multiple_of(c * width, 64), width)
    other = pl.ds(pl.multiple_of((1 - c) * width, 64), width)
    sems = [[getattr(R, p + n) for n in ("a_s", "a_r", "x_s", "x_r", "r_s", "r_r")] for p in ("one_", "two_")]
    one = Pass(False, zs, R.wu, R.wd, R.xg, R.x, R.ps, R.pr, R.act, R.gp, R.rows, R.rin, sems[0])
    two = Pass(True, zs, R.wd, R.wu, R.xg_back, R.gx, R.ps, R.pr_back, R.gh, R.gp, R.rows, R.rin, sems[1])
    order = reorder(sources, half, r // half, False)
    exports = []

    def export(n, own_src, own_dst, src, dst):
        keep = pltpu.make_async_copy(own_src, own_dst, R.l_s.at[n])
        give = remote(src, dst, R.e_s.at[n], R.e_r.at[n], sibling)
        keep.start()
        give.start()
        exports.append((keep, give))

    for cp in S.loads:
        cp.wait()
    for cp in S.swaps:
        cp.wait_recv()
    arrived((S.sends[0], S.sends[1:]))
    rows = nn(order, R.rq[...].reshape(sources * r, dh)).astype(BF).reshape(half, m, dh)
    for e in range(half):
        one.spread(e, rows[e])

    @pl.loop(0, half)
    def _(e):
        one.first(e)
        one.cross(e).start()

    @pl.loop(0, half)
    def _(e):
        R.xt[e] = jnp.transpose(R.x[e])

    arrived((S.sends_g[0], S.sends_g[1:]))
    R.grads[...] = nn(order, R.rg[...].reshape(sources * r, dh + 128)).astype(BF).reshape(half, m, dh + 128)
    export(0, R.xt.at[:, own, :], R.xt_own, R.xt.at[:, other, :], R.xt_sib)

    def turn(e):
        result = one.total(e)
        R.results[e] = result
        scale = R.grads[e, :, dh:].astype(F32)[:, :1]
        two.spread(e, (R.grads[e, :, :dh].astype(F32) + scale * result.astype(F32)).astype(BF))

    lag, lag2 = 3, 6
    start = max(half, lag2 + 1)
    ahead = 2

    def step(t, fixed=True):
        if not fixed or t < half:
            one.second(t)
        if fixed and t - start >= 0 and t - start < half:
            two.second(t - start)
        if not fixed or 0 <= t - lag < half:
            turn(t - lag)
        if not fixed or 0 <= t - lag2 < half:
            one.settle(t - lag2)
            two.first(t - lag2)

    begun = 0
    t = 0
    while t < lag2:
        step(t)
        t += 1
    safe = max(t, start - ahead)
    if safe > t and half > t:
        stop = min(safe, half)

        @pl.loop(t, stop)
        def _(k):
            step(k, False)

        t = stop
    given = None
    pending = []

    def report():
        returned = S.route.collect(R.rb)
        n, d = returned.shape
        mixed = R.res[...] + S.gate * returned
        diff = mixed - S.teacher
        weighted = S.valid * diff
        grad = S.cotangent + 2.0 * weighted * S.scale
        R.sorted_out[pl.ds((zs - 1) * n, n), :] = mixed.astype(BF)
        pending.extend(gather_z(zs, R.sorted_out, n, R.o_s, R.o_r))
        hot = S.route.own_hot.astype(F32)
        R.stat[...] = jnp.zeros_like(R.stat)
        R.stat[0:1, 0:EXP] = jnp.sum(hot, axis=0, keepdims=True)
        R.stat[1:2, 0:EXP] = jnp.sum(hot * S.gate, axis=0, keepdims=True)
        R.stat[2:3, :] = jnp.broadcast_to(jnp.sum(weighted * diff * S.scale), (1, 128))
        for s, peer in enumerate(z_peers(zs)):
            cp = remote(R.stat, R.stat_in.at[s], R.t_s.at[s], R.t_r.at[s], peer)
            cp.start()
            pending.append(cp)
        R.gm[...] = grad
        grad_gate = jnp.sum(grad * returned, axis=-1, keepdims=True)
        R.gl[...] = grad_gate * S.gate * (1.0 - S.gate)

    def publish():
        total = R.stat[...]
        for s, cp in enumerate(pending[zs - 1 :]):
            cp.wait_recv()
            total = total + R.stat_in[s]
        R.stat_all[me] = total
        for k, (_, _, _, peer) in enumerate(group):
            cp = remote(R.stat_all.at[me], R.stat_all.at[me], R.u_s.at[k], R.u_r.at[k], peer)
            cp.start()
            pending.append(cp)

    while t < start + half + 1:
        step(t)
        if given is None and t - lag >= half - 1:
            given = give_back(fs, R.results, R.ret, R.rb, R.wsem.at[4], R.b_s, R.b_r)
            export(1, R.act, R.act_own, R.act, R.act_sib)
        while begun < half and begun <= t - start + ahead and begun <= t - lag2:
            two.cross(begun).start()
            begun += 1
        if 0 <= t - 1 - start < half:
            R.xg[t - 1 - start] = two.total(t - 1 - start)
        if t == half - 1 + lag2:

            @pl.loop(0, half)
            def _(e):
                R.gxt[e] = jnp.transpose(R.gx[e])

        if t == start + half - 2:
            arrived(given)
            report()
        if t == start + half - 1:
            publish()
        t += 1
    given_back = give_back(fs, R.xg, R.ret_back, R.rb_back, R.wsem.at[5], R.c_s, R.c_r)
    export(2, R.gxt.at[:, own, :], R.gxt_own, R.gxt.at[:, other, :], R.gxt_sib)
    export(3, R.gh, R.gh_own, R.gh, R.gh_sib)
    S.pending, S.exports = pending, exports
    S.waits += pending[: 2 * (zs - 1)] + S.sends[1:] + S.sends_g[1:] + given[1] + given_back[1]
    S.two = two
    arrived(given_back)
    return S.route.collect(R.rb_back)


def back(R, S, grad_back, fs, zs, rows):
    f, i, z, y, c = whereabouts()
    sibling = (f, y * 2 + 1 - c, z)
    across = (f, (1 - y) * 2 + c, z)
    same = same_core(fs)
    route = S.route
    k = R.qt.shape[0]
    gl = R.gl[...]
    grad_in = grad_back + gl * nn(route.own_hot, R.table[0:EXP, :])
    m, d = grad_in.shape
    xhat, inv = norm_parts(R.res[...])
    grad = R.gm[...] + norm_back(grad_in, xhat, inv, R.table[EXP + 1 : EXP + 2, :].astype(F32))
    R.sorted_gb[pl.ds((zs - 1) * m, m), :] = grad.astype(BF)
    gb = grad.astype(BF)
    order = owners(zs)
    pieces = []
    for s, peer in enumerate(z_peers(zs)):
        R.gct_out[s] = nn(gb, R.wo_all[lax.rem(z + s + 1, zs)].reshape(R.wo.shape)).astype(BF)
        to = R.gct.at[pl.ds(order.index(zs - s - 1) * m, m)]
        cp = remote(R.gct_out.at[s], to, R.gc_s.at[s], R.gc_r.at[s], peer)
        cp.start()
        pieces.append(cp)
    R.gct[pl.ds((zs - 1) * m, m), :] = nn(gb, R.wo[...]).astype(BF)
    gathers = gather_z(zs, R.sorted_gb, m, R.ba_s, R.ba_r)
    g2 = jnp.sum(grad_in * xhat, axis=0, keepdims=True)
    cg = _dot(route.own_hot.astype(F32) * gl, R.mi[...].astype(F32), 0, 0, TOP)
    all_tok = norm_parts(route.sort(R.tok[...]).astype(F32))[0]
    own_tok, own_inv = norm_parts(S.own_tokens)
    for cp in S.pending[: zs - 1]:
        cp.wait_recv()
    R.out[...] = route.unsort(R.sorted_out[...])
    for cp in S.pending[2 * (zs - 1) :]:
        cp.wait()
    total = R.stat_all[0]
    for n in range(1, fs * 4):
        total = total + R.stat_all[n]
    R.stat_out[...] = total
    n = R.tok.shape[0]
    swaps = [remote(R.away.at[j], R.away_in.at[j], R.k_s.at[j], R.k_r.at[j], sibling) for j in range(2)]
    cross = remote(R.far_out, R.far_in, R.k_s.at[2], R.k_r.at[2], across)

    def nothing(j):
        pass

    def made(j):
        if j == 3:
            swaps[1].start()
        if j == 1:
            swaps[1].wait_recv()
            R.far_out[...] = (R.near[1] + R.away_in[1]).astype(BF)
            cross.start()
        if j == 2:
            swaps[0].start()

    dqs = {}
    for half, steps in ((1, (0,)), (0, range(1, zs - 1))):
        for s in steps:
            pieces[s].wait_recv()
        gct = jnp.transpose(R.gct[pl.ds(half * (n // 2), n // 2), :])
        dqs[half] = S.attention.back(half, gct, half == 1, nothing if half == 1 else made)
    dq = jnp.transpose(jnp.concatenate([dqs[0], dqs[1]], axis=1)).astype(BF)
    normed = R.normed[...]
    gq = nt(dq, R.w3[0])
    mg = [tn(normed, route.unsort(dq)), None, None]
    swaps[0].wait_recv()
    near = R.near[0] + R.away_in[0]
    cross.wait_recv()
    kvg = (near + R.far_in[...].astype(F32)).astype(BF)
    kvs = route.sort(kvg)
    partial_normed = gq + nt(kvs[:, :k], R.w3[1]) + nt(kvs[:, k:], R.w3[2])
    R.gn[...] = partial_normed.astype(BF)
    scat = Scatter(zs, R.gn, R.gn_in, R.bs_s, R.bs_r)
    scat.start(0, zs)
    mg[1] = tn(normed, kvg[:, :k])
    mg[2] = tn(normed, kvg[:, k:])
    g1 = jnp.sum(partial_normed * all_tok, axis=0, keepdims=True)
    for cp in gathers:
        cp.wait_recv()
    og = tn(R.sorted_gb[...], R.ctx[...])
    dense = R.dense
    last = dense.shape[3] - TAB
    small = jnp.concatenate([cg, g1, g2, jnp.zeros((TAB - EXP - 2, d), F32)], axis=0)
    for s in range(4 * fs):
        at = (s // 4, s % 4 // 2, s % 2)
        lo = s * rows
        for j in range(3):
            dense[at[0], at[1], at[2], 0:rows, j * k : (j + 1) * k] = mg[j][lo : lo + rows, :]
        dense[at[0], at[1], at[2], 0:rows, 3 * k : 4 * k] = og[lo : lo + rows, :]
        dense[at[0], at[1], at[2], last : last + TAB, 0:rows] = small[:, lo : lo + rows]
    pair = remote(dense.at[:, :, 1 - c], R.dense_in, R.k_s.at[3], R.k_r.at[3], sibling)
    pair.start()
    pair.wait_recv()
    shares = []
    for s, (fp, yp, peer, _) in enumerate(same):
        R.give[s] = (dense[fp, yp, c] + R.dense_in[fp, yp]).astype(BF)
        cp = remote(R.give.at[s], R.taken.at[s], R.bg_s.at[s], R.bg_r.at[s], peer)
        cp.start()
        shares.append(cp)
    total = scat.finish()
    tg = grad + norm_back(total, own_tok, own_inv, R.table[EXP : EXP + 1, :].astype(F32))
    R.sorted_tg[pl.ds((zs - 1) * m, m), :] = tg.astype(BF)
    ends = gather_z(zs, R.sorted_tg, m, R.bt_s, R.bt_r)
    kept = dense[f, y, c] + R.dense_in[f, y]
    for s, cp in enumerate(shares):
        cp.wait_recv()
        kept = kept + R.taken[s].astype(F32)
    R.sm[...] = kept[last:, :128]
    smalls = []
    for s, peer in enumerate(z_peers(zs)):
        cp = remote(R.sm, R.sm_in.at[s], R.v_s.at[s], R.v_r.at[s], peer)
        cp.start()
        smalls.append(cp)
    for j in range(3):
        R.mix_out[j] = kept[:rows, j * k : (j + 1) * k]
    R.og_out[...] = jnp.transpose(kept[:rows, 3 * k :])
    for keep, give in S.exports:
        keep.wait()
        give.wait()
    for cp in ends:
        cp.wait_recv()
    R.tg_out[...] = route.unsort(R.sorted_tg[...])
    total = R.sm[...]
    for s, cp in enumerate(smalls):
        cp.wait_recv()
        total = total + R.sm_in[s]
    R.sm_out[...] = total
    for cp in S.waits + pieces + gathers + swaps + [cross, pair] + [v[1] for v in scat.copies] + shares + ends + smalls:
        cp.wait_send()

    @pl.loop(0, R.wu.shape[0])
    def _(e):
        S.two.settle(e)


def layer_body(names, fs, zs, gather, rows, *refs):
    R = SimpleNamespace(**dict(zip(names, refs)))
    S = head(R, fs, zs, gather)
    grad_back = middle(R, S, fs, zs)
    back(R, S, grad_back, fs, zs, rows)


def per_device(tokens, mixing_weight, output_weight, first_gain, second_gain, centroids, expert_up,
               expert_down, prefix_length, assignment, validity, teacher, cotangent):
    fs, zs = lax.axis_size("fsdp"), lax.axis_size("tp")
    n, d = tokens.shape[1], tokens.shape[2]
    rows, k = mixing_weight.shape[0], mixing_weight.shape[2]
    local_experts, width, units = expert_up.shape
    half = local_experts // 2
    experts = centroids.shape[0]
    sources = fs * 4
    heads = k // HD
    dma = pltpu.SemaphoreType.DMA
    per = CAP // zs
    m = n // zs
    r = half * per
    dh = d // 2
    own_rows = sources * per
    slots_in = sources * CAP
    others = 2 * fs - 1
    smem = pl.BlockSpec(memory_space=pltpu.SMEM)
    anyspec = pl.BlockSpec(memory_space=ANY)

    mixing = mixing_weight.transpose(1, 0, 2)
    ins = [("prefix", prefix_length, smem), ("tok", tokens[0], vspec()), ("chosen", assignment.reshape(1, n), vspec()),
           ("tea", teacher[0], vspec()), ("cot", cotangent[0], vspec()),
           ("up", expert_up, anyspec), ("dn", expert_down.transpose(0, 2, 1), anyspec)]
    scratch = []
    weights = [("w3", (3, d, k), BF), ("wo", (d, k), BF), ("table", (TAB, d), BF), ("valid", (sources, n), F32)]
    gather = rows % 16 == 0
    pairs = 2 * fs if gather else 1
    if gather:
        ins += [("mix", mixing, vspec()), ("ow", output_weight, vspec()), ("cent", centroids, vspec()),
                ("gain1", first_gain.reshape(1, rows), vspec()), ("gain2", second_gain.reshape(1, rows), vspec()),
                ("here", validity, vspec())]
        scratch += weights
        scratch += [("small", (TAB, n), F32), ("small_all", (sources, TAB, n), BF)]
        scratch += [(v, (others + w, 4), dma) for v, w in (("p_s", 0), ("p_r", 0), ("q_s", 1), ("q_r", 1))]
    else:
        small = jnp.concatenate(
            [
                jnp.pad(jnp.concatenate([centroids, first_gain[None], second_gain[None]]), ((0, 0), (0, n - rows))),
                validity.astype(BF),
                jnp.zeros((TAB - experts - 3, n), BF),
            ]
        )
        everyone = ("fsdp", "ctx")
        table = lax.all_gather(small, everyone, axis=0)
        full = (
            lax.all_gather(mixing, everyone, axis=1, tiled=True),
            lax.all_gather(output_weight, everyone, axis=1, tiled=True).T,
            table[:, :, :rows].transpose(1, 0, 2).reshape(TAB, d),
            table[:, experts + 2, :].astype(F32),
        )
        ins += [(w[0], v, vspec()) for w, v in zip(weights, full)]
    hidden, received, left = (half, slots_in, units), (half, slots_in, dh), (half, width, slots_in)
    outs = [(name, shape, BF, anyspec) for name, shape in (
        ("xt_own", left), ("xt_sib", left), ("act_own", hidden), ("act_sib", hidden),
        ("gxt_own", left), ("gxt_sib", left), ("gh_own", hidden), ("gh_sib", hidden))]
    outs += [("tg_out", (n, d), BF, vspec()), ("out", (n, d), BF, vspec()), ("mix_out", (3, rows, k), F32, vspec()),
             ("og_out", (k, rows), F32, vspec()), ("sm_out", (TAB, 128), F32, vspec()), ("stat_out", (8, 128), F32, vspec())]
    piece = (rows + (-rows % 16) + TAB, 4 * k)
    slots = (fs, 2, 2, r)
    scratch += [
        ("normed", (n, d), BF), ("qt", (k, n), BF), ("kv", (4, n, 2 * k), BF), ("pt", (heads, 4, n, n), BF),
        ("scores", (heads, 4, n, n), F32), ("ctx", (n, k), BF), ("ctx_in", (zs - 1, m, k), BF), ("wo_all", (zs, pairs, 2, d // (2 * pairs), k), BF),
        ("gct", (n, k), BF), ("gct_out", (zs - 1, m, k), BF),
        ("res", (m, d), F32), ("mi", (m, d), BF), ("slots", slots + (dh,), BF), ("slots_g", slots + (dh + 128,), BF),
        ("wu", (half, dh, units), BF), ("wd", (half, dh, units), BF), ("gp", hidden, BF),
        ("act", hidden, BF), ("gh", hidden, BF), ("x", received, BF), ("gx", received, BF),
        ("xt", (half, dh, slots_in), BF), ("gxt", (half, dh, slots_in), BF),
        ("rq", (sources, r, dh), BF), ("rg", (sources, r, dh + 128), BF), ("grads", (half, own_rows, dh + 128), BF),
        ("results", (half, own_rows, dh), BF), ("xg", (half, own_rows, dh), BF), ("xg_back", (half, own_rows, dh), BF),
        ("ret", (sources, r, dh), BF), ("ret_back", (sources, r, dh), BF),
        ("rb", (sources, r, dh), BF), ("rb_back", (sources, r, dh), BF),
        ("sorted_out", (n, d), BF), ("stat", (8, 128), F32), ("stat_in", (zs - 1, 8, 128), F32),
        ("stat_all", (sources, 8, 128), F32),
        ("ps", hidden, BF), ("pr", hidden, BF), ("pr_back", hidden, BF), ("rows", received, BF),
        ("rin", (half, zs - 1, own_rows, dh), BF), ("gm", (m, d), F32), ("gl", (m, 1), F32),
        ("sorted_gb", (n, d), BF), ("near", (2, n, 2 * k), F32), ("away", (2, n, 2 * k), F32),
        ("away_in", (2, n, 2 * k), F32), ("far_out", (n, 2 * k), BF), ("far_in", (n, 2 * k), BF), ("gn", (n, d), BF),
        ("gn_in", (zs - 1, m, d), BF), ("sorted_tg", (n, d), BF), ("dense", (fs, 2, 2) + piece, F32),
        ("dense_in", (fs, 2) + piece, F32), ("give", (others,) + piece, BF), ("taken", (others,) + piece, BF),
        ("sm", (TAB, 128), F32), ("sm_in", (zs - 1, TAB, 128), F32),
    ]
    for name, shape in (("hz", (zs - 1,)), ("wx", (2,)), ("kv", (3,)), ("d", (sources - 1,)), ("g", (sources - 1,)),
                        ("b", (sources - 1,)), ("c", (sources - 1,)), ("u", (sources - 1,)), ("o", (zs - 1,)),
                        ("t", (zs - 1,)), ("e", (4,)), ("ba", (zs - 1,)), ("bs", (zs - 1,)), ("bt", (zs - 1,)),
                        ("v", (zs - 1,)), ("k", (4,)), ("wz", (zs - 1, pairs)), ("wy", (zs - 1,)), ("gc", (zs - 1,)), ("bg", (others,)),
                        ("one_a", (half, zs - 1)), ("one_x", (half,)), ("one_r", (half, zs - 1)),
                        ("two_a", (half, zs - 1)), ("two_x", (half,)), ("two_r", (half, zs - 1))):
        scratch += [(name + "_s", shape, dma), (name + "_r", shape, dma)]
    scratch += [("wsem", (6,), dma), ("l_s", (4,), dma)]
    names = [v[0] for v in ins] + [v[0] for v in outs] + [v[0] for v in scratch]
    results = pl.pallas_call(
        partial(layer_body, names, fs, zs, gather, rows),
        out_shape=[sds(v[1], v[2]) for v in outs],
        in_specs=[v[2] for v in ins],
        out_specs=[v[3] for v in outs],
        scratch_shapes=[dma(v[1]) if v[2] is dma else VMEM(v[1], v[2]) for v in scratch],
        compiler_params=params(1, 60),
        name="layer",
    )(*[v[1] for v in ins])
    xt, xt_x, act, act_x, gxt, gxt_x, gh, gh_x = results[:8]
    shapes = [sds((n, d), BF), sds((n, d), BF), sds((3, rows, k), F32), sds((k, rows), F32),
              sds((experts, rows), F32), sds((1, rows), F32), sds((1, rows), F32)]
    up, down, tokens_gradient, activations, mix_part, out_part, cen_part, g1, g2, balance, distill = finish(
        n * sources, (xt, gh, xt_x, gh_x, gxt, act, gxt_x, act_x), results[8:], shapes
    )
    return (
        activations[None],
        tokens_gradient[None],
        mix_part.transpose(1, 0, 2),
        out_part,
        g1.reshape(rows),
        g2.reshape(rows),
        cen_part,
        up.reshape(local_experts, width, units),
        down.reshape(local_experts, width, units).transpose(0, 2, 1),
        balance.reshape(()),
        distill.reshape(()),
    )


def solution(mesh):
    in_specs = (
        P("fsdp", "ctx", None),
        P(("fsdp", "ctx"), None, "tp"),
        P("tp", ("fsdp", "ctx")),
        P(("fsdp", "ctx")),
        P(("fsdp", "ctx")),
        P(None, ("fsdp", "ctx")),
        P("fsdp", "ctx", "tp"),
        P("fsdp", "tp", "ctx"),
        P("fsdp"),
        P("fsdp", "ctx", None),
        P("fsdp", "ctx"),
        P("fsdp", "ctx", None),
        P("fsdp", "ctx", None),
    )
    out_specs = (
        P("fsdp", "ctx", None),
        P("fsdp", "ctx", None),
        P(("fsdp", "ctx"), None, "tp"),
        P("tp", ("fsdp", "ctx")),
        P(("fsdp", "ctx")),
        P(("fsdp", "ctx")),
        P(None, ("fsdp", "ctx")),
        P("fsdp", "ctx", "tp"),
        P("fsdp", "tp", "ctx"),
        P(),
        P(),
    )
    return jax.shard_map(
        per_device, mesh=mesh, in_specs=in_specs, out_specs=out_specs, check_vma=False
    )
```
